32 devices in a mesh: groups: 2 (over y), state: 4 (over z), dp: 2 (over x), sub: 2 (over core).
Axes of the slice: x: 2, y: 2, z: 4, core: 2. Of those that a mesh axis runs over, the one named last changes fastest.
Arguments:
- transition: bfloat16 [4, 4, 1024, 16384], P(None, 'state', None, ('dp', 'sub')), may hold values from 0 to 55, as said below
- emission: bfloat16 [4, 512, 4, 4, 1024], P(None, 'groups', ('dp', 'sub')), parts along dimension 1, may hold values from 0 to 1100, as said below
- start: float32 [512, 4, 4, 1024], P('groups', ('dp', 'sub'), 'state'), parts along dimension 0, may hold values from 0.1 to 10
Outputs:
- messages: float32 [4, 512, 4, 4, 1024], P(None, 'groups', ('dp', 'sub'), 'state'), parts along dimension 1
- log_scale: float32 [512], P('groups'), parts along dimension 0
The draws below stay inside these ranges and needn't reach their ends.
There are 2 independent parts, one for each index of `groups`. The reference program is written for one: setup_inputs(seed, part) draws one part's arguments, and reference() takes and returns one part's arrays. A program takes and returns all parts, laid end to end along the dimension named above; an argument that names none is the same for every part. Nothing has to cross between parts.
Inputs may be any that keep to these rules, and one draw needn't show every extreme that they name: `transition`: positive. `emission`: positive.
All inputs are finite; a program needn't handle non-finite values.
Results may differ from the reference program's by a relative error of at most 0.00057.
Values may be sent and summed in bfloat16 or wider, within the bound.
No kernel may reach another device: no remote copies, remote signals or barrier semaphores. Data moves between devices by JAX's collectives and lax.ppermute only.
A program may use at most 192 MiB of HBM per device.

```python
import math
import jax
import jax.numpy as jnp
from jax import lax

H = 16384
SEQS = 256
STEPS = 4
ROWBLK = 4
COLBLK = 4
PIECE = 1024


def draw_transition(key, part):
    key = jax.random.fold_in(key, 7)
    full_shape = (COLBLK, ROWBLK, PIECE, H)
    rough_part = jnp.clip(jax.random.normal(key, full_shape, jnp.float32), -4.0, 4.0)
    return jnp.exp(2.5 * rough_part - 6.0).astype(jnp.bfloat16)


def draw_emission(key, part):
    key = jax.random.fold_in(key, 11)
    key_rough, key_seq, key_state = jax.random.split(key, 3)
    full_shape = (STEPS, SEQS, COLBLK, ROWBLK, PIECE)
    position = (jnp.arange(COLBLK, dtype=jnp.float32)[:, None] * ROWBLK + jnp.arange(ROWBLK, dtype=jnp.float32)[None, :]) / max(COLBLK * ROWBLK - 1, 1)
    state_ramp = jnp.exp(math.log(3.0) * position)
    state_scale = jnp.exp(jax.random.uniform(key_state, (COLBLK, ROWBLK, PIECE), jnp.float32, 0.0, math.log(10.0)))
    rough_part = jnp.clip(jax.random.normal(key_rough, full_shape, jnp.float32), -4.0, 4.0)
    seq_scale = jnp.exp(jax.random.uniform(key_seq, (STEPS, SEQS), jnp.float32, 0.0, math.log(10.0)))
    weights_out = jnp.exp(1.2 * rough_part - 4.0) * (state_ramp[:, :, None] * state_scale)[None, None] * seq_scale[:, :, None, None, None]
    return weights_out.astype(jnp.bfloat16)


def steps_of(own_key, dims, pieces, least, largest):
    factor_of, own = 1.0, jax.random.fold_in(own_key, 6)
    for dim, parts in pieces:
        draws = jnp.exp(jax.random.uniform(jax.random.fold_in(own, dim), (parts,), jnp.float32, least / len(pieces), largest / len(pieces)))
        factor_of = factor_of * jnp.repeat(draws, dims[dim] // parts).reshape([-1 if axis == dim else 1 for axis in range(len(dims))])
    return factor_of


def setup_inputs(seed: int = 0, part: int = 0) -> dict:
    key_of = jax.random.split(jax.random.key(seed), 4)
    part_splits = jax.random.split(jax.random.fold_in(key_of[3], part), 4)
    transition = draw_transition(jax.random.fold_in(key_of[3], 71), part)
    emission = draw_emission(jax.random.fold_in(jax.random.fold_in(key_of[3], part), 71), part)
    start = jnp.clip(jnp.exp(math.log(10.0) - 4.6051702 * jax.random.uniform(part_splits[2], (SEQS, COLBLK, ROWBLK, PIECE), jnp.float32) ** steps_of(part_splits[2], (SEQS, COLBLK, ROWBLK, PIECE), ((1, 4), (2, 4)), -0.2, 0.2)), 0.1, 10.0)
    return {"transition": transition, "emission": emission, "start": start}


def reference(transition, emission, start):
    message = start
    log_total = jnp.zeros((SEQS,), jnp.float32)
    history = []
    for step_idx in range(STEPS):
        lowered = message.astype(jnp.bfloat16)

        def add_block(running, block_idx):
            weight_rows = lax.dynamic_index_in_dim(transition, block_idx, 1, keepdims=False)
            weight_rows = weight_rows.reshape(COLBLK * PIECE, H)
            left_side = lax.dynamic_index_in_dim(lowered, block_idx, 2, keepdims=False)
            left_side = left_side.reshape(SEQS, COLBLK * PIECE)
            part_block = jnp.dot(left_side, weight_rows, preferred_element_type=jnp.float32)
            return running + part_block, None

        mixed, _ = lax.scan(add_block, jnp.zeros((SEQS, H), jnp.float32), jnp.arange(ROWBLK, dtype=jnp.int32))
        weighted = mixed.reshape(SEQS, COLBLK, ROWBLK, PIECE) * emission[step_idx].astype(jnp.float32)
        normal_sum = jnp.sum(weighted.reshape(SEQS, H), axis=1) / H
        message = weighted / normal_sum[:, None, None, None]
        log_total = log_total + jnp.log(normal_sum)
        history.append(message)
    return jnp.stack(history), log_total
```

```python
import functools

import jax
import jax.numpy as jnp
from jax import lax
from jax.experimental import pallas as pl
from jax.experimental.pallas import tpu as pltpu
from jax.sharding import PartitionSpec as P

STEPS = 4
HALVES = 2
TOP = 60000.0
START_TOP = 10.0


def product_kernel(num_x, with_peak, idx_ref, *refs):
    x_refs, t_ref, out_ref = refs[:num_x], refs[num_x], refs[num_x + 1]
    depth = x_refs[0].shape[1]
    total = None
    for q in range(num_x):
        rows = pl.ds(pl.multiple_of(idx_ref[1 + q] * depth, depth), depth)
        term = jnp.dot(x_refs[q][...], t_ref[rows, :], preferred_element_type=jnp.float32)
        total = term if total is None else total + term
    out_ref[0] = total
    if with_peak:
        peak_ref = refs[num_x + 2]
        here = jnp.max(t_ref[...].astype(jnp.float32).reshape(-1, 8, t_ref.shape[1]), axis=0)
        first = jnp.logical_and(pl.program_id(0) == 0, pl.program_id(1) == 0)

        @pl.when(first)
        def _():
            peak_ref[...] = here

        @pl.when(jnp.logical_not(first))
        def _():
            peak_ref[...] = jnp.maximum(peak_ref[...], here)


def product(indices, xs, table, blocks, with_peak):
    seqs, depth = xs[0].shape
    rows, width = table.shape
    piece = width // blocks
    tile = min(512, piece)
    per = piece // tile

    def place(o, c, idx):
        return (0, lax.rem(idx[0] + o, blocks) * per + c)

    out_shape = [jax.ShapeDtypeStruct((blocks, seqs, piece), jnp.float32)]
    out_specs = [pl.BlockSpec((1, seqs, tile), lambda o, c, idx: (o, 0, c))]
    if with_peak:
        out_shape.append(jax.ShapeDtypeStruct((8, tile), jnp.float32))
        out_specs.append(pl.BlockSpec((8, tile), lambda o, c, idx: (0, 0)))
    return pl.pallas_call(
        functools.partial(product_kernel, len(xs), with_peak),
        grid_spec=pltpu.PrefetchScalarGridSpec(
            num_scalar_prefetch=1,
            grid=(blocks, per),
            in_specs=[pl.BlockSpec((seqs, depth), lambda o, c, idx: (0, 0)) for _ in xs]
            + [pl.BlockSpec((rows, tile), place)],
            out_specs=out_specs,
        ),
        out_shape=out_shape,
        compiler_params=pltpu.CompilerParams(vmem_limit_bytes=32 * 2**20),
        cost_estimate=pl.CostEstimate(
            flops=2 * seqs * rows * width, bytes_accessed=2 * rows * width, transcendentals=0
        ),
        name="product_peak" if with_peak else "product",
    )(indices, *xs, table)


def gather_blocks(block):
    dp, sub = lax.axis_size("dp"), lax.axis_size("sub")
    found = [block]
    for k in range(1, dp):
        found.append(lax.ppermute(block, "dp", [(i, (i + k) % dp) for i in range(dp)]))
    out = []
    for l in range(sub):
        for item in found:
            out.append(item if l == 0 else lax.ppermute(item, "sub", [(i, (i + l) % sub) for i in range(sub)]))
    return out


def block_owners():
    dp, sub = lax.axis_size("dp"), lax.axis_size("sub")
    x, c = lax.axis_index("dp"), lax.axis_index("sub")
    return [
        lax.rem(x + dp - k, dp) * sub + lax.rem(c + sub - l, sub) for l in range(sub) for k in range(dp)
    ]


def line_sum(parts, into, back, first_into, first_back_r, first_back_l):
    n = lax.axis_size("state")
    right = left = None
    for k in range(1, n):
        scale = first_into if k == 1 else into
        to_r, to_l = parts[n - k], parts[k]
        if k > 1:
            to_r = to_r + right.astype(jnp.float32) * (first_back_r if k == 2 else back)
            to_l = to_l + left.astype(jnp.float32) * (first_back_l if k == 2 else back)
        right = lax.ppermute((to_r * scale).astype(jnp.float16), "state", [(i, i + 1) for i in range(k)])
        left = lax.ppermute((to_l * scale).astype(jnp.float16), "state", [(i, i - 1) for i in range(n - k, n)])
    last_r, last_l = (first_back_r, first_back_l) if n == 2 else (back, back)
    return parts[0] + right.astype(jnp.float32) * last_r + left.astype(jnp.float32) * last_l


def shards(transition, emission, start):
    seq_count = start.shape[0]
    piece = start.shape[3]
    blocks = lax.axis_size("state")
    me = lax.axis_index("state")
    table = transition.reshape(transition.shape[0] * piece, transition.shape[3])
    hidden = blocks * piece * lax.axis_size("dp") * lax.axis_size("sub")
    half = seq_count // HALVES
    indices = jnp.stack([me] + block_owners()).astype(jnp.int32)
    weights = jnp.transpose(emission[:, :, 0], (0, 2, 1, 3))
    weights = jnp.concatenate([weights, weights], axis=1)
    weights = lax.dynamic_slice_in_dim(weights, me, blocks, 1)

    messages = [start[h * half : (h + 1) * half, 0, 0] for h in range(HALVES)]
    history, normals = [], []
    into = back = None
    for step in range(STEPS):
        step_messages, step_normals = [], []
        for h in range(HALVES):
            rows = slice(h * half, (h + 1) * half)
            xs = gather_blocks(messages[h].astype(jnp.bfloat16))
            first = step == 0 and h == 0
            if first:
                parts, peak = product(indices, xs, table, blocks, True)
                own_peak = jnp.max(peak)
                peaks = lax.all_gather(jnp.full((1, 128), own_peak), "state", axis=0, tiled=True)[:, 0]
                top_peak = jnp.max(peaks)
                into = TOP / (hidden * top_peak)
                back = hidden * top_peak / TOP
                peak_r = lax.dynamic_index_in_dim(peaks, lax.rem(me + blocks - 1, blocks), 0, False)
                peak_l = lax.dynamic_index_in_dim(peaks, lax.rem(me + 1, blocks), 0, False)
                spread = hidden * START_TOP
                scales = (
                    into / START_TOP, back * START_TOP,
                    TOP / (spread * own_peak), spread * peak_r / TOP, spread * peak_l / TOP,
                )
            else:
                (parts,) = product(indices, xs, table, blocks, False)
                grow = START_TOP if step == 0 else 1.0
                scales = (into / grow, back * grow, into / grow, back * grow, back * grow)
            step_weights = weights[step, :, rows].astype(jnp.float32)
            own_sum = jnp.sum(parts * step_weights, axis=(0, 2))
            sums = lax.all_gather(own_sum[None], ("state", "dp", "sub"), axis=0, tiled=True)
            normal = jnp.sum(sums, axis=0) / hidden
            summed = line_sum([parts[o] for o in range(blocks)], *scales)
            message = summed * step_weights[0] / normal[:, None]
            messages[h] = message
            step_messages.append(message)
            step_normals.append(normal)
        history.append(jnp.concatenate(step_messages, axis=0))
        normals.append(jnp.concatenate(step_normals, axis=0))
    log_scale = functools.reduce(lambda a, b: a + b, [jnp.log(x) for x in normals])
    out = jnp.stack(history).reshape(STEPS, seq_count, 1, 1, piece)
    return out, log_scale


def solution(mesh):
    in_specs = (
        P(None, "state", None, ("dp", "sub")),
        P(None, "groups", ("dp", "sub"), None, None),
        P("groups", ("dp", "sub"), "state", None),
    )
    out_specs = (P(None, "groups", ("dp", "sub"), "state", None), P("groups"))
    return jax.shard_map(shards, mesh=mesh, in_specs=in_specs, out_specs=out_specs, check_vma=False)
```

```python
import functools

import jax
import jax.numpy as jnp
from jax import lax
from jax.experimental import pallas as pl
from jax.experimental.pallas import tpu as pltpu
from jax.sharding import PartitionSpec as P

STEPS = 4
HALVES = 2
TOP = 60000.0
START_TOP = 10.0


def product_kernel(num_x, with_peak, idx_ref, *refs):
    x_refs, t_ref, out_ref = refs[:num_x], refs[num_x], refs[num_x + 1]
    depth = x_refs[0].shape[1]
    total = None
    for q in range(num_x):
        rows = pl.ds(pl.multiple_of(idx_ref[1 + q] * depth, depth), depth)
        term = jnp.dot(x_refs[q][...], t_ref[rows, :], preferred_element_type=jnp.float32)
        total = term if total is None else total + term
    out_ref[0] = total
    if with_peak:
        peak_ref = refs[num_x + 2]
        here = jnp.max(t_ref[...].astype(jnp.float32).reshape(-1, 8, t_ref.shape[1]), axis=0)
        first = jnp.logical_and(pl.program_id(0) == 0, pl.program_id(1) == 0)

        @pl.when(first)
        def _():
            peak_ref[...] = here

        @pl.when(jnp.logical_not(first))
        def _():
            peak_ref[...] = jnp.maximum(peak_ref[...], here)


def product(indices, xs, table, blocks, with_peak):
    seqs, depth = xs[0].shape
    rows, width = table.shape
    piece = width // blocks
    tile = min(512, piece)
    per = piece // tile

    def place(o, c, idx):
        return (0, lax.rem(idx[0] + o, blocks) * per + c)

    out_shape = [jax.ShapeDtypeStruct((blocks, seqs, piece), jnp.float32)]
    out_specs = [pl.BlockSpec((1, seqs, tile), lambda o, c, idx: (o, 0, c))]
    if with_peak:
        out_shape.append(jax.ShapeDtypeStruct((8, tile), jnp.float32))
        out_specs.append(pl.BlockSpec((8, tile), lambda o, c, idx: (0, 0)))
    return pl.pallas_call(
        functools.partial(product_kernel, len(xs), with_peak),
        grid_spec=pltpu.PrefetchScalarGridSpec(
            num_scalar_prefetch=1,
            grid=(blocks, per),
            in_specs=[pl.BlockSpec((seqs, depth), lambda o, c, idx: (0, 0)) for _ in xs]
            + [pl.BlockSpec((rows, tile), place)],
            out_specs=out_specs,
        ),
        out_shape=out_shape,
        compiler_params=pltpu.CompilerParams(vmem_limit_bytes=32 * 2**20),
        cost_estimate=pl.CostEstimate(
            flops=2 * seqs * rows * width, bytes_accessed=2 * rows * width, transcendentals=0
        ),
        name="product_peak" if with_peak else "product",
    )(indices, *xs, table)


def gather_blocks(block):
    dp, sub = lax.axis_size("dp"), lax.axis_size("sub")
    found = [block]
    for k in range(1, dp):
        found.append(lax.ppermute(block, "dp", [(i, (i + k) % dp) for i in range(dp)]))
    out = []
    for l in range(sub):
        for item in found:
            out.append(item if l == 0 else lax.ppermute(item, "sub", [(i, (i + l) % sub) for i in range(sub)]))
    return out


def block_owners():
    dp, sub = lax.axis_size("dp"), lax.axis_size("sub")
    x, c = lax.axis_index("dp"), lax.axis_index("sub")
    return [
        lax.rem(x + dp - k, dp) * sub + lax.rem(c + sub - l, sub) for l in range(sub) for k in range(dp)
    ]


def line_sum(parts, into, back, first_into, first_back_r, first_back_l):
    n = lax.axis_size("state")
    right = left = None
    for k in range(1, n):
        scale = first_into if k == 1 else into
        to_r, to_l = parts[n - k], parts[k]
        if k > 1:
            to_r = to_r + right.astype(jnp.float32) * (first_back_r if k == 2 else back)
            to_l = to_l + left.astype(jnp.float32) * (first_back_l if k == 2 else back)
        right = lax.ppermute((to_r * scale).astype(jnp.float16), "state", [(i, i + 1) for i in range(k)])
        left = lax.ppermute((to_l * scale).astype(jnp.float16), "state", [(i, i - 1) for i in range(n - k, n)])
    last_r, last_l = (first_back_r, first_back_l) if n == 2 else (back, back)
    return parts[0] + right.astype(jnp.float32) * last_r + left.astype(jnp.float32) * last_l


def general(transition, emission, start):
    seq_count = start.shape[0]
    piece = start.shape[3]
    blocks = lax.axis_size("state")
    me = lax.axis_index("state")
    table = transition.reshape(transition.shape[0] * piece, transition.shape[3])
    hidden = blocks * piece * lax.axis_size("dp") * lax.axis_size("sub")
    half = seq_count // HALVES
    indices = jnp.stack([me] + block_owners()).astype(jnp.int32)
    weights = jnp.transpose(emission[:, :, 0], (0, 2, 1, 3))
    weights = jnp.concatenate([weights, weights], axis=1)
    weights = lax.dynamic_slice_in_dim(weights, me, blocks, 1)

    messages = [start[h * half : (h + 1) * half, 0, 0] for h in range(HALVES)]
    history, normals = [], []
    into = back = None
    for step in range(STEPS):
        step_messages, step_normals = [], []
        for h in range(HALVES):
            rows = slice(h * half, (h + 1) * half)
            xs = gather_blocks(messages[h].astype(jnp.bfloat16))
            first = step == 0 and h == 0
            if first:
                parts, peak = product(indices, xs, table, blocks, True)
                own_peak = jnp.max(peak)
                peaks = lax.all_gather(jnp.full((1, 128), own_peak), "state", axis=0, tiled=True)[:, 0]
                top_peak = jnp.max(peaks)
                into = TOP / (hidden * top_peak)
                back = hidden * top_peak / TOP
                peak_r = lax.dynamic_index_in_dim(peaks, lax.rem(me + blocks - 1, blocks), 0, False)
                peak_l = lax.dynamic_index_in_dim(peaks, lax.rem(me + 1, blocks), 0, False)
                spread = hidden * START_TOP
                scales = (
                    into / START_TOP, back * START_TOP,
                    TOP / (spread * own_peak), spread * peak_r / TOP, spread * peak_l / TOP,
                )
            else:
                (parts,) = product(indices, xs, table, blocks, False)
                grow = START_TOP if step == 0 else 1.0
                scales = (into / grow, back * grow, into / grow, back * grow, back * grow)
            step_weights = weights[step, :, rows].astype(jnp.float32)
            own_sum = jnp.sum(parts * step_weights, axis=(0, 2))
            sums = lax.all_gather(own_sum[None], ("state", "dp", "sub"), axis=0, tiled=True)
            normal = jnp.sum(sums, axis=0) / hidden
            summed = line_sum([parts[o] for o in range(blocks)], *scales)
            message = summed * step_weights[0] / normal[:, None]
            messages[h] = message
            step_messages.append(message)
            step_normals.append(normal)
        history.append(jnp.concatenate(step_messages, axis=0))
        normals.append(jnp.concatenate(step_normals, axis=0))
    log_scale = functools.reduce(lambda a, b: a + b, [jnp.log(x) for x in normals])
    out = jnp.stack(history).reshape(STEPS, seq_count, 1, 1, piece)
    return out, log_scale


SLOTS = ((3, 2, 1, 0), (0, 2, 3, 1), (3, 1, 0, 2), (0, 1, 2, 3))
PAIRS = [(0, 1), (1, 0), (2, 3), (3, 2)]
FROM_OUTER = [(0, 2), (3, 1)]
FROM_INNER = [(1, 2), (2, 1)]
LAST = [(1, 3), (2, 0), (0, 1), (3, 2)]
CHUNK = 256
VMEM = pl.BlockSpec(memory_space=pltpu.VMEM)
SMEM = pl.BlockSpec(memory_space=pltpu.SMEM)
ANY = pl.BlockSpec(memory_space=pl.ANY)
F32, BF16 = jnp.float32, jnp.bfloat16


def call(body, out_shape, out_specs, in_specs, scratch=(), aliases=None, flops=0, size=0, name=None):
    return pl.pallas_call(
        body,
        out_shape=out_shape,
        in_specs=in_specs,
        out_specs=out_specs,
        scratch_shapes=list(scratch),
        input_output_aliases=aliases or {},
        compiler_params=pltpu.CompilerParams(vmem_limit_bytes=12 * 2**20),
        cost_estimate=pl.CostEstimate(flops=flops, bytes_accessed=size, transcendentals=0),
        name=name,
    )


def shape(dims, dtype):
    return jax.ShapeDtypeStruct(dims, dtype)


def encode(x):
    x = x * x
    x = x * x
    return (x * x).astype(BF16)


def decode(y):
    y = y.astype(F32)
    return jnp.where(y > 0.0, jnp.exp2(0.125 * jnp.log2(y)), 0.0)


def load_body(table_ref, held_ref, peak_ref, sems):
    count = sems.shape[0]
    rows = table_ref.shape[0] // count
    copies = [
        pltpu.make_async_copy(table_ref.at[pl.ds(i * rows, rows)], held_ref.at[pl.ds(i * rows, rows)], sems.at[i])
        for i in range(count)
    ]
    for copy in copies:
        copy.start()
    top = jnp.zeros((16, table_ref.shape[1]), BF16)
    for i, copy in enumerate(copies):
        copy.wait()

        def step(k, best, i=i):
            at = pl.multiple_of(i * rows + k * 16, 16)
            return jnp.maximum(best, held_ref[pl.ds(at, 16), :])

        top = lax.fori_loop(0, rows // 16, step, top)
    peak_ref[...] = jnp.full(peak_ref.shape, jnp.max(top.astype(F32)), F32)


def load(table):
    return call(
        load_body, (pltpu.VMEM(table.shape, table.dtype), shape((8, 128), F32)), (VMEM, VMEM), [ANY],
        [pltpu.SemaphoreType.DMA((8,))], size=2 * table.size, name="load_table",
    )(table)


def merge_body(combine, a, b, c, d, table_ref, out):
    out[...] = combine(combine(a[...], b[...]), combine(c[...], d[...]))


def merge(combine, tiles, table):
    body = functools.partial(merge_body, combine)
    return call(body, shape((8, 128), F32), VMEM, [VMEM] * 5, size=1000, name="merge")(*tiles, table)


def all_swaps(tile, axes):
    return [tile] + [lax.ppermute(tile, axes, [(i, i ^ k) for i in range(4)]) for k in range(1, 4)]


def products(idx, slot, x_refs, table_ref, weights_ref, sums_ref, put):
    piece = weights_ref.shape[1]
    depth = x_refs[0].shape[1]

    def chunk(c, _):
        at = pl.multiple_of(c * CHUNK, CHUNK)
        cols = pl.ds(pl.multiple_of(idx[slot] * piece + at, CHUNK), CHUNK)
        total = None
        for q, x in enumerate(x_refs):
            rows = pl.ds(pl.multiple_of(idx[4 + q] * depth, depth), depth)
            term = jnp.dot(x[...], table_ref[rows, cols], preferred_element_type=F32)
            total = term if total is None else total + term
        here = pl.ds(at, CHUNK)
        put(here, total)
        weighted = total * weights_ref[:, here].astype(F32)
        sums = sums_ref[...]
        for k in range(CHUNK // 128):
            sums = sums + weighted[:, k * 128 : (k + 1) * 128]
        sums_ref[...] = sums
        return 0

    lax.fori_loop(0, piece // CHUNK, chunk, 0)


def weight_copies(idx, slots, step, at, half, weights_ref, held, sems):
    return [
        pltpu.make_async_copy(weights_ref.at[step, idx[s], pl.ds(at, half)], held.at[k], sems.at[k])
        for k, s in enumerate(slots)
    ]


def first_body(step, at, spread, idx, peak_ref, *refs):
    xs, (table_ref, weights_ref, out0, out1, sums_ref, held, sems) = refs[:4], refs[4:]
    copies = weight_copies(idx, (0, 1), step, at, out0.shape[0], weights_ref, held, sems)
    for copy in copies:
        copy.start()
    scale = (TOP / spread) / peak_ref[0:1, 0:1]
    sums_ref[...] = jnp.zeros_like(sums_ref)
    for slot, out in enumerate((out0, out1)):
        copies[slot].wait()

        def put(here, total, out=out):
            out[:, here] = encode(total * scale)

        products(idx, slot, xs, table_ref, held.at[slot], sums_ref, put)


def second_body(step, at, idx, sums_in, *refs):
    xs, (table_ref, weights_ref, out0, out1, total_ref, sums_ref, held, sems) = refs[:4], refs[4:]
    copies = weight_copies(idx, (2, 3), step, at, out0.shape[0], weights_ref, held, sems)
    for copy in copies:
        copy.start()
    sums_ref[...] = sums_in[...]
    for k, out in enumerate((out0, out1)):
        copies[k].wait()

        def put(here, total, out=out):
            out[:, here] = total

        products(idx, 2 + k, xs, table_ref, held.at[k], sums_ref, put)
    total_ref[...] = jnp.broadcast_to(jnp.sum(sums_ref[...].T, axis=0, keepdims=True), total_ref.shape)


def far_body(spread, idx, peak_ref, part_ref, pair_ref, table_ref, out):
    scale = (TOP / spread) / peak_ref[0:1, 0:1]

    @pl.when(idx[8] == 1)
    def _():
        out[...] = encode(part_ref[...] * scale + decode(pair_ref[...]))

    @pl.when(idx[8] == 0)
    def _():
        out[...] = encode(part_ref[...] * scale)


def last_body(step, at, spread, hidden, has_out, idx, peak_ref, own_ref, pair_ref, outer_ref, inner_ref, far_ref, *refs):
    sums, refs = refs[:4], refs[4:]
    table_ref, weights_ref = refs[:2]
    lowered_ref, normal_ref, out_ref, total_ref, weight_held, made, sems = refs[3 if has_out else 2 :]
    half = own_ref.shape[0]
    fetch = pltpu.make_async_copy(weights_ref.at[step, idx[3], pl.ds(at, half)], weight_held, sems.at[0])
    fetch.start()
    unscale = peak_ref[0:1, 0:1] * (spread / TOP)
    normal = ((sums[0][...] + sums[1][...]) + (sums[2][...] + sums[3][...])) / hidden
    normal_ref[...] = normal
    inverse = jnp.broadcast_to(1.0 / normal[0:1, :], (half, half)).T

    @pl.when(idx[8] == 1)
    def _():
        total_ref[...] = (decode(outer_ref[...]) + decode(inner_ref[...])) + decode(far_ref[...])

    @pl.when(idx[8] == 0)
    def _():
        total_ref[...] = decode(pair_ref[...]) + decode(far_ref[...])

    fetch.wait()
    for k in range(own_ref.shape[1] // 128):
        here = slice(k * 128, (k + 1) * 128)
        mixed = own_ref[:, here] + total_ref[:, here] * unscale
        message = mixed * weight_held[:, here].astype(F32) * inverse
        lowered_ref[:, here] = message.astype(BF16)
        made[:, k, :] = message
    write = pltpu.make_async_copy(made, out_ref.at[step, pl.ds(at, half)], sems.at[1])
    write.start()
    write.wait()


def fast(transition, emission, start):
    seqs, piece = start.shape[0], start.shape[3]
    hidden = 16 * piece
    half = seqs // HALVES
    table = transition.reshape(4 * piece, 4 * piece)
    me = lax.axis_index("state")
    d = lax.axis_index("dp") * 2 + lax.axis_index("sub")
    slots = jnp.asarray(SLOTS, jnp.int32)[me]
    inner = jnp.logical_and(me > 0, me < 3)
    idx = jnp.concatenate(
        [slots, jnp.stack([d, d ^ 1, d ^ 2, d ^ 3, inner]).astype(jnp.int32)]
    )
    weights = jnp.transpose(emission[:, :, 0], (0, 2, 1, 3))
    tile = shape((8, 128), F32)
    wide, code = shape((half, piece), F32), shape((half, piece), BF16)
    dma = pltpu.SemaphoreType.DMA

    table, weights, idx = lax.optimization_barrier((table, weights, idx))
    weights = pltpu.with_memory_space_constraint(weights, pltpu.HBM)
    held, peak = load(table)
    held = pltpu.with_memory_space_constraint(held, pltpu.VMEM)
    peak = merge(jnp.maximum, all_swaps(peak, "state"), held)
    lowered = [start[h * half : (h + 1) * half, 0, 0].astype(BF16) for h in range(HALVES)]
    out, normals = None, []
    work = 2 * half * 4 * piece * 2 * piece
    for step in range(STEPS):
        spread = hidden * 1.01 * (START_TOP if step == 0 else 1.0)
        for h in range(HALVES):
            at = h * half
            own = lowered[h]
            across = lax.ppermute(own, "dp", [(0, 1), (1, 0)])
            xs = [own, lax.ppermute(own, "sub", [(0, 1), (1, 0)]), across, lax.ppermute(across, "sub", [(0, 1), (1, 0)])]
            send0, send1, sums = call(
                functools.partial(first_body, step, at, spread),
                (code, code, shape((half, 128), F32)), (VMEM,) * 3, [SMEM] + [VMEM] * 6 + [ANY],
                [pltpu.VMEM((2, half, piece), BF16), dma((2,))], flops=work, size=2**20, name="product_first",
            )(idx, peak, *xs, held, weights)
            pair = lax.ppermute(send0, "state", PAIRS)
            from_outer = lax.ppermute(send1, "state", FROM_OUTER)
            from_inner = lax.ppermute(send1, "state", FROM_INNER)
            part2, part3, total = call(
                functools.partial(second_body, step, at),
                (wide, wide, tile), (VMEM,) * 3, [SMEM] + [VMEM] * 6 + [ANY],
                [pltpu.VMEM((half, 128), F32), pltpu.VMEM((2, half, piece), BF16), dma((2,))],
                flops=work, size=2**20, name="product_second",
            )(idx, sums, *xs, held, weights)
            total = merge(jnp.add, all_swaps(total, ("dp", "sub")), held)
            totals = all_swaps(total, "state")
            send2 = call(
                functools.partial(far_body, spread), code, VMEM, [SMEM] + [VMEM] * 4, size=2**20, name="far_block"
            )(idx, peak, part2, pair, held)
            far = lax.ppermute(send2, "state", LAST)
            has_out = out is not None
            args = [idx, peak, part3, pair, from_outer, from_inner, far, *totals, held, weights]
            specs = [SMEM] + [VMEM] * 11 + [ANY]
            if has_out:
                args, specs = args + [out], specs + [ANY]
            lowered[h], normal, out = call(
                functools.partial(last_body, step, at, spread, hidden, has_out),
                (code, tile, shape((STEPS, seqs, piece // 128, 128), F32)), (VMEM, VMEM, ANY), specs,
                [wide_scratch(half, piece), pltpu.VMEM((half, piece), BF16),
                 pltpu.VMEM((half, piece // 128, 128), F32), dma((2,))],
                aliases={len(args) - 1: 2} if has_out else None, size=2**21, name="normalise",
            )(*args)
            normals.append(normal[0])
    logs = jnp.log(jnp.stack(normals).reshape(STEPS, seqs))
    log_scale = ((logs[0] + logs[1]) + logs[2]) + logs[3]
    return out.reshape(STEPS, seqs, 1, 1, piece), log_scale


def wide_scratch(half, piece):
    return pltpu.VMEM((half, piece), F32)


def shards(transition, emission, start):
    sizes = [lax.axis_size(name) for name in ("state", "dp", "sub")]
    if sizes == [4, 2, 2] and start.shape[0] == HALVES * 128 and start.shape[3] % CHUNK == 0:
        return fast(transition, emission, start)
    return general(transition, emission, start)


def solution(mesh):
    in_specs = (
        P(None, "state", None, ("dp", "sub")),
        P(None, "groups", ("dp", "sub"), None, None),
        P("groups", ("dp", "sub"), "state", None),
    )
    out_specs = (P(None, "groups", ("dp", "sub"), "state", None), P("groups"))
    return jax.shard_map(shards, mesh=mesh, in_specs=in_specs, out_specs=out_specs, check_vma=False)
```

```python
import functools

import jax
import jax.numpy as jnp
from jax import lax
from jax.experimental import pallas as pl
from jax.experimental.pallas import tpu as pltpu
from jax.sharding import PartitionSpec as P

STEPS = 4
HALVES = 2
TOP = 60000.0
START_TOP = 10.0


def product_kernel(num_x, with_peak, idx_ref, *refs):
    x_refs, t_ref, out_ref = refs[:num_x], refs[num_x], refs[num_x + 1]
    depth = x_refs[0].shape[1]
    total = None
    for q in range(num_x):
        rows = pl.ds(pl.multiple_of(idx_ref[1 + q] * depth, depth), depth)
        term = jnp.dot(x_refs[q][...], t_ref[rows, :], preferred_element_type=jnp.float32)
        total = term if total is None else total + term
    out_ref[0] = total
    if with_peak:
        peak_ref = refs[num_x + 2]
        here = jnp.max(t_ref[...].astype(jnp.float32).reshape(-1, 8, t_ref.shape[1]), axis=0)
        first = jnp.logical_and(pl.program_id(0) == 0, pl.program_id(1) == 0)

        @pl.when(first)
        def _():
            peak_ref[...] = here

        @pl.when(jnp.logical_not(first))
        def _():
            peak_ref[...] = jnp.maximum(peak_ref[...], here)


def product(indices, xs, table, blocks, with_peak):
    seqs, depth = xs[0].shape
    rows, width = table.shape
    piece = width // blocks
    tile = min(512, piece)
    per = piece // tile

    def place(o, c, idx):
        return (0, lax.rem(idx[0] + o, blocks) * per + c)

    out_shape = [jax.ShapeDtypeStruct((blocks, seqs, piece), jnp.float32)]
    out_specs = [pl.BlockSpec((1, seqs, tile), lambda o, c, idx: (o, 0, c))]
    if with_peak:
        out_shape.append(jax.ShapeDtypeStruct((8, tile), jnp.float32))
        out_specs.append(pl.BlockSpec((8, tile), lambda o, c, idx: (0, 0)))
    return pl.pallas_call(
        functools.partial(product_kernel, len(xs), with_peak),
        grid_spec=pltpu.PrefetchScalarGridSpec(
            num_scalar_prefetch=1,
            grid=(blocks, per),
            in_specs=[pl.BlockSpec((seqs, depth), lambda o, c, idx: (0, 0)) for _ in xs]
            + [pl.BlockSpec((rows, tile), place)],
            out_specs=out_specs,
        ),
        out_shape=out_shape,
        compiler_params=pltpu.CompilerParams(vmem_limit_bytes=32 * 2**20),
        cost_estimate=pl.CostEstimate(
            flops=2 * seqs * rows * width, bytes_accessed=2 * rows * width, transcendentals=0
        ),
        name="product_peak" if with_peak else "product",
    )(indices, *xs, table)


def gather_blocks(block):
    dp, sub = lax.axis_size("dp"), lax.axis_size("sub")
    found = [block]
    for k in range(1, dp):
        found.append(lax.ppermute(block, "dp", [(i, (i + k) % dp) for i in range(dp)]))
    out = []
    for l in range(sub):
        for item in found:
            out.append(item if l == 0 else lax.ppermute(item, "sub", [(i, (i + l) % sub) for i in range(sub)]))
    return out


def block_owners():
    dp, sub = lax.axis_size("dp"), lax.axis_size("sub")
    x, c = lax.axis_index("dp"), lax.axis_index("sub")
    return [
        lax.rem(x + dp - k, dp) * sub + lax.rem(c + sub - l, sub) for l in range(sub) for k in range(dp)
    ]


def line_sum(parts, into, back, first_into, first_back_r, first_back_l):
    n = lax.axis_size("state")
    right = left = None
    for k in range(1, n):
        scale = first_into if k == 1 else into
        to_r, to_l = parts[n - k], parts[k]
        if k > 1:
            to_r = to_r + right.astype(jnp.float32) * (first_back_r if k == 2 else back)
            to_l = to_l + left.astype(jnp.float32) * (first_back_l if k == 2 else back)
        right = lax.ppermute((to_r * scale).astype(jnp.float16), "state", [(i, i + 1) for i in range(k)])
        left = lax.ppermute((to_l * scale).astype(jnp.float16), "state", [(i, i - 1) for i in range(n - k, n)])
    last_r, last_l = (first_back_r, first_back_l) if n == 2 else (back, back)
    return parts[0] + right.astype(jnp.float32) * last_r + left.astype(jnp.float32) * last_l


def general(transition, emission, start):
    seq_count = start.shape[0]
    piece = start.shape[3]
    blocks = lax.axis_size("state")
    me = lax.axis_index("state")
    table = transition.reshape(transition.shape[0] * piece, transition.shape[3])
    hidden = blocks * piece * lax.axis_size("dp") * lax.axis_size("sub")
    half = seq_count // HALVES
    indices = jnp.stack([me] + block_owners()).astype(jnp.int32)
    weights = jnp.transpose(emission[:, :, 0], (0, 2, 1, 3))
    weights = jnp.concatenate([weights, weights], axis=1)
    weights = lax.dynamic_slice_in_dim(weights, me, blocks, 1)

    messages = [start[h * half : (h + 1) * half, 0, 0] for h in range(HALVES)]
    history, normals = [], []
    into = back = None
    for step in range(STEPS):
        step_messages, step_normals = [], []
        for h in range(HALVES):
            rows = slice(h * half, (h + 1) * half)
            xs = gather_blocks(messages[h].astype(jnp.bfloat16))
            first = step == 0 and h == 0
            if first:
                parts, peak = product(indices, xs, table, blocks, True)
                own_peak = jnp.max(peak)
                peaks = lax.all_gather(jnp.full((1, 128), own_peak), "state", axis=0, tiled=True)[:, 0]
                top_peak = jnp.max(peaks)
                into = TOP / (hidden * top_peak)
                back = hidden * top_peak / TOP
                peak_r = lax.dynamic_index_in_dim(peaks, lax.rem(me + blocks - 1, blocks), 0, False)
                peak_l = lax.dynamic_index_in_dim(peaks, lax.rem(me + 1, blocks), 0, False)
                spread = hidden * START_TOP
                scales = (
                    into / START_TOP, back * START_TOP,
                    TOP / (spread * own_peak), spread * peak_r / TOP, spread * peak_l / TOP,
                )
            else:
                (parts,) = product(indices, xs, table, blocks, False)
                grow = START_TOP if step == 0 else 1.0
                scales = (into / grow, back * grow, into / grow, back * grow, back * grow)
            step_weights = weights[step, :, rows].astype(jnp.float32)
            own_sum = jnp.sum(parts * step_weights, axis=(0, 2))
            sums = lax.all_gather(own_sum[None], ("state", "dp", "sub"), axis=0, tiled=True)
            normal = jnp.sum(sums, axis=0) / hidden
            summed = line_sum([parts[o] for o in range(blocks)], *scales)
            message = summed * step_weights[0] / normal[:, None]
            messages[h] = message
            step_messages.append(message)
            step_normals.append(normal)
        history.append(jnp.concatenate(step_messages, axis=0))
        normals.append(jnp.concatenate(step_normals, axis=0))
    log_scale = functools.reduce(lambda a, b: a + b, [jnp.log(x) for x in normals])
    out = jnp.stack(history).reshape(STEPS, seq_count, 1, 1, piece)
    return out, log_scale


SLOTS = ((3, 2, 1, 0), (0, 2, 3, 1), (3, 1, 0, 2), (0, 1, 2, 3))
PAIRS = [(0, 1), (1, 0), (2, 3), (3, 2)]
FROM_OUTER = [(0, 2), (3, 1)]
FROM_INNER = [(1, 2), (2, 1)]
LAST = [(1, 3), (2, 0), (0, 1), (3, 2)]
CHUNK = 512
VMEM = pl.BlockSpec(memory_space=pltpu.VMEM)
SMEM = pl.BlockSpec(memory_space=pltpu.SMEM)
ANY = pl.BlockSpec(memory_space=pl.ANY)
F32, BF16 = jnp.float32, jnp.bfloat16


def shape(dims, dtype):
    return jax.ShapeDtypeStruct(dims, dtype)


class Order:
    def __init__(self):
        self.last = None

    def __call__(self, body, outs, out_specs, args, specs, scratch=(), aliases=None, name=None):
        count = len(args)
        if self.last is not None:
            args, specs = [*args, self.last], [*specs, ANY]
        extra = len(args) - count

        def run(*refs):
            body(*refs[:count], *refs[count + extra :])

        result = pl.pallas_call(
            run,
            out_shape=tuple(outs),
            in_specs=list(specs),
            out_specs=tuple(out_specs),
            scratch_shapes=list(scratch),
            input_output_aliases=aliases or {},
            compiler_params=pltpu.CompilerParams(vmem_limit_bytes=12 * 2**20),
            cost_estimate=pl.CostEstimate(flops=0, bytes_accessed=1024, transcendentals=0),
            name=name,
        )(*args)
        self.last = result[0]
        return result


def encode(x):
    x = x * x
    x = x * x
    return (x * x).astype(BF16)


def decode(y):
    y = y.astype(F32)
    return jnp.where(y > 0.0, jnp.exp2(0.125 * jnp.log2(y)), 0.0)


def load_body(table_ref, held_ref, peak_ref, sems):
    count = sems.shape[0]
    rows = table_ref.shape[0] // count
    copies = [
        pltpu.make_async_copy(table_ref.at[pl.ds(i * rows, rows)], held_ref.at[pl.ds(i * rows, rows)], sems.at[i])
        for i in range(count)
    ]
    for copy in copies:
        copy.start()
    top = jnp.zeros((16, table_ref.shape[1]), BF16)
    for i, copy in enumerate(copies):
        copy.wait()

        def step(k, best, i=i):
            at = pl.multiple_of(i * rows + k * 16, 16)
            return jnp.maximum(best, held_ref[pl.ds(at, 16), :])

        top = lax.fori_loop(0, rows // 16, step, top)
    peak_ref[...] = jnp.full(peak_ref.shape, jnp.max(top.astype(F32)), F32)


def corner(ref):
    return ref[0:1, 0:1]


def top_of(peaks):
    return jnp.maximum(
        jnp.maximum(corner(peaks[0]), corner(peaks[1])), jnp.maximum(corner(peaks[2]), corner(peaks[3]))
    )


def all_swaps(tile, axes):
    return [tile] + [lax.ppermute(tile, axes, [(i, i ^ k) for i in range(4)]) for k in range(1, 4)]


def products(idx, slot, left_ref, table_ref, weights_ref, sums_ref, put):
    piece = weights_ref.shape[1]
    for c in range(piece // CHUNK):
        here = slice(c * CHUNK, (c + 1) * CHUNK)
        cols = pl.ds(pl.multiple_of(idx[slot] * piece + c * CHUNK, CHUNK), CHUNK)
        total = jnp.dot(left_ref[...], table_ref[:, cols], preferred_element_type=F32)
        put(here, total)
        weighted = total * weights_ref[:, here].astype(F32)
        sums = sums_ref[...]
        for k in range(CHUNK // 128):
            sums = sums + weighted[:, k * 128 : (k + 1) * 128]
        sums_ref[...] = sums


def fetch_weights(idx, slots, step, at, weights_ref, held, sems):
    half = held.shape[1]
    copies = [
        pltpu.make_async_copy(weights_ref.at[step, idx[s], pl.ds(at, half)], held.at[k], sems.at[k])
        for k, s in enumerate(slots)
    ]
    for copy in copies:
        copy.start()
    return copies


def first_body(step, at, spread, idx, x0, x1, x2, x3, table_ref, weights_ref, *refs):
    peaks, (out_ref, sums_ref, left_ref, held, sems) = refs[:-5], refs[-5:]
    (copy,) = fetch_weights(idx, (0,), step, at, weights_ref, held, sems)
    depth = x0.shape[1]
    for q, x in enumerate((x0, x1, x2, x3)):
        left_ref[:, pl.ds(pl.multiple_of(idx[4 + q] * depth, depth), depth)] = x[...]
    scale = (TOP / spread) / (corner(peaks[0]) if step == 0 else top_of(peaks))
    sums_ref[...] = jnp.zeros_like(sums_ref)
    copy.wait()

    def put(here, total):
        out_ref[:, here] = encode(total * scale)

    products(idx, 0, left_ref, table_ref, held.at[0], sums_ref, put)


def next_body(step, at, spread, idx, left_ref, sums_in, table_ref, weights_ref, *refs):
    peaks, (out_ref, sums_ref, held, sems) = refs[:-4], refs[-4:]
    (copy,) = fetch_weights(idx, (1,), step, at, weights_ref, held, sems)
    scale = (TOP / spread) / (corner(peaks[0]) if step == 0 else top_of(peaks))
    sums_ref[...] = sums_in[...]
    copy.wait()

    def put(here, total):
        out_ref[:, here] = encode(total * scale)

    products(idx, 1, left_ref, table_ref, held.at[0], sums_ref, put)


def rest_body(step, at, write, has_out, idx, left_ref, sums_in, table_ref, weights_ref, *refs):
    if write is not None:
        message_ref, refs = refs[0], refs[2 if has_out else 1 :]
    (part_ref, own_ref, tile_ref, own_weights_ref), refs = refs[:4], refs[4:]
    if write is not None:
        out_ref, refs = refs[0], refs[1:]
    sums_ref, held, sems = refs
    if write is not None:
        copy_out = pltpu.make_async_copy(message_ref, out_ref.at[write[0], pl.ds(write[1], message_ref.shape[0])], sems.at[2])
        copy_out.start()
    copies = fetch_weights(idx, (2, 3), step, at, weights_ref, held, sems)
    sums_ref[...] = sums_in[...]
    for k, out in enumerate((part_ref, own_ref)):
        copies[k].wait()

        def put(here, total, out=out):
            out[:, here] = total

        products(idx, 2 + k, left_ref, table_ref, held.at[k], sums_ref, put)
    own_weights_ref[...] = held[1]
    tile_ref[...] = jnp.broadcast_to(jnp.sum(sums_ref[...].T, axis=0, keepdims=True), tile_ref.shape)
    if write is not None:
        copy_out.wait()


def add_body(a_ref, b_ref, table_ref, *refs):
    refs[-1][...] = a_ref[...] + b_ref[...]


def far_body(step, spread, forward, idx, part_ref, pair_ref, table_ref, *refs):
    peaks, refs = refs[:4], refs[4:]
    if forward:
        refs[2][...] = refs[0][...]
        refs = refs[1:]
    out = refs[0]
    top = top_of(peaks)
    scale = (TOP / spread) / top

    @pl.when(idx[8] == 1)
    def _():
        pair = decode(pair_ref[...])
        if step == 0:
            pair = pair * (corner(peaks[1]) / top)
        out[...] = encode(part_ref[...] * scale + pair)

    @pl.when(idx[8] == 0)
    def _():
        out[...] = encode(part_ref[...] * scale)


def last_body(step, spread, hidden, finish, idx, own_ref, pair_ref, outer_ref, inner_ref, far_ref, mine_ref, theirs_ref, weights_ref, table_ref, *refs):
    peaks, logs_in, refs = refs[:4], refs[4] if step else None, refs[5 if step else 4 :]
    if finish is not None:
        refs = refs[1:]
    lowered_ref, message_ref, logs_ref = refs[:3]
    if finish is not None:
        out_ref, mixed_ref, sem = refs[3:]
    else:
        (mixed_ref,) = refs[3:]
    half = own_ref.shape[0]
    top = top_of(peaks)
    unscale = top * (spread / TOP)
    normal = (mine_ref[...] + theirs_ref[...]) / hidden
    logs = jnp.log(normal)
    logs_ref[...] = logs if logs_in is None else logs_in[...] + logs
    inverse = jnp.broadcast_to(1.0 / normal[0:1, :], (half, half)).T

    def sent_by(k):
        return corner(peaks[k]) * (spread / TOP) if step == 0 else unscale

    @pl.when(idx[8] == 1)
    def _():
        mixed_ref[...] = (
            own_ref[...]
            + (decode(outer_ref[...]) * sent_by(2) + decode(inner_ref[...]) * sent_by(3))
            + decode(far_ref[...]) * unscale
        )

    @pl.when(idx[8] == 0)
    def _():
        mixed_ref[...] = own_ref[...] + (decode(pair_ref[...]) * sent_by(1) + decode(far_ref[...]) * unscale)

    for k in range(own_ref.shape[1] // 128):
        here = slice(k * 128, (k + 1) * 128)
        message = mixed_ref[:, here] * weights_ref[:, here].astype(F32) * inverse
        lowered_ref[:, here] = message.astype(BF16)
        message_ref[:, k, :] = message
    if finish is not None:
        write = pltpu.make_async_copy(message_ref, out_ref.at[finish[0], pl.ds(finish[1], half)], sem)
        write.start()
        write.wait()


def fast(transition, emission, start):
    seqs, piece = start.shape[0], start.shape[3]
    hidden = 16 * piece
    half = seqs // HALVES
    table = transition.reshape(4 * piece, 4 * piece)
    me = lax.axis_index("state")
    d = lax.axis_index("dp") * 2 + lax.axis_index("sub")
    slots = jnp.asarray(SLOTS, jnp.int32)[me]
    inner = jnp.logical_and(me > 0, me < 3)
    idx = jnp.concatenate([slots, jnp.stack([d, d ^ 1, d ^ 2, d ^ 3, inner]).astype(jnp.int32)])
    weights = jnp.transpose(emission[:, :, 0], (0, 2, 1, 3))
    wide, code = shape((half, piece), F32), shape((half, piece), BF16)
    square, tile = shape((half, 128), F32), shape((8, 128), F32)
    rows = shape((half, piece // 128, 128), F32)
    out_shape = shape((STEPS, seqs, piece // 128, 128), F32)
    dma = pltpu.SemaphoreType.DMA
    order = Order()

    table, weights, idx = lax.optimization_barrier((table, weights, idx))
    weights = pltpu.with_memory_space_constraint(weights, pltpu.HBM)
    held, peak = order(
        load_body, [pltpu.VMEM(table.shape, table.dtype), shape((8, 128), F32)], [VMEM] * 2, [table], [ANY],
        [dma((8,))], name="load_table",
    )
    order.last = peak
    held = pltpu.with_memory_space_constraint(held, pltpu.VMEM)
    peaks = all_swaps(peak, "state")

    spreads = [hidden * 1.01 * (START_TOP if step == 0 else 1.0) for step in range(STEPS)]
    state = [{"lowered": start[h * half : (h + 1) * half, 0, 0].astype(BF16)} for h in range(HALVES)]
    box = {"out": None}

    def swap(h, axis, k):
        s = state[h]
        s["their"] = lax.ppermute(s["tile"], axis, [(i, i ^ k) for i in range(lax.axis_size(axis))])

    def add(h, after=()):
        s = state[h]
        s["tile"] = order(
            add_body, [tile], [VMEM], [s["tile"], s["their"], held, *after], [VMEM] * 3 + [ANY] * len(after),
            name="add_sums",
        )[0]

    def gather(h):
        s = state[h]
        own = s["lowered"]
        s["across"] = lax.ppermute(own, "dp", [(0, 1), (1, 0)])
        s["xs"] = [own, lax.ppermute(own, "sub", [(0, 1), (1, 0)])]

    def gather_rest(h, across):
        state[h]["xs"] += [across, lax.ppermute(across, "sub", [(0, 1), (1, 0)])]

    def begin(step, h):
        s, at, spread = state[h], h * half, spreads[step]
        used = [peak] if step == 0 else peaks
        send, sums, left = order(
            functools.partial(first_body, step, at, spread),
            [code, square, shape((half, 4 * piece), BF16)], [VMEM] * 3,
            [idx, *s["xs"], held, weights, *used], [SMEM] + [VMEM] * 5 + [ANY] + [VMEM] * len(used),
            [pltpu.VMEM((1, half, piece), BF16), dma((1,))], name="product_first",
        )
        s["pair"] = lax.ppermute(send, "state", PAIRS)
        waiting = "tile" in state[1 - h]
        if waiting:
            add(1 - h)
            swap(1 - h, "state", 2)
        send, sums = order(
            functools.partial(next_body, step, at, spread), [code, square], [VMEM] * 2,
            [idx, left, sums, held, weights, *used], [SMEM] + [VMEM] * 3 + [ANY] + [VMEM] * len(used),
            [pltpu.VMEM((1, half, piece), BF16), dma((1,))], name="product_next",
        )
        s["inner"] = lax.ppermute(send, "state", FROM_INNER)
        s["outer"] = lax.ppermute(send, "state", FROM_OUTER)
        s["left"], s["sums"] = left, sums

    def proceed(step, h, forward, message=None, place=None):
        s, at = state[h], h * half
        args = [idx, s["left"], s["sums"], held, weights]
        specs = [SMEM] + [VMEM] * 3 + [ANY]
        outs, out_specs, aliases = [wide, wide, tile, code], [VMEM] * 4, None
        has_out = box["out"] is not None
        if place is not None:
            args, specs = args + [message], specs + [VMEM]
            outs, out_specs = outs + [out_shape], out_specs + [ANY]
            if has_out:
                aliases = {len(args): 4}
                args, specs = args + [box["out"]], specs + [ANY]
        result = order(
            functools.partial(rest_body, step, at, place, has_out), outs, out_specs, args, specs,
            [pltpu.VMEM((half, 128), F32), pltpu.VMEM((2, half, piece), BF16), dma((3,))], aliases,
            name="product_rest",
        )
        part, s["own"], s["tile"], s["weights"] = result[:4]
        if place is not None:
            box["out"] = result[4]
        swap(h, "sub", 1)
        args = [idx, part, s["pair"], held, *peaks]
        if forward:
            args.append(state[1 - h]["across"])
        count = 2 if forward else 1
        result = order(
            functools.partial(far_body, step, spreads[step], forward), [code] * count, [VMEM] * count,
            args, [SMEM] + [VMEM] * (len(args) - 1), name="far_block",
        )
        if forward:
            gather_rest(1 - h, result[1])
        s["far"] = lax.ppermute(result[0], "state", LAST)
        add(h, [s["inner"]])
        swap(h, "dp", 1)
        add(h, [s["outer"]])
        swap(h, "state", 1)

    def finish(step, h):
        s = state[h]
        args = [idx, s["own"], s["pair"], s["outer"], s["inner"], s["far"], s["tile"], s["their"], s["weights"], held, *peaks]
        specs = [SMEM] + [VMEM] * 13
        if step:
            args, specs = args + [s["logs"]], specs + [VMEM]
        outs, out_specs, aliases, place = [code, rows, tile], [VMEM] * 3, None, None
        scratch = [pltpu.VMEM((half, piece), F32)]
        if step == STEPS - 1 and h == HALVES - 1:
            place = (step, h * half)
            aliases = {len(args): 3}
            args, specs = args + [box["out"]], specs + [ANY]
            outs, out_specs, scratch = outs + [out_shape], out_specs + [ANY], scratch + [dma]
        result = order(
            functools.partial(last_body, step, spreads[step], hidden, place), outs, out_specs, args, specs,
            scratch, aliases, name="normalise",
        )
        s["lowered"], s["message"], s["logs"] = result[:3]
        if place is not None:
            box["out"] = result[3]

    for h in range(HALVES):
        gather(h)
        gather_rest(h, state[h]["across"])
    for step in range(STEPS):
        begin(step, 0)
        if step:
            finish(step - 1, 1)
            gather(1)
            proceed(step, 0, True, state[1]["message"], (step - 1, half))
        else:
            proceed(step, 0, False)
        begin(step, 1)
        finish(step, 0)
        more = step < STEPS - 1
        if more:
            gather(0)
        proceed(step, 1, more, state[0]["message"], (step, 0))
    add(1)
    swap(1, "state", 2)
    finish(STEPS - 1, 1)
    log_scale = jnp.concatenate([s["logs"][0] for s in state])
    return box["out"].reshape(STEPS, seqs, 1, 1, piece), log_scale


def shards(transition, emission, start):
    sizes = [lax.axis_size(name) for name in ("state", "dp", "sub")]
    if sizes == [4, 2, 2] and start.shape[0] == HALVES * 128 and start.shape[3] % CHUNK == 0:
        return fast(transition, emission, start)
    return general(transition, emission, start)


def solution(mesh):
    in_specs = (
        P(None, "state", None, ("dp", "sub")),
        P(None, "groups", ("dp", "sub"), None, None),
        P("groups", ("dp", "sub"), "state", None),
    )
    out_specs = (P(None, "groups", ("dp", "sub"), "state", None), P("groups"))
    return jax.shard_map(shards, mesh=mesh, in_specs=in_specs, out_specs=out_specs, check_vma=False)
```

```python
import functools

import jax
import jax.numpy as jnp
from jax import lax
from jax.experimental import pallas as pl
from jax.experimental.pallas import tpu as pltpu
from jax.sharding import PartitionSpec as P

STEPS = 4
HALVES = 2
TOP = 60000.0
START_TOP = 10.0


def product_kernel(num_x, with_peak, idx_ref, *refs):
    x_refs, t_ref, out_ref = refs[:num_x], refs[num_x], refs[num_x + 1]
    depth = x_refs[0].shape[1]
    total = None
    for q in range(num_x):
        rows = pl.ds(pl.multiple_of(idx_ref[1 + q] * depth, depth), depth)
        term = jnp.dot(x_refs[q][...], t_ref[rows, :], preferred_element_type=jnp.float32)
        total = term if total is None else total + term
    out_ref[0] = total
    if with_peak:
        peak_ref = refs[num_x + 2]
        here = jnp.max(t_ref[...].astype(jnp.float32).reshape(-1, 8, t_ref.shape[1]), axis=0)
        first = jnp.logical_and(pl.program_id(0) == 0, pl.program_id(1) == 0)

        @pl.when(first)
        def _():
            peak_ref[...] = here

        @pl.when(jnp.logical_not(first))
        def _():
            peak_ref[...] = jnp.maximum(peak_ref[...], here)


def product(indices, xs, table, blocks, with_peak):
    seqs, depth = xs[0].shape
    rows, width = table.shape
    piece = width // blocks
    tile = min(512, piece)
    per = piece // tile

    def place(o, c, idx):
        return (0, lax.rem(idx[0] + o, blocks) * per + c)

    out_shape = [jax.ShapeDtypeStruct((blocks, seqs, piece), jnp.float32)]
    out_specs = [pl.BlockSpec((1, seqs, tile), lambda o, c, idx: (o, 0, c))]
    if with_peak:
        out_shape.append(jax.ShapeDtypeStruct((8, tile), jnp.float32))
        out_specs.append(pl.BlockSpec((8, tile), lambda o, c, idx: (0, 0)))
    return pl.pallas_call(
        functools.partial(product_kernel, len(xs), with_peak),
        grid_spec=pltpu.PrefetchScalarGridSpec(
            num_scalar_prefetch=1,
            grid=(blocks, per),
            in_specs=[pl.BlockSpec((seqs, depth), lambda o, c, idx: (0, 0)) for _ in xs]
            + [pl.BlockSpec((rows, tile), place)],
            out_specs=out_specs,
        ),
        out_shape=out_shape,
        compiler_params=pltpu.CompilerParams(vmem_limit_bytes=32 * 2**20),
        cost_estimate=pl.CostEstimate(
            flops=2 * seqs * rows * width, bytes_accessed=2 * rows * width, transcendentals=0
        ),
        name="product_peak" if with_peak else "product",
    )(indices, *xs, table)


def gather_blocks(block):
    dp, sub = lax.axis_size("dp"), lax.axis_size("sub")
    found = [block]
    for k in range(1, dp):
        found.append(lax.ppermute(block, "dp", [(i, (i + k) % dp) for i in range(dp)]))
    out = []
    for l in range(sub):
        for item in found:
            out.append(item if l == 0 else lax.ppermute(item, "sub", [(i, (i + l) % sub) for i in range(sub)]))
    return out


def block_owners():
    dp, sub = lax.axis_size("dp"), lax.axis_size("sub")
    x, c = lax.axis_index("dp"), lax.axis_index("sub")
    return [
        lax.rem(x + dp - k, dp) * sub + lax.rem(c + sub - l, sub) for l in range(sub) for k in range(dp)
    ]


def line_sum(parts, into, back, first_into, first_back_r, first_back_l):
    n = lax.axis_size("state")
    right = left = None
    for k in range(1, n):
        scale = first_into if k == 1 else into
        to_r, to_l = parts[n - k], parts[k]
        if k > 1:
            to_r = to_r + right.astype(jnp.float32) * (first_back_r if k == 2 else back)
            to_l = to_l + left.astype(jnp.float32) * (first_back_l if k == 2 else back)
        right = lax.ppermute((to_r * scale).astype(jnp.float16), "state", [(i, i + 1) for i in range(k)])
        left = lax.ppermute((to_l * scale).astype(jnp.float16), "state", [(i, i - 1) for i in range(n - k, n)])
    last_r, last_l = (first_back_r, first_back_l) if n == 2 else (back, back)
    return parts[0] + right.astype(jnp.float32) * last_r + left.astype(jnp.float32) * last_l


def general(transition, emission, start):
    seq_count = start.shape[0]
    piece = start.shape[3]
    blocks = lax.axis_size("state")
    me = lax.axis_index("state")
    table = transition.reshape(transition.shape[0] * piece, transition.shape[3])
    hidden = blocks * piece * lax.axis_size("dp") * lax.axis_size("sub")
    half = seq_count // HALVES
    indices = jnp.stack([me] + block_owners()).astype(jnp.int32)
    weights = jnp.transpose(emission[:, :, 0], (0, 2, 1, 3))
    weights = jnp.concatenate([weights, weights], axis=1)
    weights = lax.dynamic_slice_in_dim(weights, me, blocks, 1)

    messages = [start[h * half : (h + 1) * half, 0, 0] for h in range(HALVES)]
    history, normals = [], []
    into = back = None
    for step in range(STEPS):
        step_messages, step_normals = [], []
        for h in range(HALVES):
            rows = slice(h * half, (h + 1) * half)
            xs = gather_blocks(messages[h].astype(jnp.bfloat16))
            first = step == 0 and h == 0
            if first:
                parts, peak = product(indices, xs, table, blocks, True)
                own_peak = jnp.max(peak)
                peaks = lax.all_gather(jnp.full((1, 128), own_peak), "state", axis=0, tiled=True)[:, 0]
                top_peak = jnp.max(peaks)
                into = TOP / (hidden * top_peak)
                back = hidden * top_peak / TOP
                peak_r = lax.dynamic_index_in_dim(peaks, lax.rem(me + blocks - 1, blocks), 0, False)
                peak_l = lax.dynamic_index_in_dim(peaks, lax.rem(me + 1, blocks), 0, False)
                spread = hidden * START_TOP
                scales = (
                    into / START_TOP, back * START_TOP,
                    TOP / (spread * own_peak), spread * peak_r / TOP, spread * peak_l / TOP,
                )
            else:
                (parts,) = product(indices, xs, table, blocks, False)
                grow = START_TOP if step == 0 else 1.0
                scales = (into / grow, back * grow, into / grow, back * grow, back * grow)
            step_weights = weights[step, :, rows].astype(jnp.float32)
            own_sum = jnp.sum(parts * step_weights, axis=(0, 2))
            sums = lax.all_gather(own_sum[None], ("state", "dp", "sub"), axis=0, tiled=True)
            normal = jnp.sum(sums, axis=0) / hidden
            summed = line_sum([parts[o] for o in range(blocks)], *scales)
            message = summed * step_weights[0] / normal[:, None]
            messages[h] = message
            step_messages.append(message)
            step_normals.append(normal)
        history.append(jnp.concatenate(step_messages, axis=0))
        normals.append(jnp.concatenate(step_normals, axis=0))
    log_scale = functools.reduce(lambda a, b: a + b, [jnp.log(x) for x in normals])
    out = jnp.stack(history).reshape(STEPS, seq_count, 1, 1, piece)
    return out, log_scale


SLOTS = ((3, 1, 2, 0), (0, 2, 3, 1), (3, 1, 0, 2), (0, 2, 1, 3))
NEAR = [(0, 1), (1, 0), (2, 3), (3, 2)]
MIDDLE = [(1, 2), (2, 1)]
FAR = [(0, 2), (2, 0), (1, 3), (3, 1)]
CHUNK = 512
VMEM = pl.BlockSpec(memory_space=pltpu.VMEM)
SMEM = pl.BlockSpec(memory_space=pltpu.SMEM)
ANY = pl.BlockSpec(memory_space=pl.ANY)
F32, BF16 = jnp.float32, jnp.bfloat16


def shape(dims, dtype):
    return jax.ShapeDtypeStruct(dims, dtype)


class Order:
    def __init__(self):
        self.last = None

    def __call__(self, body, outs, out_specs, args, specs, scratch=(), aliases=None, name=None):
        count = len(args)
        if self.last is not None:
            args, specs = [*args, self.last], [*specs, ANY]
        extra = len(args) - count

        def run(*refs):
            body(*refs[:count], *refs[count + extra :])

        result = pl.pallas_call(
            run,
            out_shape=tuple(outs),
            in_specs=list(specs),
            out_specs=tuple(out_specs),
            scratch_shapes=list(scratch),
            input_output_aliases=aliases or {},
            compiler_params=pltpu.CompilerParams(vmem_limit_bytes=12 * 2**20),
            cost_estimate=pl.CostEstimate(flops=0, bytes_accessed=1024, transcendentals=0),
            name=name,
        )(*args)
        self.last = result[0]
        return result


def encode(x):
    x = x * x
    x = x * x
    return (x * x).astype(BF16)


def decode(y):
    y = y.astype(F32)
    return jnp.where(y > 0.0, jnp.exp2(0.125 * jnp.log2(y)), 0.0)


def load_body(table_ref, held_ref, peak_ref, sems):
    count = sems.shape[0]
    rows = table_ref.shape[0] // count
    copies = [
        pltpu.make_async_copy(table_ref.at[pl.ds(i * rows, rows)], held_ref.at[pl.ds(i * rows, rows)], sems.at[i])
        for i in range(count)
    ]
    for copy in copies:
        copy.start()
    top = jnp.zeros((16, table_ref.shape[1]), BF16)
    for i, copy in enumerate(copies):
        copy.wait()

        def step(k, best, i=i):
            at = pl.multiple_of(i * rows + k * 16, 16)
            return jnp.maximum(best, held_ref[pl.ds(at, 16), :])

        top = lax.fori_loop(0, rows // 16, step, top)
    peak_ref[...] = jnp.full(peak_ref.shape, jnp.max(top.astype(F32)), F32)


def corner(ref):
    return ref[0:1, 0:1]


def top_of(peaks):
    return jnp.maximum(
        jnp.maximum(corner(peaks[0]), corner(peaks[1])), jnp.maximum(corner(peaks[2]), corner(peaks[3]))
    )


def all_swaps(tile, axes):
    return [tile] + [lax.ppermute(tile, axes, [(i, i ^ k) for i in range(4)]) for k in range(1, 4)]


def products(idx, slot, left_ref, table_ref, weights_ref, sums_ref, put):
    piece = weights_ref.shape[1]
    for c in range(piece // CHUNK):
        here = slice(c * CHUNK, (c + 1) * CHUNK)
        cols = pl.ds(pl.multiple_of(idx[slot] * piece + c * CHUNK, CHUNK), CHUNK)
        total = jnp.dot(left_ref[...], table_ref[:, cols], preferred_element_type=F32)
        put(here, total)
        weighted = total * weights_ref[:, here].astype(F32)
        sums = sums_ref[...]
        for k in range(CHUNK // 128):
            sums = sums + weighted[:, k * 128 : (k + 1) * 128]
        sums_ref[...] = sums


def fetch_weights(idx, slots, step, at, weights_ref, held, sems):
    half = held.shape[1]
    copies = [
        pltpu.make_async_copy(weights_ref.at[step, idx[s], pl.ds(at, half)], held.at[k], sems.at[k])
        for k, s in enumerate(slots)
    ]
    for copy in copies:
        copy.start()
    return copies


def first_body(step, at, spread, waiting, idx, x0, x1, x2, x3, table_ref, weights_ref, *refs):
    if waiting:
        mine_ref, theirs_ref, *refs, tile_ref, held, sems = refs
        tile_ref[...] = mine_ref[...] + theirs_ref[...]
        refs = (*refs, held, sems)
    peaks, (near_ref, middle_ref, sums_ref, left_ref, held, sems) = refs[:-6], refs[-6:]
    copies = fetch_weights(idx, (0, 1), step, at, weights_ref, held, sems)
    half, depth = x0.shape
    for q, x in enumerate((x0, x1, x2, x3)):
        left_ref[:, pl.ds(pl.multiple_of(idx[4 + q] * depth, depth), depth)] = x[...]
    scale = (TOP / spread) / (corner(peaks[0]) if step == 0 else top_of(peaks))
    sums_ref[...] = jnp.zeros_like(sums_ref)
    for slot in range(2):
        copies[slot].wait()

        def put(here, total, slot=slot):
            code = encode(total * scale)
            near_ref[slot * half : (slot + 1) * half, here] = code
            if slot == 1:
                middle_ref[:, here] = code

        products(idx, slot, left_ref, table_ref, held.at[slot], sums_ref, put)


def rest_body(step, at, write, has_out, idx, left_ref, sums_in, table_ref, weights_ref, *refs):
    if write is not None:
        message_ref, refs = refs[0], refs[2 if has_out else 1 :]
    (part_ref, own_ref, tile_ref, own_weights_ref), refs = refs[:4], refs[4:]
    if write is not None:
        out_ref, refs = refs[0], refs[1:]
    sums_ref, held, sems = refs
    if write is not None:
        copy_out = pltpu.make_async_copy(message_ref, out_ref.at[write[0], pl.ds(write[1], message_ref.shape[0])], sems.at[2])
        copy_out.start()
    copies = fetch_weights(idx, (2, 3), step, at, weights_ref, held, sems)
    sums_ref[...] = sums_in[...]
    for k, out in enumerate((part_ref, own_ref)):
        copies[k].wait()

        def put(here, total, out=out):
            out[:, here] = total

        products(idx, 2 + k, left_ref, table_ref, held.at[k], sums_ref, put)
    own_weights_ref[...] = held[1]
    tile_ref[...] = jnp.broadcast_to(jnp.sum(sums_ref[...].T, axis=0, keepdims=True), tile_ref.shape)
    if write is not None:
        copy_out.wait()


def add_body(a_ref, b_ref, table_ref, *refs):
    refs[-1][...] = a_ref[...] + b_ref[...]


def far_body(step, spread, forward, idx, part_ref, near_ref, table_ref, *refs):
    peaks, refs = refs[:4], refs[4:]
    if forward:
        refs[2][...] = refs[0][...]
        refs = refs[1:]
    out = refs[0]
    top = top_of(peaks)
    scale = (TOP / spread) / top

    @pl.when(idx[8] == 1)
    def _():
        near = decode(near_ref[: part_ref.shape[0], :])
        if step == 0:
            near = near * (corner(peaks[1]) / top)
        out[...] = encode(part_ref[...] * scale + near)

    @pl.when(idx[8] == 0)
    def _():
        out[...] = encode(part_ref[...] * scale)


def last_body(step, spread, hidden, finish, idx, own_ref, near_ref, middle_ref, far_ref, mine_ref, theirs_ref, weights_ref, table_ref, *refs):
    peaks, logs_in, refs = refs[:4], refs[4] if step else None, refs[5 if step else 4 :]
    if finish is not None:
        refs = refs[1:]
    lowered_ref, message_ref, logs_ref = refs[:3]
    if finish is not None:
        out_ref, mixed_ref, sem = refs[3:]
    else:
        (mixed_ref,) = refs[3:]
    half = own_ref.shape[0]
    top = top_of(peaks)
    unscale = top * (spread / TOP)
    normal = (mine_ref[...] + theirs_ref[...]) / hidden
    logs = jnp.log(normal)
    logs_ref[...] = logs if logs_in is None else logs_in[...] + logs
    inverse = jnp.broadcast_to(1.0 / normal[0:1, :], (half, half)).T

    def sent_by(k):
        return corner(peaks[k]) * (spread / TOP) if step == 0 else unscale

    @pl.when(idx[8] == 1)
    def _():
        mixed_ref[...] = (
            own_ref[...]
            + (decode(near_ref[half:, :]) * sent_by(1) + decode(middle_ref[...]) * sent_by(3))
            + decode(far_ref[...]) * unscale
        )

    @pl.when(idx[8] == 0)
    def _():
        mixed_ref[...] = own_ref[...] + (decode(near_ref[:half, :]) * sent_by(1) + decode(far_ref[...]) * unscale)

    for k in range(own_ref.shape[1] // 128):
        here = slice(k * 128, (k + 1) * 128)
        message = mixed_ref[:, here] * weights_ref[:, here].astype(F32) * inverse
        lowered_ref[:, here] = message.astype(BF16)
        message_ref[:, k, :] = message
    if finish is not None:
        write = pltpu.make_async_copy(message_ref, out_ref.at[finish[0], pl.ds(finish[1], half)], sem)
        write.start()
        write.wait()


def fast(transition, emission, start):
    seqs, piece = start.shape[0], start.shape[3]
    hidden = 16 * piece
    half = seqs // HALVES
    table = transition.reshape(4 * piece, 4 * piece)
    me = lax.axis_index("state")
    d = lax.axis_index("dp") * 2 + lax.axis_index("sub")
    slots = jnp.asarray(SLOTS, jnp.int32)[me]
    inner = jnp.logical_and(me > 0, me < 3)
    idx = jnp.concatenate([slots, jnp.stack([d, d ^ 1, d ^ 2, d ^ 3, inner]).astype(jnp.int32)])
    weights = jnp.transpose(emission[:, :, 0], (0, 2, 1, 3))
    wide, code = shape((half, piece), F32), shape((half, piece), BF16)
    square, tile = shape((half, 128), F32), shape((8, 128), F32)
    rows = shape((half, piece // 128, 128), F32)
    out_shape = shape((STEPS, seqs, piece // 128, 128), F32)
    dma = pltpu.SemaphoreType.DMA
    order = Order()

    table, weights, idx = lax.optimization_barrier((table, weights, idx))
    weights = pltpu.with_memory_space_constraint(weights, pltpu.HBM)
    held, peak = order(
        load_body, [pltpu.VMEM(table.shape, table.dtype), shape((8, 128), F32)], [VMEM] * 2, [table], [ANY],
        [dma((8,))], name="load_table",
    )
    order.last = peak
    held = pltpu.with_memory_space_constraint(held, pltpu.VMEM)
    peaks = all_swaps(peak, "state")

    spreads = [hidden * 1.01 * (START_TOP if step == 0 else 1.0) for step in range(STEPS)]
    state = [{"lowered": start[h * half : (h + 1) * half, 0, 0].astype(BF16)} for h in range(HALVES)]
    box = {"out": None}

    def swap(h, axis, k):
        s = state[h]
        s["their"] = lax.ppermute(s["tile"], axis, [(i, i ^ k) for i in range(lax.axis_size(axis))])

    def add(h, after=()):
        s = state[h]
        s["tile"] = order(
            add_body, [tile], [VMEM], [s["tile"], s["their"], held, *after], [VMEM] * 3 + [ANY] * len(after),
            name="add_sums",
        )[0]

    def gather(h):
        s = state[h]
        own = s["lowered"]
        s["across"] = lax.ppermute(own, "dp", [(0, 1), (1, 0)])
        s["xs"] = [own, lax.ppermute(own, "sub", [(0, 1), (1, 0)])]

    def gather_rest(h, across):
        state[h]["xs"] += [across, lax.ppermute(across, "sub", [(0, 1), (1, 0)])]

    def begin(step, h):
        s, at, spread = state[h], h * half, spreads[step]
        used = [peak] if step == 0 else peaks
        other = state[1 - h]
        waiting = "tile" in other
        extra = [other["tile"], other["their"]] if waiting else []
        near, middle, sums, left, *added = order(
            functools.partial(first_body, step, at, spread, waiting),
            [shape((2 * half, piece), BF16), code, square, shape((half, 4 * piece), BF16)] + [tile] * waiting,
            [VMEM] * (4 + waiting),
            [idx, *s["xs"], held, weights, *extra, *used],
            [SMEM] + [VMEM] * 5 + [ANY] + [VMEM] * (len(extra) + len(used)),
            [pltpu.VMEM((2, half, piece), BF16), dma((2,))], name="product_first",
        )
        if waiting:
            other["tile"] = added[0]
            swap(1 - h, "state", 2)
        s["near"] = lax.ppermute(near, "state", NEAR)
        s["middle"] = lax.ppermute(middle, "state", MIDDLE)
        s["left"], s["sums"] = left, sums

    def proceed(step, h, forward, message=None, place=None):
        s, at = state[h], h * half
        args = [idx, s["left"], s["sums"], held, weights]
        specs = [SMEM] + [VMEM] * 3 + [ANY]
        outs, out_specs, aliases = [wide, wide, tile, code], [VMEM] * 4, None
        has_out = box["out"] is not None
        if place is not None:
            args, specs = args + [message], specs + [VMEM]
            outs, out_specs = outs + [out_shape], out_specs + [ANY]
            if has_out:
                aliases = {len(args): 4}
                args, specs = args + [box["out"]], specs + [ANY]
        result = order(
            functools.partial(rest_body, step, at, place, has_out), outs, out_specs, args, specs,
            [pltpu.VMEM((half, 128), F32), pltpu.VMEM((2, half, piece), BF16), dma((3,))], aliases,
            name="product_rest",
        )
        part, s["own"], s["tile"], s["weights"] = result[:4]
        if place is not None:
            box["out"] = result[4]
        swap(h, "sub", 1)
        args = [idx, part, s["near"], held, *peaks]
        if forward:
            args.append(state[1 - h]["across"])
        count = 2 if forward else 1
        result = order(
            functools.partial(far_body, step, spreads[step], forward), [code] * count, [VMEM] * count,
            args, [SMEM] + [VMEM] * (len(args) - 1), name="far_block",
        )
        if forward:
            gather_rest(1 - h, result[1])
        s["far"] = lax.ppermute(result[0], "state", FAR)
        add(h, [s["middle"]])
        swap(h, "dp", 1)
        add(h)
        swap(h, "state", 1)

    def finish(step, h):
        s = state[h]
        args = [idx, s["own"], s["near"], s["middle"], s["far"], s["tile"], s["their"], s["weights"], held, *peaks]
        specs = [SMEM] + [VMEM] * 12
        if step:
            args, specs = args + [s["logs"]], specs + [VMEM]
        outs, out_specs, aliases, place = [code, rows, tile], [VMEM] * 3, None, None
        scratch = [pltpu.VMEM((half, piece), F32)]
        if step == STEPS - 1 and h == HALVES - 1:
            place = (step, h * half)
            aliases = {len(args): 3}
            args, specs = args + [box["out"]], specs + [ANY]
            outs, out_specs, scratch = outs + [out_shape], out_specs + [ANY], scratch + [dma]
        result = order(
            functools.partial(last_body, step, spreads[step], hidden, place), outs, out_specs, args, specs,
            scratch, aliases, name="normalise",
        )
        s["lowered"], s["message"], s["logs"] = result[:3]
        if place is not None:
            box["out"] = result[3]

    for s in state:
        own = s["lowered"]
        s["xs"] = [own] + [lax.ppermute(own, ("dp", "sub"), [(i, i ^ k) for i in range(4)]) for k in (1, 2, 3)]
    for step in range(STEPS):
        begin(step, 0)
        if step:
            finish(step - 1, 1)
            gather(1)
            proceed(step, 0, True, state[1]["message"], (step - 1, half))
        else:
            proceed(step, 0, False)
        begin(step, 1)
        finish(step, 0)
        more = step < STEPS - 1
        if more:
            gather(0)
        proceed(step, 1, more, state[0]["message"], (step, 0))
    add(1)
    swap(1, "state", 2)
    finish(STEPS - 1, 1)
    log_scale = jnp.concatenate([s["logs"][0] for s in state])
    return box["out"].reshape(STEPS, seqs, 1, 1, piece), log_scale


def shards(transition, emission, start):
    sizes = [lax.axis_size(name) for name in ("state", "dp", "sub")]
    if sizes == [4, 2, 2] and start.shape[0] == HALVES * 128 and start.shape[3] % CHUNK == 0:
        return fast(transition, emission, start)
    return general(transition, emission, start)


def solution(mesh):
    in_specs = (
        P(None, "state", None, ("dp", "sub")),
        P(None, "groups", ("dp", "sub"), None, None),
        P("groups", ("dp", "sub"), "state", None),
    )
    out_specs = (P(None, "groups", ("dp", "sub"), "state", None), P("groups"))
    return jax.shard_map(shards, mesh=mesh, in_specs=in_specs, out_specs=out_specs, check_vma=False)
```

```python
import functools

import jax
import jax.numpy as jnp
from jax import lax
from jax.experimental import pallas as pl
from jax.experimental.pallas import tpu as pltpu
from jax.sharding import PartitionSpec as P

STEPS = 4
HALVES = 2
TOP = 60000.0
START_TOP = 10.0


def product_kernel(num_x, with_peak, idx_ref, *refs):
    x_refs, t_ref, out_ref = refs[:num_x], refs[num_x], refs[num_x + 1]
    depth = x_refs[0].shape[1]
    total = None
    for q in range(num_x):
        rows = pl.ds(pl.multiple_of(idx_ref[1 + q] * depth, depth), depth)
        term = jnp.dot(x_refs[q][...], t_ref[rows, :], preferred_element_type=jnp.float32)
        total = term if total is None else total + term
    out_ref[0] = total
    if with_peak:
        peak_ref = refs[num_x + 2]
        here = jnp.max(t_ref[...].astype(jnp.float32).reshape(-1, 8, t_ref.shape[1]), axis=0)
        first = jnp.logical_and(pl.program_id(0) == 0, pl.program_id(1) == 0)

        @pl.when(first)
        def _():
            peak_ref[...] = here

        @pl.when(jnp.logical_not(first))
        def _():
            peak_ref[...] = jnp.maximum(peak_ref[...], here)


def product(indices, xs, table, blocks, with_peak):
    seqs, depth = xs[0].shape
    rows, width = table.shape
    piece = width // blocks
    tile = min(512, piece)
    per = piece // tile

    def place(o, c, idx):
        return (0, lax.rem(idx[0] + o, blocks) * per + c)

    out_shape = [jax.ShapeDtypeStruct((blocks, seqs, piece), jnp.float32)]
    out_specs = [pl.BlockSpec((1, seqs, tile), lambda o, c, idx: (o, 0, c))]
    if with_peak:
        out_shape.append(jax.ShapeDtypeStruct((8, tile), jnp.float32))
        out_specs.append(pl.BlockSpec((8, tile), lambda o, c, idx: (0, 0)))
    return pl.pallas_call(
        functools.partial(product_kernel, len(xs), with_peak),
        grid_spec=pltpu.PrefetchScalarGridSpec(
            num_scalar_prefetch=1,
            grid=(blocks, per),
            in_specs=[pl.BlockSpec((seqs, depth), lambda o, c, idx: (0, 0)) for _ in xs]
            + [pl.BlockSpec((rows, tile), place)],
            out_specs=out_specs,
        ),
        out_shape=out_shape,
        compiler_params=pltpu.CompilerParams(vmem_limit_bytes=32 * 2**20),
        cost_estimate=pl.CostEstimate(
            flops=2 * seqs * rows * width, bytes_accessed=2 * rows * width, transcendentals=0
        ),
        name="product_peak" if with_peak else "product",
    )(indices, *xs, table)


def gather_blocks(block):
    dp, sub = lax.axis_size("dp"), lax.axis_size("sub")
    found = [block]
    for k in range(1, dp):
        found.append(lax.ppermute(block, "dp", [(i, (i + k) % dp) for i in range(dp)]))
    out = []
    for l in range(sub):
        for item in found:
            out.append(item if l == 0 else lax.ppermute(item, "sub", [(i, (i + l) % sub) for i in range(sub)]))
    return out


def block_owners():
    dp, sub = lax.axis_size("dp"), lax.axis_size("sub")
    x, c = lax.axis_index("dp"), lax.axis_index("sub")
    return [
        lax.rem(x + dp - k, dp) * sub + lax.rem(c + sub - l, sub) for l in range(sub) for k in range(dp)
    ]


def line_sum(parts, into, back, first_into, first_back_r, first_back_l):
    n = lax.axis_size("state")
    right = left = None
    for k in range(1, n):
        scale = first_into if k == 1 else into
        to_r, to_l = parts[n - k], parts[k]
        if k > 1:
            to_r = to_r + right.astype(jnp.float32) * (first_back_r if k == 2 else back)
            to_l = to_l + left.astype(jnp.float32) * (first_back_l if k == 2 else back)
        right = lax.ppermute((to_r * scale).astype(jnp.float16), "state", [(i, i + 1) for i in range(k)])
        left = lax.ppermute((to_l * scale).astype(jnp.float16), "state", [(i, i - 1) for i in range(n - k, n)])
    last_r, last_l = (first_back_r, first_back_l) if n == 2 else (back, back)
    return parts[0] + right.astype(jnp.float32) * last_r + left.astype(jnp.float32) * last_l


def general(transition, emission, start):
    seq_count = start.shape[0]
    piece = start.shape[3]
    blocks = lax.axis_size("state")
    me = lax.axis_index("state")
    table = transition.reshape(transition.shape[0] * piece, transition.shape[3])
    hidden = blocks * piece * lax.axis_size("dp") * lax.axis_size("sub")
    half = seq_count // HALVES
    indices = jnp.stack([me] + block_owners()).astype(jnp.int32)
    weights = jnp.transpose(emission[:, :, 0], (0, 2, 1, 3))
    weights = jnp.concatenate([weights, weights], axis=1)
    weights = lax.dynamic_slice_in_dim(weights, me, blocks, 1)

    messages = [start[h * half : (h + 1) * half, 0, 0] for h in range(HALVES)]
    history, normals = [], []
    into = back = None
    for step in range(STEPS):
        step_messages, step_normals = [], []
        for h in range(HALVES):
            rows = slice(h * half, (h + 1) * half)
            xs = gather_blocks(messages[h].astype(jnp.bfloat16))
            first = step == 0 and h == 0
            if first:
                parts, peak = product(indices, xs, table, blocks, True)
                own_peak = jnp.max(peak)
                peaks = lax.all_gather(jnp.full((1, 128), own_peak), "state", axis=0, tiled=True)[:, 0]
                top_peak = jnp.max(peaks)
                into = TOP / (hidden * top_peak)
                back = hidden * top_peak / TOP
                peak_r = lax.dynamic_index_in_dim(peaks, lax.rem(me + blocks - 1, blocks), 0, False)
                peak_l = lax.dynamic_index_in_dim(peaks, lax.rem(me + 1, blocks), 0, False)
                spread = hidden * START_TOP
                scales = (
                    into / START_TOP, back * START_TOP,
                    TOP / (spread * own_peak), spread * peak_r / TOP, spread * peak_l / TOP,
                )
            else:
                (parts,) = product(indices, xs, table, blocks, False)
                grow = START_TOP if step == 0 else 1.0
                scales = (into / grow, back * grow, into / grow, back * grow, back * grow)
            step_weights = weights[step, :, rows].astype(jnp.float32)
            own_sum = jnp.sum(parts * step_weights, axis=(0, 2))
            sums = lax.all_gather(own_sum[None], ("state", "dp", "sub"), axis=0, tiled=True)
            normal = jnp.sum(sums, axis=0) / hidden
            summed = line_sum([parts[o] for o in range(blocks)], *scales)
            message = summed * step_weights[0] / normal[:, None]
            messages[h] = message
            step_messages.append(message)
            step_normals.append(normal)
        history.append(jnp.concatenate(step_messages, axis=0))
        normals.append(jnp.concatenate(step_normals, axis=0))
    log_scale = functools.reduce(lambda a, b: a + b, [jnp.log(x) for x in normals])
    out = jnp.stack(history).reshape(STEPS, seq_count, 1, 1, piece)
    return out, log_scale


SLOTS = ((3, 2, 1, 0), (0, 2, 3, 1), (3, 1, 0, 2), (0, 1, 2, 3))
PAIRS = [(0, 1), (1, 0), (2, 3), (3, 2)]
FROM_OUTER = [(0, 2), (3, 1)]
FROM_INNER = [(1, 2), (2, 1)]
LAST = [(1, 3), (2, 0), (0, 1), (3, 2)]
CHUNK = 512
VMEM = pl.BlockSpec(memory_space=pltpu.VMEM)
SMEM = pl.BlockSpec(memory_space=pltpu.SMEM)
ANY = pl.BlockSpec(memory_space=pl.ANY)
F32, BF16 = jnp.float32, jnp.bfloat16


def shape(dims, dtype):
    return jax.ShapeDtypeStruct(dims, dtype)


class Order:
    def __init__(self):
        self.last = None

    def __call__(self, body, outs, out_specs, args, specs, scratch=(), aliases=None, name=None):
        count = len(args)
        if self.last is not None:
            args, specs = [*args, self.last], [*specs, ANY]
        extra = len(args) - count

        def run(*refs):
            body(*refs[:count], *refs[count + extra :])

        result = pl.pallas_call(
            run,
            out_shape=tuple(outs),
            in_specs=list(specs),
            out_specs=tuple(out_specs),
            scratch_shapes=list(scratch),
            input_output_aliases=aliases or {},
            compiler_params=pltpu.CompilerParams(vmem_limit_bytes=12 * 2**20),
            cost_estimate=pl.CostEstimate(flops=0, bytes_accessed=1024, transcendentals=0),
            name=name,
        )(*args)
        self.last = result[0]
        return result


def encode(x):
    x = x * x
    x = x * x
    return (x * x).astype(BF16)


def decode(y):
    y = y.astype(F32)
    return jnp.where(y > 0.0, jnp.exp2(0.125 * jnp.log2(y)), 0.0)


def load_body(table_ref, held_ref, peak_ref, sems):
    count = sems.shape[0]
    rows = table_ref.shape[0] // count
    copies = [
        pltpu.make_async_copy(table_ref.at[pl.ds(i * rows, rows)], held_ref.at[pl.ds(i * rows, rows)], sems.at[i])
        for i in range(count)
    ]
    for copy in copies:
        copy.start()
    top = jnp.zeros((16, table_ref.shape[1]), BF16)
    for i, copy in enumerate(copies):
        copy.wait()

        def step(k, best, i=i):
            at = pl.multiple_of(i * rows + k * 16, 16)
            return jnp.maximum(best, held_ref[pl.ds(at, 16), :])

        top = lax.fori_loop(0, rows // 16, step, top)
    peak_ref[...] = jnp.full(peak_ref.shape, jnp.max(top.astype(F32)), F32)


def corner(ref):
    return ref[0:1, 0:1]


def top_of(peaks):
    return jnp.maximum(
        jnp.maximum(corner(peaks[0]), corner(peaks[1])), jnp.maximum(corner(peaks[2]), corner(peaks[3]))
    )


def all_swaps(tile, axes):
    return [tile] + [lax.ppermute(tile, axes, [(i, i ^ k) for i in range(4)]) for k in range(1, 4)]


def products(idx, slot, left_ref, table_ref, weights_ref, sums_ref, put):
    piece = weights_ref.shape[1]
    for c in range(piece // CHUNK):
        here = slice(c * CHUNK, (c + 1) * CHUNK)
        cols = pl.ds(pl.multiple_of(idx[slot] * piece + c * CHUNK, CHUNK), CHUNK)
        total = jnp.dot(left_ref[...], table_ref[:, cols], preferred_element_type=F32)
        put(here, total)
        weighted = total * weights_ref[:, here].astype(F32)
        sums = sums_ref[...]
        for k in range(CHUNK // 128):
            sums = sums + weighted[:, k * 128 : (k + 1) * 128]
        sums_ref[...] = sums


def fetch_weights(idx, slots, step, at, weights_ref, held, sems):
    half = held.shape[1]
    copies = [
        pltpu.make_async_copy(weights_ref.at[step, idx[s], pl.ds(at, half)], held.at[k], sems.at[k])
        for k, s in enumerate(slots)
    ]
    for copy in copies:
        copy.start()
    return copies


def first_body(step, at, spread, idx, x0, x1, x2, x3, table_ref, weights_ref, *refs):
    peaks, (out0_ref, out1_ref, sums_ref, left_ref, held, sems) = refs[:-6], refs[-6:]
    copies = fetch_weights(idx, (0, 1), step, at, weights_ref, held, sems)
    depth = x0.shape[1]
    for q, x in enumerate((x0, x1, x2, x3)):
        left_ref[:, pl.ds(pl.multiple_of(idx[4 + q] * depth, depth), depth)] = x[...]
    scale = (TOP / spread) / (corner(peaks[0]) if step == 0 else top_of(peaks))
    sums_ref[...] = jnp.zeros_like(sums_ref)
    for slot, out_ref in enumerate((out0_ref, out1_ref)):
        copies[slot].wait()

        def put(here, total, out_ref=out_ref):
            out_ref[:, here] = encode(total * scale)

        products(idx, slot, left_ref, table_ref, held.at[slot], sums_ref, put)


def rest_body(step, at, write, has_out, idx, left_ref, sums_in, table_ref, weights_ref, *refs):
    if write is not None:
        message_ref, refs = refs[0], refs[2 if has_out else 1 :]
    (part_ref, own_ref, tile_ref, own_weights_ref), refs = refs[:4], refs[4:]
    if write is not None:
        out_ref, refs = refs[0], refs[1:]
    sums_ref, held, sems = refs
    if write is not None:
        copy_out = pltpu.make_async_copy(message_ref, out_ref.at[write[0], pl.ds(write[1], message_ref.shape[0])], sems.at[2])
        copy_out.start()
    copies = fetch_weights(idx, (2, 3), step, at, weights_ref, held, sems)
    sums_ref[...] = sums_in[...]
    for k, out in enumerate((part_ref, own_ref)):
        copies[k].wait()

        def put(here, total, out=out):
            out[:, here] = total

        products(idx, 2 + k, left_ref, table_ref, held.at[k], sums_ref, put)
    own_weights_ref[...] = held[1]
    tile_ref[...] = jnp.broadcast_to(jnp.sum(sums_ref[...].T, axis=0, keepdims=True), tile_ref.shape)
    if write is not None:
        copy_out.wait()


def add_body(a_ref, b_ref, table_ref, *refs):
    refs[-1][...] = a_ref[...] + b_ref[...]


def far_body(step, spread, forward, idx, part_ref, pair_ref, table_ref, *refs):
    peaks, refs = refs[:4], refs[4:]
    if forward:
        refs[2][...] = refs[0][...]
        refs = refs[1:]
    out = refs[0]
    top = top_of(peaks)
    scale = (TOP / spread) / top

    @pl.when(idx[8] == 1)
    def _():
        pair = decode(pair_ref[...])
        if step == 0:
            pair = pair * (corner(peaks[1]) / top)
        out[...] = encode(part_ref[...] * scale + pair)

    @pl.when(idx[8] == 0)
    def _():
        out[...] = encode(part_ref[...] * scale)


def last_body(step, spread, hidden, finish, idx, own_ref, pair_ref, outer_ref, inner_ref, far_ref, mine_ref, theirs_ref, weights_ref, table_ref, *refs):
    peaks, logs_in, refs = refs[:4], refs[4] if step else None, refs[5 if step else 4 :]
    if finish is not None:
        refs = refs[1:]
    lowered_ref, message_ref, logs_ref = refs[:3]
    if finish is not None:
        out_ref, mixed_ref, sem = refs[3:]
    else:
        (mixed_ref,) = refs[3:]
    half = own_ref.shape[0]
    top = top_of(peaks)
    unscale = top * (spread / TOP)
    normal = (mine_ref[...] + theirs_ref[...]) / hidden
    logs = jnp.log(normal)
    logs_ref[...] = logs if logs_in is None else logs_in[...] + logs
    inverse = jnp.broadcast_to(1.0 / normal[0:1, :], (half, half)).T

    def sent_by(k):
        return corner(peaks[k]) * (spread / TOP) if step == 0 else unscale

    @pl.when(idx[8] == 1)
    def _():
        mixed_ref[...] = (
            own_ref[...]
            + (decode(outer_ref[...]) * sent_by(2) + decode(inner_ref[...]) * sent_by(3))
            + decode(far_ref[...]) * unscale
        )

    @pl.when(idx[8] == 0)
    def _():
        mixed_ref[...] = own_ref[...] + (decode(pair_ref[...]) * sent_by(1) + decode(far_ref[...]) * unscale)

    for k in range(own_ref.shape[1] // 128):
        here = slice(k * 128, (k + 1) * 128)
        message = mixed_ref[:, here] * weights_ref[:, here].astype(F32) * inverse
        lowered_ref[:, here] = message.astype(BF16)
        message_ref[:, k, :] = message
    if finish is not None:
        write = pltpu.make_async_copy(message_ref, out_ref.at[finish[0], pl.ds(finish[1], half)], sem)
        write.start()
        write.wait()


def fast(transition, emission, start):
    seqs, piece = start.shape[0], start.shape[3]
    hidden = 16 * piece
    half = seqs // HALVES
    table = transition.reshape(4 * piece, 4 * piece)
    me = lax.axis_index("state")
    d = lax.axis_index("dp") * 2 + lax.axis_index("sub")
    slots = jnp.asarray(SLOTS, jnp.int32)[me]
    inner = jnp.logical_and(me > 0, me < 3)
    idx = jnp.concatenate([slots, jnp.stack([d, d ^ 1, d ^ 2, d ^ 3, inner]).astype(jnp.int32)])
    weights = jnp.transpose(emission[:, :, 0], (0, 2, 1, 3))
    wide, code = shape((half, piece), F32), shape((half, piece), BF16)
    square, tile = shape((half, 128), F32), shape((8, 128), F32)
    rows = shape((half, piece // 128, 128), F32)
    out_shape = shape((STEPS, seqs, piece // 128, 128), F32)
    dma = pltpu.SemaphoreType.DMA
    order = Order()

    table, weights, idx = lax.optimization_barrier((table, weights, idx))
    weights = pltpu.with_memory_space_constraint(weights, pltpu.HBM)
    held, peak = order(
        load_body, [pltpu.VMEM(table.shape, table.dtype), shape((8, 128), F32)], [VMEM] * 2, [table], [ANY],
        [dma((8,))], name="load_table",
    )
    order.last = peak
    held = pltpu.with_memory_space_constraint(held, pltpu.VMEM)
    peaks = all_swaps(peak, "state")

    spreads = [hidden * 1.01 * (START_TOP if step == 0 else 1.0) for step in range(STEPS)]
    state = [{"lowered": start[h * half : (h + 1) * half, 0, 0].astype(BF16)} for h in range(HALVES)]
    box = {"out": None}

    def swap(h, axis, k):
        s = state[h]
        s["their"] = lax.ppermute(s["tile"], axis, [(i, i ^ k) for i in range(lax.axis_size(axis))])

    def add(h, after=()):
        s = state[h]
        s["tile"] = order(
            add_body, [tile], [VMEM], [s["tile"], s["their"], held, *after], [VMEM] * 3 + [ANY] * len(after),
            name="add_sums",
        )[0]

    def gather(h):
        s = state[h]
        own = s["lowered"]
        s["across"] = lax.ppermute(own, "dp", [(0, 1), (1, 0)])
        s["xs"] = [own, lax.ppermute(own, "sub", [(0, 1), (1, 0)])]

    def gather_rest(h, across):
        state[h]["xs"] += [across, lax.ppermute(across, "sub", [(0, 1), (1, 0)])]

    def begin(step, h):
        s, at, spread = state[h], h * half, spreads[step]
        used = [peak] if step == 0 else peaks
        send0, send1, sums, left = order(
            functools.partial(first_body, step, at, spread),
            [code, code, square, shape((half, 4 * piece), BF16)], [VMEM] * 4,
            [idx, *s["xs"], held, weights, *used], [SMEM] + [VMEM] * 5 + [ANY] + [VMEM] * len(used),
            [pltpu.VMEM((2, half, piece), BF16), dma((2,))], name="product_first",
        )
        if "tile" in state[1 - h]:
            add(1 - h)
            swap(1 - h, "sub", 1)
        s["pair"] = lax.ppermute(send0, "state", PAIRS)
        s["outer"] = lax.ppermute(send1, "state", FROM_OUTER)
        s["inner"] = lax.ppermute(send1, "state", FROM_INNER)
        s["left"], s["sums"] = left, sums

    def proceed(step, h, forward, message=None, place=None):
        s, at = state[h], h * half
        args = [idx, s["left"], s["sums"], held, weights]
        specs = [SMEM] + [VMEM] * 3 + [ANY]
        outs, out_specs, aliases = [wide, wide, tile, code], [VMEM] * 4, None
        has_out = box["out"] is not None
        if place is not None:
            args, specs = args + [message], specs + [VMEM]
            outs, out_specs = outs + [out_shape], out_specs + [ANY]
            if has_out:
                aliases = {len(args): 4}
                args, specs = args + [box["out"]], specs + [ANY]
        result = order(
            functools.partial(rest_body, step, at, place, has_out), outs, out_specs, args, specs,
            [pltpu.VMEM((half, 128), F32), pltpu.VMEM((2, half, piece), BF16), dma((3,))], aliases,
            name="product_rest",
        )
        part, s["own"], s["tile"], s["weights"] = result[:4]
        if place is not None:
            box["out"] = result[4]
        swap(h, "state", 1)
        args = [idx, part, s["pair"], held, *peaks]
        if forward:
            args.append(state[1 - h]["across"])
        count = 2 if forward else 1
        result = order(
            functools.partial(far_body, step, spreads[step], forward), [code] * count, [VMEM] * count,
            args, [SMEM] + [VMEM] * (len(args) - 1), name="far_block",
        )
        if forward:
            gather_rest(1 - h, result[1])
        s["far"] = lax.ppermute(result[0], "state", LAST)
        add(h, [s["outer"]])
        swap(h, "dp", 1)
        add(h, [s["inner"]])
        swap(h, "state", 2)

    def finish(step, h):
        s = state[h]
        args = [idx, s["own"], s["pair"], s["outer"], s["inner"], s["far"], s["tile"], s["their"], s["weights"], held, *peaks]
        specs = [SMEM] + [VMEM] * 13
        if step:
            args, specs = args + [s["logs"]], specs + [VMEM]
        outs, out_specs, aliases, place = [code, rows, tile], [VMEM] * 3, None, None
        scratch = [pltpu.VMEM((half, piece), F32)]
        if step == STEPS - 1 and h == HALVES - 1:
            place = (step, h * half)
            aliases = {len(args): 3}
            args, specs = args + [box["out"]], specs + [ANY]
            outs, out_specs, scratch = outs + [out_shape], out_specs + [ANY], scratch + [dma]
        result = order(
            functools.partial(last_body, step, spreads[step], hidden, place), outs, out_specs, args, specs,
            scratch, aliases, name="normalise",
        )
        s["lowered"], s["message"], s["logs"] = result[:3]
        if place is not None:
            box["out"] = result[3]

    for s in state:
        own = s["lowered"]
        s["xs"] = [own] + [lax.ppermute(own, ("dp", "sub"), [(i, i ^ k) for i in range(4)]) for k in (1, 2, 3)]
    for step in range(STEPS):
        begin(step, 0)
        if step:
            finish(step - 1, 1)
            gather(1)
            proceed(step, 0, True, state[1]["message"], (step - 1, half))
        else:
            proceed(step, 0, False)
        begin(step, 1)
        finish(step, 0)
        more = step < STEPS - 1
        if more:
            gather(0)
        proceed(step, 1, more, state[0]["message"], (step, 0))
    add(1)
    swap(1, "sub", 1)
    finish(STEPS - 1, 1)
    log_scale = jnp.concatenate([s["logs"][0] for s in state])
    return box["out"].reshape(STEPS, seqs, 1, 1, piece), log_scale


def shards(transition, emission, start):
    sizes = [lax.axis_size(name) for name in ("state", "dp", "sub")]
    if sizes == [4, 2, 2] and start.shape[0] == HALVES * 128 and start.shape[3] % CHUNK == 0:
        return fast(transition, emission, start)
    return general(transition, emission, start)


def solution(mesh):
    in_specs = (
        P(None, "state", None, ("dp", "sub")),
        P(None, "groups", ("dp", "sub"), None, None),
        P("groups", ("dp", "sub"), "state", None),
    )
    out_specs = (P(None, "groups", ("dp", "sub"), "state", None), P("groups"))
    return jax.shard_map(shards, mesh=mesh, in_specs=in_specs, out_specs=out_specs, check_vma=False)
```

```python
import functools

import jax
import jax.numpy as jnp
from jax import lax
from jax.experimental import pallas as pl
from jax.experimental.pallas import tpu as pltpu
from jax.sharding import PartitionSpec as P

STEPS = 4
HALVES = 2
TOP = 60000.0
START_TOP = 10.0


def product_kernel(num_x, with_peak, idx_ref, *refs):
    x_refs, t_ref, out_ref = refs[:num_x], refs[num_x], refs[num_x + 1]
    depth = x_refs[0].shape[1]
    total = None
    for q in range(num_x):
        rows = pl.ds(pl.multiple_of(idx_ref[1 + q] * depth, depth), depth)
        term = jnp.dot(x_refs[q][...], t_ref[rows, :], preferred_element_type=jnp.float32)
        total = term if total is None else total + term
    out_ref[0] = total
    if with_peak:
        peak_ref = refs[num_x + 2]
        here = jnp.max(t_ref[...].astype(jnp.float32).reshape(-1, 8, t_ref.shape[1]), axis=0)
        first = jnp.logical_and(pl.program_id(0) == 0, pl.program_id(1) == 0)

        @pl.when(first)
        def _():
            peak_ref[...] = here

        @pl.when(jnp.logical_not(first))
        def _():
            peak_ref[...] = jnp.maximum(peak_ref[...], here)


def product(indices, xs, table, blocks, with_peak):
    seqs, depth = xs[0].shape
    rows, width = table.shape
    piece = width // blocks
    tile = min(512, piece)
    per = piece // tile

    def place(o, c, idx):
        return (0, lax.rem(idx[0] + o, blocks) * per + c)

    out_shape = [jax.ShapeDtypeStruct((blocks, seqs, piece), jnp.float32)]
    out_specs = [pl.BlockSpec((1, seqs, tile), lambda o, c, idx: (o, 0, c))]
    if with_peak:
        out_shape.append(jax.ShapeDtypeStruct((8, tile), jnp.float32))
        out_specs.append(pl.BlockSpec((8, tile), lambda o, c, idx: (0, 0)))
    return pl.pallas_call(
        functools.partial(product_kernel, len(xs), with_peak),
        grid_spec=pltpu.PrefetchScalarGridSpec(
            num_scalar_prefetch=1,
            grid=(blocks, per),
            in_specs=[pl.BlockSpec((seqs, depth), lambda o, c, idx: (0, 0)) for _ in xs]
            + [pl.BlockSpec((rows, tile), place)],
            out_specs=out_specs,
        ),
        out_shape=out_shape,
        compiler_params=pltpu.CompilerParams(vmem_limit_bytes=32 * 2**20),
        cost_estimate=pl.CostEstimate(
            flops=2 * seqs * rows * width, bytes_accessed=2 * rows * width, transcendentals=0
        ),
        name="product_peak" if with_peak else "product",
    )(indices, *xs, table)


def gather_blocks(block):
    dp, sub = lax.axis_size("dp"), lax.axis_size("sub")
    found = [block]
    for k in range(1, dp):
        found.append(lax.ppermute(block, "dp", [(i, (i + k) % dp) for i in range(dp)]))
    out = []
    for l in range(sub):
        for item in found:
            out.append(item if l == 0 else lax.ppermute(item, "sub", [(i, (i + l) % sub) for i in range(sub)]))
    return out


def block_owners():
    dp, sub = lax.axis_size("dp"), lax.axis_size("sub")
    x, c = lax.axis_index("dp"), lax.axis_index("sub")
    return [
        lax.rem(x + dp - k, dp) * sub + lax.rem(c + sub - l, sub) for l in range(sub) for k in range(dp)
    ]


def line_sum(parts, into, back, first_into, first_back_r, first_back_l):
    n = lax.axis_size("state")
    right = left = None
    for k in range(1, n):
        scale = first_into if k == 1 else into
        to_r, to_l = parts[n - k], parts[k]
        if k > 1:
            to_r = to_r + right.astype(jnp.float32) * (first_back_r if k == 2 else back)
            to_l = to_l + left.astype(jnp.float32) * (first_back_l if k == 2 else back)
        right = lax.ppermute((to_r * scale).astype(jnp.float16), "state", [(i, i + 1) for i in range(k)])
        left = lax.ppermute((to_l * scale).astype(jnp.float16), "state", [(i, i - 1) for i in range(n - k, n)])
    last_r, last_l = (first_back_r, first_back_l) if n == 2 else (back, back)
    return parts[0] + right.astype(jnp.float32) * last_r + left.astype(jnp.float32) * last_l


def general(transition, emission, start):
    seq_count = start.shape[0]
    piece = start.shape[3]
    blocks = lax.axis_size("state")
    me = lax.axis_index("state")
    table = transition.reshape(transition.shape[0] * piece, transition.shape[3])
    hidden = blocks * piece * lax.axis_size("dp") * lax.axis_size("sub")
    half = seq_count // HALVES
    indices = jnp.stack([me] + block_owners()).astype(jnp.int32)
    weights = jnp.transpose(emission[:, :, 0], (0, 2, 1, 3))
    weights = jnp.concatenate([weights, weights], axis=1)
    weights = lax.dynamic_slice_in_dim(weights, me, blocks, 1)

    messages = [start[h * half : (h + 1) * half, 0, 0] for h in range(HALVES)]
    history, normals = [], []
    into = back = None
    for step in range(STEPS):
        step_messages, step_normals = [], []
        for h in range(HALVES):
            rows = slice(h * half, (h + 1) * half)
            xs = gather_blocks(messages[h].astype(jnp.bfloat16))
            first = step == 0 and h == 0
            if first:
                parts, peak = product(indices, xs, table, blocks, True)
                own_peak = jnp.max(peak)
                peaks = lax.all_gather(jnp.full((1, 128), own_peak), "state", axis=0, tiled=True)[:, 0]
                top_peak = jnp.max(peaks)
                into = TOP / (hidden * top_peak)
                back = hidden * top_peak / TOP
                peak_r = lax.dynamic_index_in_dim(peaks, lax.rem(me + blocks - 1, blocks), 0, False)
                peak_l = lax.dynamic_index_in_dim(peaks, lax.rem(me + 1, blocks), 0, False)
                spread = hidden * START_TOP
                scales = (
                    into / START_TOP, back * START_TOP,
                    TOP / (spread * own_peak), spread * peak_r / TOP, spread * peak_l / TOP,
                )
            else:
                (parts,) = product(indices, xs, table, blocks, False)
                grow = START_TOP if step == 0 else 1.0
                scales = (into / grow, back * grow, into / grow, back * grow, back * grow)
            step_weights = weights[step, :, rows].astype(jnp.float32)
            own_sum = jnp.sum(parts * step_weights, axis=(0, 2))
            sums = lax.all_gather(own_sum[None], ("state", "dp", "sub"), axis=0, tiled=True)
            normal = jnp.sum(sums, axis=0) / hidden
            summed = line_sum([parts[o] for o in range(blocks)], *scales)
            message = summed * step_weights[0] / normal[:, None]
            messages[h] = message
            step_messages.append(message)
            step_normals.append(normal)
        history.append(jnp.concatenate(step_messages, axis=0))
        normals.append(jnp.concatenate(step_normals, axis=0))
    log_scale = functools.reduce(lambda a, b: a + b, [jnp.log(x) for x in normals])
    out = jnp.stack(history).reshape(STEPS, seq_count, 1, 1, piece)
    return out, log_scale


SLOTS = ((3, 2, 1, 0), (0, 2, 3, 1), (3, 1, 0, 2), (0, 1, 2, 3))
PAIRS = [(0, 1), (1, 0), (2, 3), (3, 2)]
FROM_OUTER = [(0, 2), (3, 1)]
FROM_INNER = [(1, 2), (2, 1)]
LAST = [(1, 3), (2, 0), (0, 1), (3, 2)]
CHUNK = 512
VMEM = pl.BlockSpec(memory_space=pltpu.VMEM)
SMEM = pl.BlockSpec(memory_space=pltpu.SMEM)
ANY = pl.BlockSpec(memory_space=pl.ANY)
F32, BF16 = jnp.float32, jnp.bfloat16


def shape(dims, dtype):
    return jax.ShapeDtypeStruct(dims, dtype)


class Order:
    def __init__(self):
        self.last = None

    def __call__(self, body, outs, out_specs, args, specs, scratch=(), aliases=None, name=None):
        count = len(args)
        if self.last is not None:
            args, specs = [*args, self.last], [*specs, ANY]
        extra = len(args) - count

        def run(*refs):
            body(*refs[:count], *refs[count + extra :])

        result = pl.pallas_call(
            run,
            out_shape=tuple(outs),
            in_specs=list(specs),
            out_specs=tuple(out_specs),
            scratch_shapes=list(scratch),
            input_output_aliases=aliases or {},
            compiler_params=pltpu.CompilerParams(vmem_limit_bytes=12 * 2**20),
            cost_estimate=pl.CostEstimate(flops=0, bytes_accessed=1024, transcendentals=0),
            name=name,
        )(*args)
        self.last = result[0]
        return result


def encode(x):
    x = x * x
    x = x * x
    return (x * x).astype(BF16)


def decode(y):
    y = y.astype(F32)
    return jnp.where(y > 0.0, jnp.exp2(0.125 * jnp.log2(y)), 0.0)


def load_body(table_ref, held_ref, peak_ref, sems):
    count = sems.shape[0]
    rows = table_ref.shape[0] // count
    copies = [
        pltpu.make_async_copy(table_ref.at[pl.ds(i * rows, rows)], held_ref.at[pl.ds(i * rows, rows)], sems.at[i])
        for i in range(count)
    ]
    for copy in copies:
        copy.start()
    top = jnp.zeros((16, table_ref.shape[1]), BF16)
    for i, copy in enumerate(copies):
        copy.wait()

        def step(k, best, i=i):
            at = pl.multiple_of(i * rows + k * 16, 16)
            return jnp.maximum(best, held_ref[pl.ds(at, 16), :])

        top = lax.fori_loop(0, rows // 16, step, top)
    peak_ref[...] = jnp.full(peak_ref.shape, jnp.max(top.astype(F32)), F32)


def corner(ref):
    return ref[0:1, 0:1]


def top_of(peaks):
    return jnp.maximum(
        jnp.maximum(corner(peaks[0]), corner(peaks[1])), jnp.maximum(corner(peaks[2]), corner(peaks[3]))
    )


def all_swaps(tile, axes):
    return [tile] + [lax.ppermute(tile, axes, [(i, i ^ k) for i in range(4)]) for k in range(1, 4)]


def products(idx, slot, left_ref, table_ref, weights_ref, sums_ref, put):
    piece = weights_ref.shape[1]
    for c in range(piece // CHUNK):
        here = slice(c * CHUNK, (c + 1) * CHUNK)
        cols = pl.ds(pl.multiple_of(idx[slot] * piece + c * CHUNK, CHUNK), CHUNK)
        total = jnp.dot(left_ref[...], table_ref[:, cols], preferred_element_type=F32)
        put(here, total)
        weighted = total * weights_ref[:, here].astype(F32)
        sums = sums_ref[...]
        for k in range(CHUNK // 128):
            sums = sums + weighted[:, k * 128 : (k + 1) * 128]
        sums_ref[...] = sums


def fetch_weights(idx, slots, step, at, weights_ref, held, sems):
    half = held.shape[1]
    copies = [
        pltpu.make_async_copy(weights_ref.at[step, idx[s], pl.ds(at, half)], held.at[k], sems.at[k])
        for k, s in enumerate(slots)
    ]
    for copy in copies:
        copy.start()
    return copies


def first_body(step, at, spread, extra, idx, x0, x1, x2, x3, table_ref, weights_ref, *refs):
    refs = refs[extra:]
    peaks, (out0_ref, out1_ref, sums_ref, left_ref, held, sems) = refs[:-6], refs[-6:]
    copies = fetch_weights(idx, (0, 1), step, at, weights_ref, held, sems)
    depth = x0.shape[1]
    for q, x in enumerate((x0, x1, x2, x3)):
        left_ref[:, pl.ds(pl.multiple_of(idx[4 + q] * depth, depth), depth)] = x[...]
    scale = (TOP / spread) / (corner(peaks[0]) if step == 0 else top_of(peaks))
    sums_ref[...] = jnp.zeros_like(sums_ref)
    for slot, out_ref in enumerate((out0_ref, out1_ref)):
        copies[slot].wait()

        def put(here, total, out_ref=out_ref):
            out_ref[:, here] = encode(total * scale)

        products(idx, slot, left_ref, table_ref, held.at[slot], sums_ref, put)


def rest_body(step, at, write, has_out, extra, idx, left_ref, sums_in, table_ref, weights_ref, *refs):
    refs = refs[extra:]
    if write is not None:
        message_ref, refs = refs[0], refs[2 if has_out else 1 :]
    (part_ref, own_ref, tile_ref, own_weights_ref), refs = refs[:4], refs[4:]
    if write is not None:
        out_ref, refs = refs[0], refs[1:]
    sums_ref, held, sems = refs
    if write is not None:
        copy_out = pltpu.make_async_copy(message_ref, out_ref.at[write[0], pl.ds(write[1], message_ref.shape[0])], sems.at[2])
        copy_out.start()
    copies = fetch_weights(idx, (2, 3), step, at, weights_ref, held, sems)
    sums_ref[...] = sums_in[...]
    for k, out in enumerate((part_ref, own_ref)):
        copies[k].wait()

        def put(here, total, out=out):
            out[:, here] = total

        products(idx, 2 + k, left_ref, table_ref, held.at[k], sums_ref, put)
    own_weights_ref[...] = held[1]
    tile_ref[...] = jnp.broadcast_to(jnp.sum(sums_ref[...].T, axis=0, keepdims=True), tile_ref.shape)
    if write is not None:
        copy_out.wait()


def add_body(a_ref, b_ref, table_ref, *refs):
    refs[-1][...] = a_ref[...] + b_ref[...]


def far_body(step, spread, forward, idx, part_ref, pair_ref, table_ref, *refs):
    peaks, refs = refs[:4], refs[4:]
    if forward:
        refs[2][...] = refs[0][...]
        refs = refs[1:]
    out = refs[0]
    top = top_of(peaks)
    scale = (TOP / spread) / top

    @pl.when(idx[8] == 1)
    def _():
        pair = decode(pair_ref[...])
        if step == 0:
            pair = pair * (corner(peaks[1]) / top)
        out[...] = encode(part_ref[...] * scale + pair)

    @pl.when(idx[8] == 0)
    def _():
        out[...] = encode(part_ref[...] * scale)


def last_body(step, spread, hidden, finish, idx, own_ref, pair_ref, outer_ref, inner_ref, far_ref, sums0, sums1, sums2, sums3, weights_ref, table_ref, *refs):
    peaks, logs_in, refs = refs[:4], refs[4] if step else None, refs[5 if step else 4 :]
    if finish is not None:
        refs = refs[1:]
    lowered_ref, message_ref, logs_ref = refs[:3]
    if finish is not None:
        out_ref, mixed_ref, sem = refs[3:]
    else:
        (mixed_ref,) = refs[3:]
    half = own_ref.shape[0]
    top = top_of(peaks)
    unscale = top * (spread / TOP)
    normal = ((sums0[...] + sums1[...]) + (sums2[...] + sums3[...])) / hidden
    logs = jnp.log(normal)
    logs_ref[...] = logs if logs_in is None else logs_in[...] + logs
    inverse = jnp.broadcast_to(1.0 / normal[0:1, :], (half, half)).T

    def sent_by(k):
        return corner(peaks[k]) * (spread / TOP) if step == 0 else unscale

    @pl.when(idx[8] == 1)
    def _():
        mixed_ref[...] = (
            own_ref[...]
            + (decode(outer_ref[...]) * sent_by(2) + decode(inner_ref[...]) * sent_by(3))
            + decode(far_ref[...]) * unscale
        )

    @pl.when(idx[8] == 0)
    def _():
        mixed_ref[...] = own_ref[...] + (decode(pair_ref[...]) * sent_by(1) + decode(far_ref[...]) * unscale)

    for k in range(own_ref.shape[1] // 128):
        here = slice(k * 128, (k + 1) * 128)
        message = mixed_ref[:, here] * weights_ref[:, here].astype(F32) * inverse
        lowered_ref[:, here] = message.astype(BF16)
        message_ref[:, k, :] = message
    if finish is not None:
        write = pltpu.make_async_copy(message_ref, out_ref.at[finish[0], pl.ds(finish[1], half)], sem)
        write.start()
        write.wait()


def fast(transition, emission, start):
    seqs, piece = start.shape[0], start.shape[3]
    hidden = 16 * piece
    half = seqs // HALVES
    table = transition.reshape(4 * piece, 4 * piece)
    me = lax.axis_index("state")
    d = lax.axis_index("dp") * 2 + lax.axis_index("sub")
    slots = jnp.asarray(SLOTS, jnp.int32)[me]
    inner = jnp.logical_and(me > 0, me < 3)
    idx = jnp.concatenate([slots, jnp.stack([d, d ^ 1, d ^ 2, d ^ 3, inner]).astype(jnp.int32)])
    weights = jnp.transpose(emission[:, :, 0], (0, 2, 1, 3))
    wide, code = shape((half, piece), F32), shape((half, piece), BF16)
    square, tile = shape((half, 128), F32), shape((8, 128), F32)
    rows = shape((half, piece // 128, 128), F32)
    out_shape = shape((STEPS, seqs, piece // 128, 128), F32)
    dma = pltpu.SemaphoreType.DMA
    order = Order()

    table, weights, idx = lax.optimization_barrier((table, weights, idx))
    weights = pltpu.with_memory_space_constraint(weights, pltpu.HBM)
    held, peak = order(
        load_body, [pltpu.VMEM(table.shape, table.dtype), shape((8, 128), F32)], [VMEM] * 2, [table], [ANY],
        [dma((8,))], name="load_table",
    )
    order.last = peak
    held = pltpu.with_memory_space_constraint(held, pltpu.VMEM)
    peaks = all_swaps(peak, "state")

    spreads = [hidden * 1.01 * (START_TOP if step == 0 else 1.0) for step in range(STEPS)]
    state = [{"lowered": start[h * half : (h + 1) * half, 0, 0].astype(BF16)} for h in range(HALVES)]
    box = {"out": None}

    def swap(h, axis, k):
        s = state[h]
        s["their"] = lax.ppermute(s["tile"], axis, [(i, i ^ k) for i in range(lax.axis_size(axis))])

    def gather_sums(h):
        add(h)
        state[h]["tiles"] = all_swaps(state[h]["tile"], ("dp", "sub"))

    def add(h, after=()):
        s = state[h]
        s["tile"] = order(
            add_body, [tile], [VMEM], [s["tile"], s["their"], held, *after], [VMEM] * 3 + [ANY] * len(after),
            name="add_sums",
        )[0]

    def gather(h):
        s = state[h]
        own = s["lowered"]
        s["across"] = lax.ppermute(own, "dp", [(0, 1), (1, 0)])
        s["xs"] = [own, lax.ppermute(own, "sub", [(0, 1), (1, 0)])]

    def gather_rest(h, across):
        state[h]["xs"] += [across, lax.ppermute(across, "sub", [(0, 1), (1, 0)])]

    def begin(step, h):
        s, at, spread = state[h], h * half, spreads[step]
        used = [peak] if step == 0 else peaks
        after = [state[1 - h]["inner"]] if "inner" in state[1 - h] else []
        send0, send1, sums, left = order(
            functools.partial(first_body, step, at, spread, len(after)),
            [code, code, square, shape((half, 4 * piece), BF16)], [VMEM] * 4,
            [idx, *s["xs"], held, weights, *after, *used],
            [SMEM] + [VMEM] * 5 + [ANY] * (1 + len(after)) + [VMEM] * len(used),
            [pltpu.VMEM((2, half, piece), BF16), dma((2,))], name="product_first",
        )
        if "tile" in state[1 - h] and not (step == STEPS - 1 and h == 1):
            gather_sums(1 - h)
        s["pair"] = lax.ppermute(send0, "state", PAIRS)
        s["outer"] = lax.ppermute(send1, "state", FROM_OUTER)
        s["inner"] = lax.ppermute(send1, "state", FROM_INNER)
        s["left"], s["sums"] = left, sums

    def proceed(step, h, forward, message=None, place=None):
        s, at = state[h], h * half
        args = [idx, s["left"], s["sums"], held, weights]
        after = state[1]["xs"][2:] if step == h == 0 else []
        args, specs = args + after, [SMEM] + [VMEM] * 3 + [ANY] * (1 + len(after))
        outs, out_specs, aliases = [wide, wide, tile, code], [VMEM] * 4, None
        has_out = box["out"] is not None
        if place is not None:
            args, specs = args + [message], specs + [VMEM]
            outs, out_specs = outs + [out_shape], out_specs + [ANY]
            if has_out:
                aliases = {len(args): 4}
                args, specs = args + [box["out"]], specs + [ANY]
        result = order(
            functools.partial(rest_body, step, at, place, has_out, len(after)), outs, out_specs, args, specs,
            [pltpu.VMEM((half, 128), F32), pltpu.VMEM((2, half, piece), BF16), dma((3,))], aliases,
            name="product_rest",
        )
        part, s["own"], s["tile"], s["weights"] = result[:4]
        if place is not None:
            box["out"] = result[4]
        swap(h, "state", 1)
        args = [idx, part, s["pair"], held, *peaks]
        if forward:
            args.append(state[1 - h]["across"])
        count = 2 if forward else 1
        result = order(
            functools.partial(far_body, step, spreads[step], forward), [code] * count, [VMEM] * count,
            args, [SMEM] + [VMEM] * (len(args) - 1), name="far_block",
        )
        if forward:
            gather_rest(1 - h, result[1])
        s["far"] = lax.ppermute(result[0], "state", LAST)
        add(h, [s["outer"]])
        swap(h, "state", 2)

    def finish(step, h):
        s = state[h]
        args = [idx, s["own"], s["pair"], s["outer"], s["inner"], s["far"], *s["tiles"], s["weights"], held, *peaks]
        specs = [SMEM] + [VMEM] * 15
        if step:
            args, specs = args + [s["logs"]], specs + [VMEM]
        outs, out_specs, aliases, place = [code, rows, tile], [VMEM] * 3, None, None
        scratch = [pltpu.VMEM((half, piece), F32)]
        if step == STEPS - 1:
            place = (step, h * half)
            aliases = {len(args): 3}
            args, specs = args + [box["out"]], specs + [ANY]
            outs, out_specs, scratch = outs + [out_shape], out_specs + [ANY], scratch + [dma]
        result = order(
            functools.partial(last_body, step, spreads[step], hidden, place), outs, out_specs, args, specs,
            scratch, aliases, name="normalise",
        )
        s["lowered"], s["message"], s["logs"] = result[:3]
        if place is not None:
            box["out"] = result[3]

    for s in state:
        own = s["lowered"]
        s["xs"] = [own] + [lax.ppermute(own, ("dp", "sub"), [(i, i ^ k) for i in range(4)]) for k in (1, 2, 3)]
    for step in range(STEPS):
        begin(step, 0)
        if step:
            finish(step - 1, 1)
            gather(1)
            proceed(step, 0, True, state[1]["message"], (step - 1, half))
        else:
            proceed(step, 0, False)
        begin(step, 1)
        if step < STEPS - 1:
            finish(step, 0)
            gather(0)
            proceed(step, 1, True, state[0]["message"], (step, 0))
        else:
            proceed(step, 1, False)
            gather_sums(0)
            finish(step, 0)
    gather_sums(1)
    finish(STEPS - 1, 1)
    log_scale = jnp.concatenate([s["logs"][0] for s in state])
    return box["out"].reshape(STEPS, seqs, 1, 1, piece), log_scale


def shards(transition, emission, start):
    sizes = [lax.axis_size(name) for name in ("state", "dp", "sub")]
    if sizes == [4, 2, 2] and start.shape[0] == HALVES * 128 and start.shape[3] % CHUNK == 0:
        return fast(transition, emission, start)
    return general(transition, emission, start)


def solution(mesh):
    in_specs = (
        P(None, "state", None, ("dp", "sub")),
        P(None, "groups", ("dp", "sub"), None, None),
        P("groups", ("dp", "sub"), "state", None),
    )
    out_specs = (P(None, "groups", ("dp", "sub"), "state", None), P("groups"))
    return jax.shard_map(shards, mesh=mesh, in_specs=in_specs, out_specs=out_specs, check_vma=False)
```

```python
import functools

import jax
import jax.numpy as jnp
from jax import lax
from jax.experimental import pallas as pl
from jax.experimental.pallas import tpu as pltpu
from jax.sharding import PartitionSpec as P

STEPS = 4
HALVES = 2
TOP = 60000.0
START_TOP = 10.0


def product_kernel(num_x, with_peak, idx_ref, *refs):
    x_refs, t_ref, out_ref = refs[:num_x], refs[num_x], refs[num_x + 1]
    depth = x_refs[0].shape[1]
    total = None
    for q in range(num_x):
        rows = pl.ds(pl.multiple_of(idx_ref[1 + q] * depth, depth), depth)
        term = jnp.dot(x_refs[q][...], t_ref[rows, :], preferred_element_type=jnp.float32)
        total = term if total is None else total + term
    out_ref[0] = total
    if with_peak:
        peak_ref = refs[num_x + 2]
        here = jnp.max(t_ref[...].astype(jnp.float32).reshape(-1, 8, t_ref.shape[1]), axis=0)
        first = jnp.logical_and(pl.program_id(0) == 0, pl.program_id(1) == 0)

        @pl.when(first)
        def _():
            peak_ref[...] = here

        @pl.when(jnp.logical_not(first))
        def _():
            peak_ref[...] = jnp.maximum(peak_ref[...], here)


def product(indices, xs, table, blocks, with_peak):
    seqs, depth = xs[0].shape
    rows, width = table.shape
    piece = width // blocks
    tile = min(512, piece)
    per = piece // tile

    def place(o, c, idx):
        return (0, lax.rem(idx[0] + o, blocks) * per + c)

    out_shape = [jax.ShapeDtypeStruct((blocks, seqs, piece), jnp.float32)]
    out_specs = [pl.BlockSpec((1, seqs, tile), lambda o, c, idx: (o, 0, c))]
    if with_peak:
        out_shape.append(jax.ShapeDtypeStruct((8, tile), jnp.float32))
        out_specs.append(pl.BlockSpec((8, tile), lambda o, c, idx: (0, 0)))
    return pl.pallas_call(
        functools.partial(product_kernel, len(xs), with_peak),
        grid_spec=pltpu.PrefetchScalarGridSpec(
            num_scalar_prefetch=1,
            grid=(blocks, per),
            in_specs=[pl.BlockSpec((seqs, depth), lambda o, c, idx: (0, 0)) for _ in xs]
            + [pl.BlockSpec((rows, tile), place)],
            out_specs=out_specs,
        ),
        out_shape=out_shape,
        compiler_params=pltpu.CompilerParams(vmem_limit_bytes=32 * 2**20),
        cost_estimate=pl.CostEstimate(
            flops=2 * seqs * rows * width, bytes_accessed=2 * rows * width, transcendentals=0
        ),
        name="product_peak" if with_peak else "product",
    )(indices, *xs, table)


def gather_blocks(block):
    dp, sub = lax.axis_size("dp"), lax.axis_size("sub")
    found = [block]
    for k in range(1, dp):
        found.append(lax.ppermute(block, "dp", [(i, (i + k) % dp) for i in range(dp)]))
    out = []
    for l in range(sub):
        for item in found:
            out.append(item if l == 0 else lax.ppermute(item, "sub", [(i, (i + l) % sub) for i in range(sub)]))
    return out


def block_owners():
    dp, sub = lax.axis_size("dp"), lax.axis_size("sub")
    x, c = lax.axis_index("dp"), lax.axis_index("sub")
    return [
        lax.rem(x + dp - k, dp) * sub + lax.rem(c + sub - l, sub) for l in range(sub) for k in range(dp)
    ]


def line_sum(parts, into, back, first_into, first_back_r, first_back_l):
    n = lax.axis_size("state")
    right = left = None
    for k in range(1, n):
        scale = first_into if k == 1 else into
        to_r, to_l = parts[n - k], parts[k]
        if k > 1:
            to_r = to_r + right.astype(jnp.float32) * (first_back_r if k == 2 else back)
            to_l = to_l + left.astype(jnp.float32) * (first_back_l if k == 2 else back)
        right = lax.ppermute((to_r * scale).astype(jnp.float16), "state", [(i, i + 1) for i in range(k)])
        left = lax.ppermute((to_l * scale).astype(jnp.float16), "state", [(i, i - 1) for i in range(n - k, n)])
    last_r, last_l = (first_back_r, first_back_l) if n == 2 else (back, back)
    return parts[0] + right.astype(jnp.float32) * last_r + left.astype(jnp.float32) * last_l


def general(transition, emission, start):
    seq_count = start.shape[0]
    piece = start.shape[3]
    blocks = lax.axis_size("state")
    me = lax.axis_index("state")
    table = transition.reshape(transition.shape[0] * piece, transition.shape[3])
    hidden = blocks * piece * lax.axis_size("dp") * lax.axis_size("sub")
    half = seq_count // HALVES
    indices = jnp.stack([me] + block_owners()).astype(jnp.int32)
    weights = jnp.transpose(emission[:, :, 0], (0, 2, 1, 3))
    weights = jnp.concatenate([weights, weights], axis=1)
    weights = lax.dynamic_slice_in_dim(weights, me, blocks, 1)

    messages = [start[h * half : (h + 1) * half, 0, 0] for h in range(HALVES)]
    history, normals = [], []
    into = back = None
    for step in range(STEPS):
        step_messages, step_normals = [], []
        for h in range(HALVES):
            rows = slice(h * half, (h + 1) * half)
            xs = gather_blocks(messages[h].astype(jnp.bfloat16))
            first = step == 0 and h == 0
            if first:
                parts, peak = product(indices, xs, table, blocks, True)
                own_peak = jnp.max(peak)
                peaks = lax.all_gather(jnp.full((1, 128), own_peak), "state", axis=0, tiled=True)[:, 0]
                top_peak = jnp.max(peaks)
                into = TOP / (hidden * top_peak)
                back = hidden * top_peak / TOP
                peak_r = lax.dynamic_index_in_dim(peaks, lax.rem(me + blocks - 1, blocks), 0, False)
                peak_l = lax.dynamic_index_in_dim(peaks, lax.rem(me + 1, blocks), 0, False)
                spread = hidden * START_TOP
                scales = (
                    into / START_TOP, back * START_TOP,
                    TOP / (spread * own_peak), spread * peak_r / TOP, spread * peak_l / TOP,
                )
            else:
                (parts,) = product(indices, xs, table, blocks, False)
                grow = START_TOP if step == 0 else 1.0
                scales = (into / grow, back * grow, into / grow, back * grow, back * grow)
            step_weights = weights[step, :, rows].astype(jnp.float32)
            own_sum = jnp.sum(parts * step_weights, axis=(0, 2))
            sums = lax.all_gather(own_sum[None], ("state", "dp", "sub"), axis=0, tiled=True)
            normal = jnp.sum(sums, axis=0) / hidden
            summed = line_sum([parts[o] for o in range(blocks)], *scales)
            message = summed * step_weights[0] / normal[:, None]
            messages[h] = message
            step_messages.append(message)
            step_normals.append(normal)
        history.append(jnp.concatenate(step_messages, axis=0))
        normals.append(jnp.concatenate(step_normals, axis=0))
    log_scale = functools.reduce(lambda a, b: a + b, [jnp.log(x) for x in normals])
    out = jnp.stack(history).reshape(STEPS, seq_count, 1, 1, piece)
    return out, log_scale


SLOTS = ((3, 2, 1, 0), (0, 2, 3, 1), (3, 1, 0, 2), (0, 1, 2, 3))
PAIRS = [(0, 1), (1, 0), (2, 3), (3, 2)]
FROM_OUTER = [(0, 2), (3, 1)]
FROM_INNER = [(1, 2), (2, 1)]
LAST = [(1, 3), (2, 0), (0, 1), (3, 2)]
CHUNK = 512
VMEM = pl.BlockSpec(memory_space=pltpu.VMEM)
SMEM = pl.BlockSpec(memory_space=pltpu.SMEM)
ANY = pl.BlockSpec(memory_space=pl.ANY)
F32, BF16 = jnp.float32, jnp.bfloat16


def shape(dims, dtype):
    return jax.ShapeDtypeStruct(dims, dtype)


class Order:
    def __init__(self):
        self.last = None

    def __call__(self, body, outs, out_specs, args, specs, scratch=(), aliases=None, name=None):
        count = len(args)
        if self.last is not None:
            args, specs = [*args, self.last], [*specs, ANY]
        extra = len(args) - count

        def run(*refs):
            body(*refs[:count], *refs[count + extra :])

        result = pl.pallas_call(
            run,
            out_shape=tuple(outs),
            in_specs=list(specs),
            out_specs=tuple(out_specs),
            scratch_shapes=list(scratch),
            input_output_aliases=aliases or {},
            compiler_params=pltpu.CompilerParams(vmem_limit_bytes=12 * 2**20),
            cost_estimate=pl.CostEstimate(flops=0, bytes_accessed=1024, transcendentals=0),
            name=name,
        )(*args)
        self.last = result[0]
        return result


def encode(x):
    x = x * x
    x = x * x
    return (x * x).astype(BF16)


def decode(y):
    y = y.astype(F32)
    return jnp.where(y > 0.0, jnp.exp2(0.125 * jnp.log2(y)), 0.0)


def load_body(table_ref, held_ref, peak_ref, sems):
    count = sems.shape[0]
    rows = table_ref.shape[0] // count
    copies = [
        pltpu.make_async_copy(table_ref.at[pl.ds(i * rows, rows)], held_ref.at[pl.ds(i * rows, rows)], sems.at[i])
        for i in range(count)
    ]
    for copy in copies:
        copy.start()
    top = jnp.zeros((16, table_ref.shape[1]), BF16)
    for i, copy in enumerate(copies):
        copy.wait()

        def step(k, best, i=i):
            at = pl.multiple_of(i * rows + k * 16, 16)
            return jnp.maximum(best, held_ref[pl.ds(at, 16), :])

        top = lax.fori_loop(0, rows // 16, step, top)
    peak_ref[...] = jnp.full(peak_ref.shape, jnp.max(top.astype(F32)), F32)


def corner(ref):
    return ref[0:1, 0:1]


def top_of(peaks):
    return jnp.maximum(
        jnp.maximum(corner(peaks[0]), corner(peaks[1])), jnp.maximum(corner(peaks[2]), corner(peaks[3]))
    )


def all_swaps(tile, axes):
    return [tile] + [lax.ppermute(tile, axes, [(i, i ^ k) for i in range(4)]) for k in range(1, 4)]


def products(idx, slot, left_ref, table_ref, weights_ref, sums_ref, arrive, put):
    piece = weights_ref.shape[1]
    for c in range(piece // CHUNK):
        here = slice(c * CHUNK, (c + 1) * CHUNK)
        cols = pl.ds(pl.multiple_of(idx[slot] * piece + c * CHUNK, CHUNK), CHUNK)
        total = jnp.dot(left_ref[...], table_ref[:, cols], preferred_element_type=F32)
        put(here, total)
        if c == 0:
            arrive.wait()
        weighted = total * weights_ref[:, here].astype(F32)
        sums = sums_ref[...]
        for k in range(CHUNK // 128):
            sums = sums + weighted[:, k * 128 : (k + 1) * 128]
        sums_ref[...] = sums


def fetch_weights(idx, slots, step, at, weights_ref, held, sems):
    half = held.shape[1]
    copies = [
        pltpu.make_async_copy(weights_ref.at[step, idx[s], pl.ds(at, half)], held.at[k], sems.at[k])
        for k, s in enumerate(slots)
    ]
    for copy in copies:
        copy.start()
    return copies


def first_body(step, at, spread, extra, idx, x0, x1, x2, x3, table_ref, weights_ref, *refs):
    refs = refs[extra:]
    peaks, (out0_ref, out1_ref, sums_ref, left_ref, held, sems) = refs[:-6], refs[-6:]
    copies = fetch_weights(idx, (0, 1), step, at, weights_ref, held, sems)
    depth = x0.shape[1]
    for q, x in enumerate((x0, x1, x2, x3)):
        left_ref[:, pl.ds(pl.multiple_of(idx[4 + q] * depth, depth), depth)] = x[...]
    scale = (TOP / spread) / (corner(peaks[0]) if step == 0 else top_of(peaks))
    sums_ref[...] = jnp.zeros_like(sums_ref)
    for slot, out_ref in enumerate((out0_ref, out1_ref)):
        def put(here, total, out_ref=out_ref):
            out_ref[:, here] = encode(total * scale)

        products(idx, slot, left_ref, table_ref, held.at[slot], sums_ref, copies[slot], put)


def rest_body(step, at, write, has_out, extra, idx, left_ref, sums_in, table_ref, weights_ref, *refs):
    refs = refs[extra:]
    if write is not None:
        message_ref, refs = refs[0], refs[2 if has_out else 1 :]
    (part_ref, own_ref, tile_ref, own_weights_ref), refs = refs[:4], refs[4:]
    if write is not None:
        out_ref, refs = refs[0], refs[1:]
    sums_ref, held, sems = refs
    if write is not None:
        copy_out = pltpu.make_async_copy(message_ref, out_ref.at[write[0], pl.ds(write[1], message_ref.shape[0])], sems.at[2])
        copy_out.start()
    copies = fetch_weights(idx, (2, 3), step, at, weights_ref, held, sems)
    sums_ref[...] = sums_in[...]
    for k, out in enumerate((part_ref, own_ref)):
        def put(here, total, out=out):
            out[:, here] = total

        products(idx, 2 + k, left_ref, table_ref, held.at[k], sums_ref, copies[k], put)
    own_weights_ref[...] = held[1]
    tile_ref[...] = jnp.broadcast_to(jnp.sum(sums_ref[...].T, axis=0, keepdims=True), tile_ref.shape)
    if write is not None:
        copy_out.wait()


def add_body(a_ref, b_ref, table_ref, *refs):
    refs[-1][...] = a_ref[...] + b_ref[...]


def far_body(step, spread, forward, idx, part_ref, pair_ref, mine_ref, theirs_ref, table_ref, *refs):
    peaks, refs = refs[:4], refs[5:]
    if forward:
        refs[3][...] = refs[0][...]
        refs = refs[1:]
    out, tile_ref = refs[:2]
    tile_ref[...] = mine_ref[...] + theirs_ref[...]
    top = top_of(peaks)
    scale = (TOP / spread) / top

    @pl.when(idx[8] == 1)
    def _():
        pair = decode(pair_ref[...])
        if step == 0:
            pair = pair * (corner(peaks[1]) / top)
        out[...] = encode(part_ref[...] * scale + pair)

    @pl.when(idx[8] == 0)
    def _():
        out[...] = encode(part_ref[...] * scale)


def last_body(step, spread, hidden, finish, idx, own_ref, pair_ref, outer_ref, inner_ref, far_ref, sums0, sums1, sums2, sums3, weights_ref, table_ref, *refs):
    peaks, logs_in, refs = refs[:4], refs[4] if step else None, refs[5 if step else 4 :]
    if finish is not None:
        refs = refs[1:]
    lowered_ref, message_ref, logs_ref = refs[:3]
    if finish is not None:
        out_ref, mixed_ref, sem = refs[3:]
    else:
        (mixed_ref,) = refs[3:]
    half = own_ref.shape[0]
    top = top_of(peaks)
    unscale = top * (spread / TOP)
    normal = ((sums0[...] + sums1[...]) + (sums2[...] + sums3[...])) / hidden
    logs = jnp.log(normal)
    logs_ref[...] = logs if logs_in is None else logs_in[...] + logs
    inverse = jnp.broadcast_to(1.0 / normal[0:1, :], (half, half)).T

    def sent_by(k):
        return corner(peaks[k]) * (spread / TOP) if step == 0 else unscale

    @pl.when(idx[8] == 1)
    def _():
        mixed_ref[...] = (
            own_ref[...]
            + (decode(outer_ref[...]) * sent_by(2) + decode(inner_ref[...]) * sent_by(3))
            + decode(far_ref[...]) * unscale
        )

    @pl.when(idx[8] == 0)
    def _():
        mixed_ref[...] = own_ref[...] + (decode(pair_ref[...]) * sent_by(1) + decode(far_ref[...]) * unscale)

    for k in range(own_ref.shape[1] // 128):
        here = slice(k * 128, (k + 1) * 128)
        message = mixed_ref[:, here] * weights_ref[:, here].astype(F32) * inverse
        lowered_ref[:, here] = message.astype(BF16)
        message_ref[:, k, :] = message
    if finish is not None:
        write = pltpu.make_async_copy(message_ref, out_ref.at[finish[0], pl.ds(finish[1], half)], sem)
        write.start()
        write.wait()


def fast(transition, emission, start):
    seqs, piece = start.shape[0], start.shape[3]
    hidden = 16 * piece
    half = seqs // HALVES
    table = transition.reshape(4 * piece, 4 * piece)
    me = lax.axis_index("state")
    d = lax.axis_index("dp") * 2 + lax.axis_index("sub")
    slots = jnp.asarray(SLOTS, jnp.int32)[me]
    inner = jnp.logical_and(me > 0, me < 3)
    idx = jnp.concatenate([slots, jnp.stack([d, d ^ 1, d ^ 2, d ^ 3, inner]).astype(jnp.int32)])
    weights = jnp.transpose(emission[:, :, 0], (0, 2, 1, 3))
    wide, code = shape((half, piece), F32), shape((half, piece), BF16)
    square, tile = shape((half, 128), F32), shape((8, 128), F32)
    rows = shape((half, piece // 128, 128), F32)
    out_shape = shape((STEPS, seqs, piece // 128, 128), F32)
    dma = pltpu.SemaphoreType.DMA
    order = Order()

    table, weights, idx = lax.optimization_barrier((table, weights, idx))
    weights = pltpu.with_memory_space_constraint(weights, pltpu.HBM)
    held, peak = order(
        load_body, [pltpu.VMEM(table.shape, table.dtype), shape((8, 128), F32)], [VMEM] * 2, [table], [ANY],
        [dma((8,))], name="load_table",
    )
    order.last = peak
    held = pltpu.with_memory_space_constraint(held, pltpu.VMEM)
    peaks = all_swaps(peak, "state")

    spreads = [hidden * 1.01 * (START_TOP if step == 0 else 1.0) for step in range(STEPS)]
    state = [{"lowered": start[h * half : (h + 1) * half, 0, 0].astype(BF16)} for h in range(HALVES)]
    box = {"out": None}

    def swap(h, axis, k):
        s = state[h]
        s["their"] = lax.ppermute(s["tile"], axis, [(i, i ^ k) for i in range(lax.axis_size(axis))])

    def gather_sums(h):
        add(h)
        state[h]["tiles"] = all_swaps(state[h]["tile"], ("dp", "sub"))

    def add(h, after=()):
        s = state[h]
        s["tile"] = order(
            add_body, [tile], [VMEM], [s["tile"], s["their"], held, *after], [VMEM] * 3 + [ANY] * len(after),
            name="add_sums",
        )[0]

    def gather(h):
        s = state[h]
        own = s["lowered"]
        s["across"] = lax.ppermute(own, "dp", [(0, 1), (1, 0)])
        s["xs"] = [own, lax.ppermute(own, "sub", [(0, 1), (1, 0)])]

    def gather_rest(h, across):
        state[h]["xs"] += [across, lax.ppermute(across, "sub", [(0, 1), (1, 0)])]

    def begin(step, h):
        s, at, spread = state[h], h * half, spreads[step]
        used = [peak] if step == 0 else peaks
        after = [state[1 - h]["inner"]] if "inner" in state[1 - h] else []
        send0, send1, sums, left = order(
            functools.partial(first_body, step, at, spread, len(after)),
            [code, code, square, shape((half, 4 * piece), BF16)], [VMEM] * 4,
            [idx, *s["xs"], held, weights, *after, *used],
            [SMEM] + [VMEM] * 5 + [ANY] * (1 + len(after)) + [VMEM] * len(used),
            [pltpu.VMEM((2, half, piece), BF16), dma((2,))], name="product_first",
        )
        if "tile" in state[1 - h] and not (step == STEPS - 1 and h == 1):
            gather_sums(1 - h)
        s["pair"] = lax.ppermute(send0, "state", PAIRS)
        s["outer"] = lax.ppermute(send1, "state", FROM_OUTER)
        s["inner"] = lax.ppermute(send1, "state", FROM_INNER)
        s["left"], s["sums"] = left, sums

    def proceed(step, h, forward, message=None, place=None):
        s, at = state[h], h * half
        args = [idx, s["left"], s["sums"], held, weights]
        after = state[1]["xs"][2:] if step == h == 0 else []
        args, specs = args + after, [SMEM] + [VMEM] * 3 + [ANY] * (1 + len(after))
        outs, out_specs, aliases = [wide, wide, tile, code], [VMEM] * 4, None
        has_out = box["out"] is not None
        if place is not None:
            args, specs = args + [message], specs + [VMEM]
            outs, out_specs = outs + [out_shape], out_specs + [ANY]
            if has_out:
                aliases = {len(args): 4}
                args, specs = args + [box["out"]], specs + [ANY]
        result = order(
            functools.partial(rest_body, step, at, place, has_out, len(after)), outs, out_specs, args, specs,
            [pltpu.VMEM((half, 128), F32), pltpu.VMEM((2, half, piece), BF16), dma((3,))], aliases,
            name="product_rest",
        )
        part, s["own"], s["tile"], s["weights"] = result[:4]
        if place is not None:
            box["out"] = result[4]
        swap(h, "state", 1)
        args = [idx, part, s["pair"], s["tile"], s["their"], held, *peaks, s["outer"]]
        specs = [SMEM] + [VMEM] * 9 + [ANY]
        if forward:
            args, specs = args + [state[1 - h]["across"]], specs + [VMEM]
        outs = [code, tile] + [code] * forward
        result = order(
            functools.partial(far_body, step, spreads[step], forward), outs, [VMEM] * len(outs),
            args, specs, name="far_block",
        )
        s["tile"] = result[1]
        swap(h, "state", 2)
        if forward:
            gather_rest(1 - h, result[2])
        s["far"] = lax.ppermute(result[0], "state", LAST)

    def finish(step, h):
        s = state[h]
        args = [idx, s["own"], s["pair"], s["outer"], s["inner"], s["far"], *s["tiles"], s["weights"], held, *peaks]
        specs = [SMEM] + [VMEM] * 15
        if step:
            args, specs = args + [s["logs"]], specs + [VMEM]
        outs, out_specs, aliases, place = [code, rows, tile], [VMEM] * 3, None, None
        scratch = [pltpu.VMEM((half, piece), F32)]
        if step == STEPS - 1:
            place = (step, h * half)
            aliases = {len(args): 3}
            args, specs = args + [box["out"]], specs + [ANY]
            outs, out_specs, scratch = outs + [out_shape], out_specs + [ANY], scratch + [dma]
        result = order(
            functools.partial(last_body, step, spreads[step], hidden, place), outs, out_specs, args, specs,
            scratch, aliases, name="normalise",
        )
        s["lowered"], s["message"], s["logs"] = result[:3]
        if place is not None:
            box["out"] = result[3]

    for s in state:
        own = s["lowered"]
        s["xs"] = [own] + [lax.ppermute(own, ("dp", "sub"), [(i, i ^ k) for i in range(4)]) for k in (1, 2, 3)]
    for step in range(STEPS):
        begin(step, 0)
        if step:
            finish(step - 1, 1)
            gather(1)
            proceed(step, 0, True, state[1]["message"], (step - 1, half))
        else:
            proceed(step, 0, False)
        begin(step, 1)
        if step < STEPS - 1:
            finish(step, 0)
            gather(0)
            proceed(step, 1, True, state[0]["message"], (step, 0))
        else:
            proceed(step, 1, False)
            gather_sums(0)
            finish(step, 0)
    gather_sums(1)
    finish(STEPS - 1, 1)
    log_scale = jnp.concatenate([s["logs"][0] for s in state])
    return box["out"].reshape(STEPS, seqs, 1, 1, piece), log_scale


def shards(transition, emission, start):
    sizes = [lax.axis_size(name) for name in ("state", "dp", "sub")]
    if sizes == [4, 2, 2] and start.shape[0] == HALVES * 128 and start.shape[3] % CHUNK == 0:
        return fast(transition, emission, start)
    return general(transition, emission, start)


def solution(mesh):
    in_specs = (
        P(None, "state", None, ("dp", "sub")),
        P(None, "groups", ("dp", "sub"), None, None),
        P("groups", ("dp", "sub"), "state", None),
    )
    out_specs = (P(None, "groups", ("dp", "sub"), "state", None), P("groups"))
    return jax.shard_map(shards, mesh=mesh, in_specs=in_specs, out_specs=out_specs, check_vma=False)
```

```python
import functools

import jax
import jax.numpy as jnp
from jax import lax
from jax.experimental import pallas as pl
from jax.experimental.pallas import tpu as pltpu
from jax.sharding import PartitionSpec as P

STEPS = 4
HALVES = 2
TOP = 60000.0
START_TOP = 10.0


def product_kernel(num_x, with_peak, idx_ref, *refs):
    x_refs, t_ref, out_ref = refs[:num_x], refs[num_x], refs[num_x + 1]
    depth = x_refs[0].shape[1]
    total = None
    for q in range(num_x):
        rows = pl.ds(pl.multiple_of(idx_ref[1 + q] * depth, depth), depth)
        term = jnp.dot(x_refs[q][...], t_ref[rows, :], preferred_element_type=jnp.float32)
        total = term if total is None else total + term
    out_ref[0] = total
    if with_peak:
        peak_ref = refs[num_x + 2]
        here = jnp.max(t_ref[...].astype(jnp.float32).reshape(-1, 8, t_ref.shape[1]), axis=0)
        first = jnp.logical_and(pl.program_id(0) == 0, pl.program_id(1) == 0)

        @pl.when(first)
        def _():
            peak_ref[...] = here

        @pl.when(jnp.logical_not(first))
        def _():
            peak_ref[...] = jnp.maximum(peak_ref[...], here)


def product(indices, xs, table, blocks, with_peak):
    seqs, depth = xs[0].shape
    rows, width = table.shape
    piece = width // blocks
    tile = min(512, piece)
    per = piece // tile

    def place(o, c, idx):
        return (0, lax.rem(idx[0] + o, blocks) * per + c)

    out_shape = [jax.ShapeDtypeStruct((blocks, seqs, piece), jnp.float32)]
    out_specs = [pl.BlockSpec((1, seqs, tile), lambda o, c, idx: (o, 0, c))]
    if with_peak:
        out_shape.append(jax.ShapeDtypeStruct((8, tile), jnp.float32))
        out_specs.append(pl.BlockSpec((8, tile), lambda o, c, idx: (0, 0)))
    return pl.pallas_call(
        functools.partial(product_kernel, len(xs), with_peak),
        grid_spec=pltpu.PrefetchScalarGridSpec(
            num_scalar_prefetch=1,
            grid=(blocks, per),
            in_specs=[pl.BlockSpec((seqs, depth), lambda o, c, idx: (0, 0)) for _ in xs]
            + [pl.BlockSpec((rows, tile), place)],
            out_specs=out_specs,
        ),
        out_shape=out_shape,
        compiler_params=pltpu.CompilerParams(vmem_limit_bytes=32 * 2**20),
        cost_estimate=pl.CostEstimate(
            flops=2 * seqs * rows * width, bytes_accessed=2 * rows * width, transcendentals=0
        ),
        name="product_peak" if with_peak else "product",
    )(indices, *xs, table)


def gather_blocks(block):
    dp, sub = lax.axis_size("dp"), lax.axis_size("sub")
    found = [block]
    for k in range(1, dp):
        found.append(lax.ppermute(block, "dp", [(i, (i + k) % dp) for i in range(dp)]))
    out = []
    for l in range(sub):
        for item in found:
            out.append(item if l == 0 else lax.ppermute(item, "sub", [(i, (i + l) % sub) for i in range(sub)]))
    return out


def block_owners():
    dp, sub = lax.axis_size("dp"), lax.axis_size("sub")
    x, c = lax.axis_index("dp"), lax.axis_index("sub")
    return [
        lax.rem(x + dp - k, dp) * sub + lax.rem(c + sub - l, sub) for l in range(sub) for k in range(dp)
    ]


def line_sum(parts, into, back, first_into, first_back_r, first_back_l):
    n = lax.axis_size("state")
    right = left = None
    for k in range(1, n):
        scale = first_into if k == 1 else into
        to_r, to_l = parts[n - k], parts[k]
        if k > 1:
            to_r = to_r + right.astype(jnp.float32) * (first_back_r if k == 2 else back)
            to_l = to_l + left.astype(jnp.float32) * (first_back_l if k == 2 else back)
        right = lax.ppermute((to_r * scale).astype(jnp.float16), "state", [(i, i + 1) for i in range(k)])
        left = lax.ppermute((to_l * scale).astype(jnp.float16), "state", [(i, i - 1) for i in range(n - k, n)])
    last_r, last_l = (first_back_r, first_back_l) if n == 2 else (back, back)
    return parts[0] + right.astype(jnp.float32) * last_r + left.astype(jnp.float32) * last_l


def general(transition, emission, start):
    seq_count = start.shape[0]
    piece = start.shape[3]
    blocks = lax.axis_size("state")
    me = lax.axis_index("state")
    table = transition.reshape(transition.shape[0] * piece, transition.shape[3])
    hidden = blocks * piece * lax.axis_size("dp") * lax.axis_size("sub")
    half = seq_count // HALVES
    indices = jnp.stack([me] + block_owners()).astype(jnp.int32)
    weights = jnp.transpose(emission[:, :, 0], (0, 2, 1, 3))
    weights = jnp.concatenate([weights, weights], axis=1)
    weights = lax.dynamic_slice_in_dim(weights, me, blocks, 1)

    messages = [start[h * half : (h + 1) * half, 0, 0] for h in range(HALVES)]
    history, normals = [], []
    into = back = None
    for step in range(STEPS):
        step_messages, step_normals = [], []
        for h in range(HALVES):
            rows = slice(h * half, (h + 1) * half)
            xs = gather_blocks(messages[h].astype(jnp.bfloat16))
            first = step == 0 and h == 0
            if first:
                parts, peak = product(indices, xs, table, blocks, True)
                own_peak = jnp.max(peak)
                peaks = lax.all_gather(jnp.full((1, 128), own_peak), "state", axis=0, tiled=True)[:, 0]
                top_peak = jnp.max(peaks)
                into = TOP / (hidden * top_peak)
                back = hidden * top_peak / TOP
                peak_r = lax.dynamic_index_in_dim(peaks, lax.rem(me + blocks - 1, blocks), 0, False)
                peak_l = lax.dynamic_index_in_dim(peaks, lax.rem(me + 1, blocks), 0, False)
                spread = hidden * START_TOP
                scales = (
                    into / START_TOP, back * START_TOP,
                    TOP / (spread * own_peak), spread * peak_r / TOP, spread * peak_l / TOP,
                )
            else:
                (parts,) = product(indices, xs, table, blocks, False)
                grow = START_TOP if step == 0 else 1.0
                scales = (into / grow, back * grow, into / grow, back * grow, back * grow)
            step_weights = weights[step, :, rows].astype(jnp.float32)
            own_sum = jnp.sum(parts * step_weights, axis=(0, 2))
            sums = lax.all_gather(own_sum[None], ("state", "dp", "sub"), axis=0, tiled=True)
            normal = jnp.sum(sums, axis=0) / hidden
            summed = line_sum([parts[o] for o in range(blocks)], *scales)
            message = summed * step_weights[0] / normal[:, None]
            messages[h] = message
            step_messages.append(message)
            step_normals.append(normal)
        history.append(jnp.concatenate(step_messages, axis=0))
        normals.append(jnp.concatenate(step_normals, axis=0))
    log_scale = functools.reduce(lambda a, b: a + b, [jnp.log(x) for x in normals])
    out = jnp.stack(history).reshape(STEPS, seq_count, 1, 1, piece)
    return out, log_scale


SLOTS = ((3, 2, 1, 0), (0, 2, 3, 1), (3, 1, 0, 2), (0, 1, 2, 3))
PAIRS = [(0, 1), (1, 0), (2, 3), (3, 2)]
FROM_OUTER = [(0, 2), (3, 1)]
FROM_INNER = [(1, 2), (2, 1)]
LAST = [(1, 3), (2, 0), (0, 1), (3, 2)]
CHUNK = 512
VMEM = pl.BlockSpec(memory_space=pltpu.VMEM)
SMEM = pl.BlockSpec(memory_space=pltpu.SMEM)
ANY = pl.BlockSpec(memory_space=pl.ANY)
F32, BF16 = jnp.float32, jnp.bfloat16


def shape(dims, dtype):
    return jax.ShapeDtypeStruct(dims, dtype)


class Order:
    def __init__(self):
        self.last = None

    def __call__(self, body, outs, out_specs, args, specs, scratch=(), aliases=None, name=None):
        count = len(args)
        if self.last is not None:
            args, specs = [*args, self.last], [*specs, ANY]
        extra = len(args) - count

        def run(*refs):
            body(*refs[:count], *refs[count + extra :])

        result = pl.pallas_call(
            run,
            out_shape=tuple(outs),
            in_specs=list(specs),
            out_specs=tuple(out_specs),
            scratch_shapes=list(scratch),
            input_output_aliases=aliases or {},
            compiler_params=pltpu.CompilerParams(vmem_limit_bytes=12 * 2**20),
            cost_estimate=pl.CostEstimate(flops=0, bytes_accessed=1024, transcendentals=0),
            name=name,
        )(*args)
        self.last = result[0]
        return result


def encode(x):
    x = x * x
    x = x * x
    return (x * x).astype(BF16)


def decode(y):
    y = y.astype(F32)
    return jnp.where(y > 0.0, jnp.exp2(0.125 * jnp.log2(y)), 0.0)


def load_body(table_ref, held_ref, peak_ref, sems):
    count = sems.shape[0]
    rows = table_ref.shape[0] // count
    copies = [
        pltpu.make_async_copy(table_ref.at[pl.ds(i * rows, rows)], held_ref.at[pl.ds(i * rows, rows)], sems.at[i])
        for i in range(count)
    ]
    for copy in copies:
        copy.start()
    top = jnp.zeros((16, table_ref.shape[1]), BF16)
    for i, copy in enumerate(copies):
        copy.wait()

        def step(k, best, i=i):
            at = pl.multiple_of(i * rows + k * 16, 16)
            return jnp.maximum(best, held_ref[pl.ds(at, 16), :])

        top = lax.fori_loop(0, rows // 16, step, top)
    peak_ref[...] = jnp.full(peak_ref.shape, jnp.max(top.astype(F32)), F32)


def corner(ref):
    return ref[0:1, 0:1]


def top_of(peaks):
    return jnp.maximum(
        jnp.maximum(corner(peaks[0]), corner(peaks[1])), jnp.maximum(corner(peaks[2]), corner(peaks[3]))
    )


def all_swaps(tile, axes):
    return [tile] + [lax.ppermute(tile, axes, [(i, i ^ k) for i in range(4)]) for k in range(1, 4)]


def products(idx, slot, left_ref, table_ref, weights_ref, sums_ref, arrive, put):
    piece = weights_ref.shape[1]
    for c in range(piece // CHUNK):
        here = slice(c * CHUNK, (c + 1) * CHUNK)
        cols = pl.ds(pl.multiple_of(idx[slot] * piece + c * CHUNK, CHUNK), CHUNK)
        total = jnp.dot(left_ref[...], table_ref[:, cols], preferred_element_type=F32)
        put(here, total)
        if c == 0:
            arrive.wait()
        weighted = total * weights_ref[:, here].astype(F32)
        sums = sums_ref[...]
        for k in range(CHUNK // 128):
            sums = sums + weighted[:, k * 128 : (k + 1) * 128]
        sums_ref[...] = sums


def fetch_weights(idx, slots, step, at, weights_ref, held, sems):
    half = held.shape[1]
    copies = [
        pltpu.make_async_copy(weights_ref.at[step, idx[s], pl.ds(at, half)], held.at[k], sems.at[k])
        for k, s in enumerate(slots)
    ]
    for copy in copies:
        copy.start()
    return copies


def first_body(step, at, spread, extra, idx, x0, x1, x2, x3, table_ref, weights_ref, *refs):
    refs = refs[extra:]
    peaks, (out0_ref, out1_ref, sums_ref, left_ref, held, sems) = refs[:-6], refs[-6:]
    copies = fetch_weights(idx, (0, 1), step, at, weights_ref, held, sems)
    depth = x0.shape[1]
    for q, x in enumerate((x0, x1, x2, x3)):
        left_ref[:, pl.ds(pl.multiple_of(idx[4 + q] * depth, depth), depth)] = x[...]
    scale = (TOP / spread) / (corner(peaks[0]) if step == 0 else top_of(peaks))
    sums_ref[...] = jnp.zeros_like(sums_ref)
    for slot, out_ref in enumerate((out0_ref, out1_ref)):
        def put(here, total, out_ref=out_ref):
            out_ref[:, here] = encode(total * scale)

        products(idx, slot, left_ref, table_ref, held.at[slot], sums_ref, copies[slot], put)


def rest_body(step, at, write, has_out, extra, idx, left_ref, sums_in, table_ref, weights_ref, *refs):
    refs = refs[extra:]
    if write is not None:
        message_ref, refs = refs[0], refs[2 if has_out else 1 :]
    (part_ref, own_ref, tile_ref, own_weights_ref), refs = refs[:4], refs[4:]
    if write is not None:
        out_ref, refs = refs[0], refs[1:]
    sums_ref, held, sems = refs
    if write is not None:
        copy_out = pltpu.make_async_copy(message_ref, out_ref.at[write[0], pl.ds(write[1], message_ref.shape[0])], sems.at[2])
        copy_out.start()
    copies = fetch_weights(idx, (2, 3), step, at, weights_ref, held, sems)
    sums_ref[...] = sums_in[...]
    for k, out in enumerate((part_ref, own_ref)):
        def put(here, total, out=out):
            out[:, here] = total

        products(idx, 2 + k, left_ref, table_ref, held.at[k], sums_ref, copies[k], put)
    own_weights_ref[...] = held[1]
    tile_ref[...] = jnp.broadcast_to(jnp.sum(sums_ref[...].T, axis=0, keepdims=True), tile_ref.shape)
    if write is not None:
        copy_out.wait()


def add_body(a_ref, b_ref, table_ref, *refs):
    refs[-1][...] = a_ref[...] + b_ref[...]


def sum_body(a_ref, b_ref, c_ref, d_ref, table_ref, out):
    out[...] = (a_ref[...] + b_ref[...]) + (c_ref[...] + d_ref[...])


def far_body(step, spread, forward, idx, part_ref, pair_ref, table_ref, *refs):
    peaks, refs = refs[:4], refs[4:]
    if forward:
        refs[2][...] = refs[0][...]
        refs = refs[1:]
    out = refs[0]
    top = top_of(peaks)
    scale = (TOP / spread) / top

    @pl.when(idx[8] == 1)
    def _():
        pair = decode(pair_ref[...])
        if step == 0:
            pair = pair * (corner(peaks[1]) / top)
        out[...] = encode(part_ref[...] * scale + pair)

    @pl.when(idx[8] == 0)
    def _():
        out[...] = encode(part_ref[...] * scale)


def last_body(step, spread, hidden, finish, idx, own_ref, pair_ref, outer_ref, inner_ref, far_ref, sums0, sums1, sums2, sums3, weights_ref, table_ref, *refs):
    peaks, logs_in, refs = refs[:4], refs[4] if step else None, refs[5 if step else 4 :]
    if finish is not None:
        refs = refs[1:]
    lowered_ref, message_ref, logs_ref = refs[:3]
    if finish is not None:
        out_ref, mixed_ref, sem = refs[3:]
    else:
        (mixed_ref,) = refs[3:]
    half = own_ref.shape[0]
    top = top_of(peaks)
    unscale = top * (spread / TOP)
    normal = ((sums0[...] + sums1[...]) + (sums2[...] + sums3[...])) / hidden
    logs = jnp.log(normal)
    logs_ref[...] = logs if logs_in is None else logs_in[...] + logs
    inverse = jnp.broadcast_to(1.0 / normal[0:1, :], (half, half)).T

    def sent_by(k):
        return corner(peaks[k]) * (spread / TOP) if step == 0 else unscale

    @pl.when(idx[8] == 1)
    def _():
        mixed_ref[...] = (
            own_ref[...]
            + (decode(outer_ref[...]) * sent_by(2) + decode(inner_ref[...]) * sent_by(3))
            + decode(far_ref[...]) * unscale
        )

    @pl.when(idx[8] == 0)
    def _():
        mixed_ref[...] = own_ref[...] + (decode(pair_ref[...]) * sent_by(1) + decode(far_ref[...]) * unscale)

    for k in range(own_ref.shape[1] // 128):
        here = slice(k * 128, (k + 1) * 128)
        message = mixed_ref[:, here] * weights_ref[:, here].astype(F32) * inverse
        lowered_ref[:, here] = message.astype(BF16)
        message_ref[:, k, :] = message
    if finish is not None:
        write = pltpu.make_async_copy(message_ref, out_ref.at[finish[0], pl.ds(finish[1], half)], sem)
        write.start()
        write.wait()


def fast(transition, emission, start):
    seqs, piece = start.shape[0], start.shape[3]
    hidden = 16 * piece
    half = seqs // HALVES
    table = transition.reshape(4 * piece, 4 * piece)
    me = lax.axis_index("state")
    d = lax.axis_index("dp") * 2 + lax.axis_index("sub")
    slots = jnp.asarray(SLOTS, jnp.int32)[me]
    inner = jnp.logical_and(me > 0, me < 3)
    idx = jnp.concatenate([slots, jnp.stack([d, d ^ 1, d ^ 2, d ^ 3, inner]).astype(jnp.int32)])
    weights = jnp.transpose(emission[:, :, 0], (0, 2, 1, 3))
    wide, code = shape((half, piece), F32), shape((half, piece), BF16)
    square, tile = shape((half, 128), F32), shape((8, 128), F32)
    rows = shape((half, piece // 128, 128), F32)
    out_shape = shape((STEPS, seqs, piece // 128, 128), F32)
    dma = pltpu.SemaphoreType.DMA
    order = Order()

    table, weights, idx = lax.optimization_barrier((table, weights, idx))
    weights = pltpu.with_memory_space_constraint(weights, pltpu.HBM)
    held, peak = order(
        load_body, [pltpu.VMEM(table.shape, table.dtype), shape((8, 128), F32)], [VMEM] * 2, [table], [ANY],
        [dma((8,))], name="load_table",
    )
    order.last = peak
    held = pltpu.with_memory_space_constraint(held, pltpu.VMEM)
    peaks = all_swaps(peak, "state")

    spreads = [hidden * 1.01 * (START_TOP if step == 0 else 1.0) for step in range(STEPS)]
    state = [{"lowered": start[h * half : (h + 1) * half, 0, 0].astype(BF16)} for h in range(HALVES)]
    box = {"out": None}

    def swap(h, axis, k):
        s = state[h]
        s["their"] = lax.ppermute(s["tile"], axis, [(i, i ^ k) for i in range(lax.axis_size(axis))])

    def gather_sums(h):
        add(h)
        state[h]["tiles"] = all_swaps(state[h]["tile"], ("dp", "sub"))

    def add(h, after=()):
        s = state[h]
        s["tile"] = order(
            add_body, [tile], [VMEM], [s["tile"], s["their"], held, *after], [VMEM] * 3 + [ANY] * len(after),
            name="add_sums",
        )[0]

    def gather(h):
        s = state[h]
        own = s["lowered"]
        s["across"] = lax.ppermute(own, "dp", [(0, 1), (1, 0)])
        s["xs"] = [own, lax.ppermute(own, "sub", [(0, 1), (1, 0)])]

    def gather_rest(h, across):
        state[h]["xs"] += [across, lax.ppermute(across, "sub", [(0, 1), (1, 0)])]

    def begin(step, h):
        s, at, spread = state[h], h * half, spreads[step]
        used = [peak] if step == 0 else peaks
        after = [state[1 - h]["inner"]] if "inner" in state[1 - h] else []
        send0, send1, sums, left = order(
            functools.partial(first_body, step, at, spread, len(after)),
            [code, code, square, shape((half, 4 * piece), BF16)], [VMEM] * 4,
            [idx, *s["xs"], held, weights, *after, *used],
            [SMEM] + [VMEM] * 5 + [ANY] * (1 + len(after)) + [VMEM] * len(used),
            [pltpu.VMEM((2, half, piece), BF16), dma((2,))], name="product_first",
        )
        if "tile" in state[1 - h] and not (step == STEPS - 1 and h == 1):
            gather_sums(1 - h)
        s["pair"] = lax.ppermute(send0, "state", PAIRS)
        s["outer"] = lax.ppermute(send1, "state", FROM_OUTER)
        s["inner"] = lax.ppermute(send1, "state", FROM_INNER)
        s["left"], s["sums"] = left, sums

    def proceed(step, h, forward, message=None, place=None):
        s, at = state[h], h * half
        args = [idx, s["left"], s["sums"], held, weights]
        after = state[1]["xs"][2:] if step == h == 0 else []
        args, specs = args + after, [SMEM] + [VMEM] * 3 + [ANY] * (1 + len(after))
        outs, out_specs, aliases = [wide, wide, tile, code], [VMEM] * 4, None
        has_out = box["out"] is not None
        if place is not None:
            args, specs = args + [message], specs + [VMEM]
            outs, out_specs = outs + [out_shape], out_specs + [ANY]
            if has_out:
                aliases = {len(args): 4}
                args, specs = args + [box["out"]], specs + [ANY]
        result = order(
            functools.partial(rest_body, step, at, place, has_out, len(after)), outs, out_specs, args, specs,
            [pltpu.VMEM((half, 128), F32), pltpu.VMEM((2, half, piece), BF16), dma((3,))], aliases,
            name="product_rest",
        )
        part, s["own"], s["tile"], s["weights"] = result[:4]
        if place is not None:
            box["out"] = result[4]
        ends = step == STEPS - 1 and h == HALVES - 1
        if ends:
            s["lines"] = all_swaps(s["tile"], "state")
        else:
            swap(h, "state", 1)
        args = [idx, part, s["pair"], held, *peaks]
        if forward:
            args.append(state[1 - h]["across"])
        count = 2 if forward else 1
        result = order(
            functools.partial(far_body, step, spreads[step], forward), [code] * count, [VMEM] * count,
            args, [SMEM] + [VMEM] * (len(args) - 1), name="far_block",
        )
        if forward:
            gather_rest(1 - h, result[1])
        s["far"] = lax.ppermute(result[0], "state", LAST)
        if not ends:
            add(h, [s["outer"]])
            swap(h, "state", 2)

    def finish(step, h):
        s = state[h]
        args = [idx, s["own"], s["pair"], s["outer"], s["inner"], s["far"], *s["tiles"], s["weights"], held, *peaks]
        specs = [SMEM] + [VMEM] * 15
        if step:
            args, specs = args + [s["logs"]], specs + [VMEM]
        outs, out_specs, aliases, place = [code, rows, tile], [VMEM] * 3, None, None
        scratch = [pltpu.VMEM((half, piece), F32)]
        if step == STEPS - 1:
            place = (step, h * half)
            aliases = {len(args): 3}
            args, specs = args + [box["out"]], specs + [ANY]
            outs, out_specs, scratch = outs + [out_shape], out_specs + [ANY], scratch + [dma]
        result = order(
            functools.partial(last_body, step, spreads[step], hidden, place), outs, out_specs, args, specs,
            scratch, aliases, name="normalise",
        )
        s["lowered"], s["message"], s["logs"] = result[:3]
        if place is not None:
            box["out"] = result[3]

    for s in state:
        own = s["lowered"]
        s["xs"] = [own] + [lax.ppermute(own, ("dp", "sub"), [(i, i ^ k) for i in range(4)]) for k in (1, 2, 3)]
    for step in range(STEPS):
        begin(step, 0)
        if step:
            finish(step - 1, 1)
            gather(1)
            proceed(step, 0, True, state[1]["message"], (step - 1, half))
        else:
            proceed(step, 0, False)
        begin(step, 1)
        if step < STEPS - 1:
            finish(step, 0)
            gather(0)
            proceed(step, 1, True, state[0]["message"], (step, 0))
        else:
            proceed(step, 1, False)
            gather_sums(0)
            finish(step, 0)
    total = order(sum_body, [tile], [VMEM], [*state[1]["lines"], held], [VMEM] * 5, name="add_lines")[0]
    state[1]["tiles"] = all_swaps(total, ("dp", "sub"))
    finish(STEPS - 1, 1)
    log_scale = jnp.concatenate([s["logs"][0] for s in state])
    return box["out"].reshape(STEPS, seqs, 1, 1, piece), log_scale


def shards(transition, emission, start):
    sizes = [lax.axis_size(name) for name in ("state", "dp", "sub")]
    if sizes == [4, 2, 2] and start.shape[0] == HALVES * 128 and start.shape[3] % CHUNK == 0:
        return fast(transition, emission, start)
    return general(transition, emission, start)


def solution(mesh):
    in_specs = (
        P(None, "state", None, ("dp", "sub")),
        P(None, "groups", ("dp", "sub"), None, None),
        P("groups", ("dp", "sub"), "state", None),
    )
    out_specs = (P(None, "groups", ("dp", "sub"), "state", None), P("groups"))
    return jax.shard_map(shards, mesh=mesh, in_specs=in_specs, out_specs=out_specs, check_vma=False)
```

```python
import functools

import jax
import jax.numpy as jnp
from jax import lax
from jax.experimental import pallas as pl
from jax.experimental.pallas import tpu as pltpu
from jax.sharding import PartitionSpec as P

STEPS = 4
HALVES = 2
TOP = 60000.0
START_TOP = 10.0


def product_kernel(num_x, with_peak, idx_ref, *refs):
    x_refs, t_ref, out_ref = refs[:num_x], refs[num_x], refs[num_x + 1]
    depth = x_refs[0].shape[1]
    total = None
    for q in range(num_x):
        rows = pl.ds(pl.multiple_of(idx_ref[1 + q] * depth, depth), depth)
        term = jnp.dot(x_refs[q][...], t_ref[rows, :], preferred_element_type=jnp.float32)
        total = term if total is None else total + term
    out_ref[0] = total
    if with_peak:
        peak_ref = refs[num_x + 2]
        here = jnp.max(t_ref[...].astype(jnp.float32).reshape(-1, 8, t_ref.shape[1]), axis=0)
        first = jnp.logical_and(pl.program_id(0) == 0, pl.program_id(1) == 0)

        @pl.when(first)
        def _():
            peak_ref[...] = here

        @pl.when(jnp.logical_not(first))
        def _():
            peak_ref[...] = jnp.maximum(peak_ref[...], here)


def product(indices, xs, table, blocks, with_peak):
    seqs, depth = xs[0].shape
    rows, width = table.shape
    piece = width // blocks
    tile = min(512, piece)
    per = piece // tile

    def place(o, c, idx):
        return (0, lax.rem(idx[0] + o, blocks) * per + c)

    out_shape = [jax.ShapeDtypeStruct((blocks, seqs, piece), jnp.float32)]
    out_specs = [pl.BlockSpec((1, seqs, tile), lambda o, c, idx: (o, 0, c))]
    if with_peak:
        out_shape.append(jax.ShapeDtypeStruct((8, tile), jnp.float32))
        out_specs.append(pl.BlockSpec((8, tile), lambda o, c, idx: (0, 0)))
    return pl.pallas_call(
        functools.partial(product_kernel, len(xs), with_peak),
        grid_spec=pltpu.PrefetchScalarGridSpec(
            num_scalar_prefetch=1,
            grid=(blocks, per),
            in_specs=[pl.BlockSpec((seqs, depth), lambda o, c, idx: (0, 0)) for _ in xs]
            + [pl.BlockSpec((rows, tile), place)],
            out_specs=out_specs,
        ),
        out_shape=out_shape,
        compiler_params=pltpu.CompilerParams(vmem_limit_bytes=32 * 2**20),
        cost_estimate=pl.CostEstimate(
            flops=2 * seqs * rows * width, bytes_accessed=2 * rows * width, transcendentals=0
        ),
        name="product_peak" if with_peak else "product",
    )(indices, *xs, table)


def gather_blocks(block):
    dp, sub = lax.axis_size("dp"), lax.axis_size("sub")
    found = [block]
    for k in range(1, dp):
        found.append(lax.ppermute(block, "dp", [(i, (i + k) % dp) for i in range(dp)]))
    out = []
    for l in range(sub):
        for item in found:
            out.append(item if l == 0 else lax.ppermute(item, "sub", [(i, (i + l) % sub) for i in range(sub)]))
    return out


def block_owners():
    dp, sub = lax.axis_size("dp"), lax.axis_size("sub")
    x, c = lax.axis_index("dp"), lax.axis_index("sub")
    return [
        lax.rem(x + dp - k, dp) * sub + lax.rem(c + sub - l, sub) for l in range(sub) for k in range(dp)
    ]


def line_sum(parts, into, back, first_into, first_back_r, first_back_l):
    n = lax.axis_size("state")
    right = left = None
    for k in range(1, n):
        scale = first_into if k == 1 else into
        to_r, to_l = parts[n - k], parts[k]
        if k > 1:
            to_r = to_r + right.astype(jnp.float32) * (first_back_r if k == 2 else back)
            to_l = to_l + left.astype(jnp.float32) * (first_back_l if k == 2 else back)
        right = lax.ppermute((to_r * scale).astype(jnp.float16), "state", [(i, i + 1) for i in range(k)])
        left = lax.ppermute((to_l * scale).astype(jnp.float16), "state", [(i, i - 1) for i in range(n - k, n)])
    last_r, last_l = (first_back_r, first_back_l) if n == 2 else (back, back)
    return parts[0] + right.astype(jnp.float32) * last_r + left.astype(jnp.float32) * last_l


def general(transition, emission, start):
    seq_count = start.shape[0]
    piece = start.shape[3]
    blocks = lax.axis_size("state")
    me = lax.axis_index("state")
    table = transition.reshape(transition.shape[0] * piece, transition.shape[3])
    hidden = blocks * piece * lax.axis_size("dp") * lax.axis_size("sub")
    half = seq_count // HALVES
    indices = jnp.stack([me] + block_owners()).astype(jnp.int32)
    weights = jnp.transpose(emission[:, :, 0], (0, 2, 1, 3))
    weights = jnp.concatenate([weights, weights], axis=1)
    weights = lax.dynamic_slice_in_dim(weights, me, blocks, 1)

    messages = [start[h * half : (h + 1) * half, 0, 0] for h in range(HALVES)]
    history, normals = [], []
    into = back = None
    for step in range(STEPS):
        step_messages, step_normals = [], []
        for h in range(HALVES):
            rows = slice(h * half, (h + 1) * half)
            xs = gather_blocks(messages[h].astype(jnp.bfloat16))
            first = step == 0 and h == 0
            if first:
                parts, peak = product(indices, xs, table, blocks, True)
                own_peak = jnp.max(peak)
                peaks = lax.all_gather(jnp.full((1, 128), own_peak), "state", axis=0, tiled=True)[:, 0]
                top_peak = jnp.max(peaks)
                into = TOP / (hidden * top_peak)
                back = hidden * top_peak / TOP
                peak_r = lax.dynamic_index_in_dim(peaks, lax.rem(me + blocks - 1, blocks), 0, False)
                peak_l = lax.dynamic_index_in_dim(peaks, lax.rem(me + 1, blocks), 0, False)
                spread = hidden * START_TOP
                scales = (
                    into / START_TOP, back * START_TOP,
                    TOP / (spread * own_peak), spread * peak_r / TOP, spread * peak_l / TOP,
                )
            else:
                (parts,) = product(indices, xs, table, blocks, False)
                grow = START_TOP if step == 0 else 1.0
                scales = (into / grow, back * grow, into / grow, back * grow, back * grow)
            step_weights = weights[step, :, rows].astype(jnp.float32)
            own_sum = jnp.sum(parts * step_weights, axis=(0, 2))
            sums = lax.all_gather(own_sum[None], ("state", "dp", "sub"), axis=0, tiled=True)
            normal = jnp.sum(sums, axis=0) / hidden
            summed = line_sum([parts[o] for o in range(blocks)], *scales)
            message = summed * step_weights[0] / normal[:, None]
            messages[h] = message
            step_messages.append(message)
            step_normals.append(normal)
        history.append(jnp.concatenate(step_messages, axis=0))
        normals.append(jnp.concatenate(step_normals, axis=0))
    log_scale = functools.reduce(lambda a, b: a + b, [jnp.log(x) for x in normals])
    out = jnp.stack(history).reshape(STEPS, seq_count, 1, 1, piece)
    return out, log_scale


SLOTS = ((3, 2, 1, 0), (0, 2, 3, 1), (3, 1, 0, 2), (0, 1, 2, 3))
PAIRS = [(0, 1), (1, 0), (2, 3), (3, 2)]
FROM_OUTER = [(0, 2), (3, 1)]
FROM_INNER = [(1, 2), (2, 1)]
LAST = [(1, 3), (2, 0), (0, 1), (3, 2)]
CHUNK = 512
VMEM = pl.BlockSpec(memory_space=pltpu.VMEM)
SMEM = pl.BlockSpec(memory_space=pltpu.SMEM)
ANY = pl.BlockSpec(memory_space=pl.ANY)
F32, BF16 = jnp.float32, jnp.bfloat16


def shape(dims, dtype):
    return jax.ShapeDtypeStruct(dims, dtype)


class Order:
    def __init__(self):
        self.last = None

    def __call__(self, body, outs, out_specs, args, specs, scratch=(), aliases=None, name=None):
        count = len(args)
        if self.last is not None:
            args, specs = [*args, self.last], [*specs, ANY]
        extra = len(args) - count

        def run(*refs):
            body(*refs[:count], *refs[count + extra :])

        result = pl.pallas_call(
            run,
            out_shape=tuple(outs),
            in_specs=list(specs),
            out_specs=tuple(out_specs),
            scratch_shapes=list(scratch),
            input_output_aliases=aliases or {},
            compiler_params=pltpu.CompilerParams(vmem_limit_bytes=12 * 2**20),
            cost_estimate=pl.CostEstimate(flops=0, bytes_accessed=1024, transcendentals=0),
            name=name,
        )(*args)
        self.last = result[0]
        return result


def encode(x):
    x = x * x
    x = x * x
    return (x * x).astype(BF16)


def decode(y):
    y = y.astype(F32)
    return jnp.where(y > 0.0, jnp.exp2(0.125 * jnp.log2(y)), 0.0)


def load_body(table_ref, held_ref, peak_ref, sems):
    count = sems.shape[0]
    rows = table_ref.shape[0] // count
    copies = [
        pltpu.make_async_copy(table_ref.at[pl.ds(i * rows, rows)], held_ref.at[pl.ds(i * rows, rows)], sems.at[i])
        for i in range(count)
    ]
    for copy in copies:
        copy.start()
    top = jnp.zeros((16, table_ref.shape[1]), BF16)
    for i, copy in enumerate(copies):
        copy.wait()

        def step(k, best, i=i):
            at = pl.multiple_of(i * rows + k * 16, 16)
            return jnp.maximum(best, held_ref[pl.ds(at, 16), :])

        top = lax.fori_loop(0, rows // 16, step, top)
    peak_ref[...] = jnp.full(peak_ref.shape, jnp.max(top.astype(F32)), F32)


def corner(ref):
    return ref[0:1, 0:1]


def top_of(peaks):
    return jnp.maximum(
        jnp.maximum(corner(peaks[0]), corner(peaks[1])), jnp.maximum(corner(peaks[2]), corner(peaks[3]))
    )


def all_swaps(tile, axes):
    return [tile] + [lax.ppermute(tile, axes, [(i, i ^ k) for i in range(4)]) for k in range(1, 4)]


def products(idx, slot, left_ref, table_ref, weights_ref, sums_ref, arrive, put):
    piece = weights_ref.shape[1]
    for c in range(piece // CHUNK):
        here = slice(c * CHUNK, (c + 1) * CHUNK)
        cols = pl.ds(pl.multiple_of(idx[slot] * piece + c * CHUNK, CHUNK), CHUNK)
        total = jnp.dot(left_ref[...], table_ref[:, cols], preferred_element_type=F32)
        put(here, total)
        if c == 0:
            arrive.wait()
        weighted = total * weights_ref[:, here].astype(F32)
        sums = sums_ref[...]
        for k in range(CHUNK // 128):
            sums = sums + weighted[:, k * 128 : (k + 1) * 128]
        sums_ref[...] = sums


def fetch_weights(idx, slots, step, at, weights_ref, held, sems):
    half = held.shape[1]
    copies = [
        pltpu.make_async_copy(weights_ref.at[step, idx[s], pl.ds(at, half)], held.at[k], sems.at[k])
        for k, s in enumerate(slots)
    ]
    for copy in copies:
        copy.start()
    return copies


def first_body(step, at, spread, idx, x0, x1, x2, x3, table_ref, weights_ref, *refs):
    peaks, (out0_ref, out1_ref, sums_ref, left_ref, held, sems) = refs[:-6], refs[-6:]
    copies = fetch_weights(idx, (0, 1), step, at, weights_ref, held, sems)
    depth = x0.shape[1]
    for q, x in enumerate((x0, x1, x2, x3)):
        left_ref[:, pl.ds(pl.multiple_of(idx[4 + q] * depth, depth), depth)] = x[...]
    scale = (TOP / spread) / (corner(peaks[0]) if step == 0 else top_of(peaks))
    sums_ref[...] = jnp.zeros_like(sums_ref)
    for slot, out_ref in enumerate((out0_ref, out1_ref)):
        def put(here, total, out_ref=out_ref):
            out_ref[:, here] = encode(total * scale)

        products(idx, slot, left_ref, table_ref, held.at[slot], sums_ref, copies[slot], put)


def rest_body(step, at, write, has_out, extra, idx, left_ref, sums_in, table_ref, weights_ref, *refs):
    refs = refs[extra:]
    if write is not None:
        message_ref, refs = refs[0], refs[2 if has_out else 1 :]
    (part_ref, own_ref, tile_ref, own_weights_ref), refs = refs[:4], refs[4:]
    if write is not None:
        out_ref, refs = refs[0], refs[1:]
    sums_ref, held, sems = refs
    if write is not None:
        copy_out = pltpu.make_async_copy(message_ref, out_ref.at[write[0], pl.ds(write[1], message_ref.shape[0])], sems.at[2])
        copy_out.start()
    copies = fetch_weights(idx, (2, 3), step, at, weights_ref, held, sems)
    sums_ref[...] = sums_in[...]
    for k, out in enumerate((part_ref, own_ref)):
        def put(here, total, out=out):
            out[:, here] = total

        products(idx, 2 + k, left_ref, table_ref, held.at[k], sums_ref, copies[k], put)
    own_weights_ref[...] = held[1]
    tile_ref[...] = jnp.broadcast_to(jnp.sum(sums_ref[...].T, axis=0, keepdims=True), tile_ref.shape)
    if write is not None:
        copy_out.wait()


def add_body(a_ref, b_ref, table_ref, *refs):
    refs[-1][...] = a_ref[...] + b_ref[...]


def far_body(step, spread, forward, extra, idx, part_ref, pair_ref, table_ref, *refs):
    peaks, refs = refs[:4], refs[4 + extra :]
    if forward:
        refs[2][...] = refs[0][...]
        refs = refs[1:]
    out = refs[0]
    top = top_of(peaks)
    scale = (TOP / spread) / top

    @pl.when(idx[8] == 1)
    def _():
        pair = decode(pair_ref[...])
        if step == 0:
            pair = pair * (corner(peaks[1]) / top)
        out[...] = encode(part_ref[...] * scale + pair)

    @pl.when(idx[8] == 0)
    def _():
        out[...] = encode(part_ref[...] * scale)


def last_body(step, spread, hidden, finish, count, idx, own_ref, pair_ref, outer_ref, inner_ref, far_ref, weights_ref, table_ref, *refs):
    tiles, refs = [ref[...] for ref in refs[:count]], refs[count:]
    peaks, logs_in, refs = refs[:4], refs[4] if step else None, refs[5 if step else 4 :]
    if finish is not None:
        refs = refs[1:]
    lowered_ref, message_ref, logs_ref = refs[:3]
    if finish is not None:
        out_ref, mixed_ref, sem = refs[3:]
    else:
        (mixed_ref,) = refs[3:]
    half = own_ref.shape[0]
    top = top_of(peaks)
    unscale = top * (spread / TOP)
    total = tiles[0] + tiles[1]
    if count == 4:
        total = total + (tiles[2] + tiles[3])
    normal = total / hidden
    logs = jnp.log(normal)
    logs_ref[...] = logs if logs_in is None else logs_in[...] + logs
    inverse = jnp.broadcast_to(1.0 / normal[0:1, :], (half, half)).T

    def sent_by(k):
        return corner(peaks[k]) * (spread / TOP) if step == 0 else unscale

    @pl.when(idx[8] == 1)
    def _():
        mixed_ref[...] = (
            own_ref[...]
            + (decode(outer_ref[...]) * sent_by(2) + decode(inner_ref[...]) * sent_by(3))
            + decode(far_ref[...]) * unscale
        )

    @pl.when(idx[8] == 0)
    def _():
        mixed_ref[...] = own_ref[...] + (decode(pair_ref[...]) * sent_by(1) + decode(far_ref[...]) * unscale)

    for k in range(own_ref.shape[1] // 128):
        here = slice(k * 128, (k + 1) * 128)
        message = mixed_ref[:, here] * weights_ref[:, here].astype(F32) * inverse
        lowered_ref[:, here] = message.astype(BF16)
        message_ref[:, k, :] = message
    if finish is not None:
        write = pltpu.make_async_copy(message_ref, out_ref.at[finish[0], pl.ds(finish[1], half)], sem)
        write.start()
        write.wait()


def fast(transition, emission, start):
    seqs, piece = start.shape[0], start.shape[3]
    hidden = 16 * piece
    half = seqs // HALVES
    table = transition.reshape(4 * piece, 4 * piece)
    me = lax.axis_index("state")
    d = lax.axis_index("dp") * 2 + lax.axis_index("sub")
    slots = jnp.asarray(SLOTS, jnp.int32)[me]
    inner = jnp.logical_and(me > 0, me < 3)
    idx = jnp.concatenate([slots, jnp.stack([d, d ^ 1, d ^ 2, d ^ 3, inner]).astype(jnp.int32)])
    weights = jnp.transpose(emission[:, :, 0], (0, 2, 1, 3))
    wide, code = shape((half, piece), F32), shape((half, piece), BF16)
    square, tile = shape((half, 128), F32), shape((8, 128), F32)
    rows = shape((half, piece // 128, 128), F32)
    out_shape = shape((STEPS, seqs, piece // 128, 128), F32)
    dma = pltpu.SemaphoreType.DMA
    order = Order()

    table, weights, idx = lax.optimization_barrier((table, weights, idx))
    weights = pltpu.with_memory_space_constraint(weights, pltpu.HBM)
    held, peak = order(
        load_body, [pltpu.VMEM(table.shape, table.dtype), shape((8, 128), F32)], [VMEM] * 2, [table], [ANY],
        [dma((8,))], name="load_table",
    )
    order.last = peak
    held = pltpu.with_memory_space_constraint(held, pltpu.VMEM)
    peaks = all_swaps(peak, "state")

    spreads = [hidden * 1.01 * (START_TOP if step == 0 else 1.0) for step in range(STEPS)]
    state = [{"lowered": start[h * half : (h + 1) * half, 0, 0].astype(BF16)} for h in range(HALVES)]
    box = {"out": None}

    def swap(h, axis, k):
        s = state[h]
        s["their"] = lax.ppermute(s["tile"], axis, [(i, i ^ k) for i in range(lax.axis_size(axis))])

    def add(h, after=()):
        s = state[h]
        s["tile"] = order(
            add_body, [tile], [VMEM], [s["tile"], s["their"], held, *after], [VMEM] * 3 + [ANY] * len(after),
            name="add_sums",
        )[0]

    def gather(h):
        s = state[h]
        own = s["lowered"]
        s["across"] = lax.ppermute(own, "dp", [(0, 1), (1, 0)])
        s["xs"] = [own, lax.ppermute(own, "sub", [(0, 1), (1, 0)])]

    def gather_rest(h, across):
        state[h]["xs"] += [across, lax.ppermute(across, "sub", [(0, 1), (1, 0)])]

    def begin(step, h):
        s, at, spread = state[h], h * half, spreads[step]
        used = [peak] if step == 0 else peaks
        send0, send1, sums, left = order(
            functools.partial(first_body, step, at, spread),
            [code, code, square, shape((half, 4 * piece), BF16)], [VMEM] * 4,
            [idx, *s["xs"], held, weights, *used], [SMEM] + [VMEM] * 5 + [ANY] + [VMEM] * len(used),
            [pltpu.VMEM((2, half, piece), BF16), dma((2,))], name="product_first",
        )
        ends = step == STEPS - 1 and h == 1
        if "tile" in state[1 - h] and not ends:
            add(1 - h)
            swap(1 - h, "sub", 1)
        s["pair"] = lax.ppermute(send0, "state", PAIRS)
        if ends:
            s["send1"] = send1
        else:
            s["outer"] = lax.ppermute(send1, "state", FROM_OUTER)
            s["inner"] = lax.ppermute(send1, "state", FROM_INNER)
        s["left"], s["sums"] = left, sums

    def proceed(step, h, forward, message=None, place=None):
        s, at = state[h], h * half
        args = [idx, s["left"], s["sums"], held, weights]
        after = state[1]["xs"][2:] if step == h == 0 else []
        args, specs = args + after, [SMEM] + [VMEM] * 3 + [ANY] * (1 + len(after))
        outs, out_specs, aliases = [wide, wide, tile, code], [VMEM] * 4, None
        has_out = box["out"] is not None
        if place is not None:
            args, specs = args + [message], specs + [VMEM]
            outs, out_specs = outs + [out_shape], out_specs + [ANY]
            if has_out:
                aliases = {len(args): 4}
                args, specs = args + [box["out"]], specs + [ANY]
        result = order(
            functools.partial(rest_body, step, at, place, has_out, len(after)), outs, out_specs, args, specs,
            [pltpu.VMEM((half, 128), F32), pltpu.VMEM((2, half, piece), BF16), dma((3,))], aliases,
            name="product_rest",
        )
        part, s["own"], s["tile"], s["weights"] = result[:4]
        if place is not None:
            box["out"] = result[4]
        swap(h, "state", 1)
        ends = step == STEPS - 1 and h == 1
        args = [idx, part, s["pair"], held, *peaks]
        if ends:
            args.append(s["their"])
        specs = [SMEM] + [VMEM] * 7 + [ANY] * ends
        if forward or ends:
            args, specs = args + [s["send1"] if ends else state[1 - h]["across"]], specs + [VMEM]
        count = 2 if forward or ends else 1
        result = order(
            functools.partial(far_body, step, spreads[step], forward or ends, int(ends)), [code] * count, [VMEM] * count,
            args, specs, name="far_block",
        )
        if ends:
            add(h)
            swap(h, "state", 2)
            s["far"] = lax.ppermute(result[0], "state", LAST)
            s["outer"] = lax.ppermute(result[1], "state", FROM_OUTER)
            s["inner"] = lax.ppermute(result[1], "state", FROM_INNER)
            return
        if forward:
            gather_rest(1 - h, result[1])
        s["far"] = lax.ppermute(result[0], "state", LAST)
        add(h, [s["outer"]])
        swap(h, "dp", 1)
        add(h, [s["inner"]])
        swap(h, "state", 2)
        if step == STEPS - 1:
            add(h)
            swap(h, "sub", 1)

    def finish(step, h):
        s = state[h]
        args = [idx, s["own"], s["pair"], s["outer"], s["inner"], s["far"], s["weights"], held]
        tiles = s.get("tiles") or [s["tile"], s["their"]]
        args += [*tiles, *peaks]
        specs = [SMEM] + [VMEM] * (len(args) - 1)
        if step:
            args, specs = args + [s["logs"]], specs + [VMEM]
        outs, out_specs, aliases, place = [code, rows, tile], [VMEM] * 3, None, None
        scratch = [pltpu.VMEM((half, piece), F32)]
        if step == STEPS - 1:
            place = (step, h * half)
            aliases = {len(args): 3}
            args, specs = args + [box["out"]], specs + [ANY]
            outs, out_specs, scratch = outs + [out_shape], out_specs + [ANY], scratch + [dma]
        result = order(
            functools.partial(last_body, step, spreads[step], hidden, place, len(tiles)), outs, out_specs, args, specs,
            scratch, aliases, name="normalise",
        )
        s["lowered"], s["message"], s["logs"] = result[:3]
        if place is not None:
            box["out"] = result[3]

    for s in state:
        own = s["lowered"]
        s["xs"] = [own] + [lax.ppermute(own, ("dp", "sub"), [(i, i ^ k) for i in range(4)]) for k in (1, 2, 3)]
    for step in range(STEPS):
        begin(step, 0)
        if step:
            finish(step - 1, 1)
            gather(1)
            proceed(step, 0, True, state[1]["message"], (step - 1, half))
        else:
            proceed(step, 0, False)
        begin(step, 1)
        if step < STEPS - 1:
            finish(step, 0)
            gather(0)
            proceed(step, 1, True, state[0]["message"], (step, 0))
        else:
            proceed(step, 1, False)
            finish(step, 0)
    add(1)
    state[1]["tiles"] = all_swaps(state[1]["tile"], ("dp", "sub"))
    finish(STEPS - 1, 1)
    log_scale = jnp.concatenate([s["logs"][0] for s in state])
    return box["out"].reshape(STEPS, seqs, 1, 1, piece), log_scale


def shards(transition, emission, start):
    sizes = [lax.axis_size(name) for name in ("state", "dp", "sub")]
    if sizes == [4, 2, 2] and start.shape[0] == HALVES * 128 and start.shape[3] % CHUNK == 0:
        return fast(transition, emission, start)
    return general(transition, emission, start)


def solution(mesh):
    in_specs = (
        P(None, "state", None, ("dp", "sub")),
        P(None, "groups", ("dp", "sub"), None, None),
        P("groups", ("dp", "sub"), "state", None),
    )
    out_specs = (P(None, "groups", ("dp", "sub"), "state", None), P("groups"))
    return jax.shard_map(shards, mesh=mesh, in_specs=in_specs, out_specs=out_specs, check_vma=False)
```

```python
import functools

import jax
import jax.numpy as jnp
from jax import lax
from jax.experimental import pallas as pl
from jax.experimental.pallas import tpu as pltpu
from jax.sharding import PartitionSpec as P

STEPS = 4
HALVES = 2
TOP = 60000.0
START_TOP = 10.0


def product_kernel(num_x, with_peak, idx_ref, *refs):
    x_refs, t_ref, out_ref = refs[:num_x], refs[num_x], refs[num_x + 1]
    depth = x_refs[0].shape[1]
    total = None
    for q in range(num_x):
        rows = pl.ds(pl.multiple_of(idx_ref[1 + q] * depth, depth), depth)
        term = jnp.dot(x_refs[q][...], t_ref[rows, :], preferred_element_type=jnp.float32)
        total = term if total is None else total + term
    out_ref[0] = total
    if with_peak:
        peak_ref = refs[num_x + 2]
        here = jnp.max(t_ref[...].astype(jnp.float32).reshape(-1, 8, t_ref.shape[1]), axis=0)
        first = jnp.logical_and(pl.program_id(0) == 0, pl.program_id(1) == 0)

        @pl.when(first)
        def _():
            peak_ref[...] = here

        @pl.when(jnp.logical_not(first))
        def _():
            peak_ref[...] = jnp.maximum(peak_ref[...], here)


def product(indices, xs, table, blocks, with_peak):
    seqs, depth = xs[0].shape
    rows, width = table.shape
    piece = width // blocks
    tile = min(512, piece)
    per = piece // tile

    def place(o, c, idx):
        return (0, lax.rem(idx[0] + o, blocks) * per + c)

    out_shape = [jax.ShapeDtypeStruct((blocks, seqs, piece), jnp.float32)]
    out_specs = [pl.BlockSpec((1, seqs, tile), lambda o, c, idx: (o, 0, c))]
    if with_peak:
        out_shape.append(jax.ShapeDtypeStruct((8, tile), jnp.float32))
        out_specs.append(pl.BlockSpec((8, tile), lambda o, c, idx: (0, 0)))
    return pl.pallas_call(
        functools.partial(product_kernel, len(xs), with_peak),
        grid_spec=pltpu.PrefetchScalarGridSpec(
            num_scalar_prefetch=1,
            grid=(blocks, per),
            in_specs=[pl.BlockSpec((seqs, depth), lambda o, c, idx: (0, 0)) for _ in xs]
            + [pl.BlockSpec((rows, tile), place)],
            out_specs=out_specs,
        ),
        out_shape=out_shape,
        compiler_params=pltpu.CompilerParams(vmem_limit_bytes=32 * 2**20),
        cost_estimate=pl.CostEstimate(
            flops=2 * seqs * rows * width, bytes_accessed=2 * rows * width, transcendentals=0
        ),
        name="product_peak" if with_peak else "product",
    )(indices, *xs, table)


def gather_blocks(block):
    dp, sub = lax.axis_size("dp"), lax.axis_size("sub")
    found = [block]
    for k in range(1, dp):
        found.append(lax.ppermute(block, "dp", [(i, (i + k) % dp) for i in range(dp)]))
    out = []
    for l in range(sub):
        for item in found:
            out.append(item if l == 0 else lax.ppermute(item, "sub", [(i, (i + l) % sub) for i in range(sub)]))
    return out


def block_owners():
    dp, sub = lax.axis_size("dp"), lax.axis_size("sub")
    x, c = lax.axis_index("dp"), lax.axis_index("sub")
    return [
        lax.rem(x + dp - k, dp) * sub + lax.rem(c + sub - l, sub) for l in range(sub) for k in range(dp)
    ]


def line_sum(parts, into, back, first_into, first_back_r, first_back_l):
    n = lax.axis_size("state")
    right = left = None
    for k in range(1, n):
        scale = first_into if k == 1 else into
        to_r, to_l = parts[n - k], parts[k]
        if k > 1:
            to_r = to_r + right.astype(jnp.float32) * (first_back_r if k == 2 else back)
            to_l = to_l + left.astype(jnp.float32) * (first_back_l if k == 2 else back)
        right = lax.ppermute((to_r * scale).astype(jnp.float16), "state", [(i, i + 1) for i in range(k)])
        left = lax.ppermute((to_l * scale).astype(jnp.float16), "state", [(i, i - 1) for i in range(n - k, n)])
    last_r, last_l = (first_back_r, first_back_l) if n == 2 else (back, back)
    return parts[0] + right.astype(jnp.float32) * last_r + left.astype(jnp.float32) * last_l


def general(transition, emission, start):
    seq_count = start.shape[0]
    piece = start.shape[3]
    blocks = lax.axis_size("state")
    me = lax.axis_index("state")
    table = transition.reshape(transition.shape[0] * piece, transition.shape[3])
    hidden = blocks * piece * lax.axis_size("dp") * lax.axis_size("sub")
    half = seq_count // HALVES
    indices = jnp.stack([me] + block_owners()).astype(jnp.int32)
    weights = jnp.transpose(emission[:, :, 0], (0, 2, 1, 3))
    weights = jnp.concatenate([weights, weights], axis=1)
    weights = lax.dynamic_slice_in_dim(weights, me, blocks, 1)

    messages = [start[h * half : (h + 1) * half, 0, 0] for h in range(HALVES)]
    history, normals = [], []
    into = back = None
    for step in range(STEPS):
        step_messages, step_normals = [], []
        for h in range(HALVES):
            rows = slice(h * half, (h + 1) * half)
            xs = gather_blocks(messages[h].astype(jnp.bfloat16))
            first = step == 0 and h == 0
            if first:
                parts, peak = product(indices, xs, table, blocks, True)
                own_peak = jnp.max(peak)
                peaks = lax.all_gather(jnp.full((1, 128), own_peak), "state", axis=0, tiled=True)[:, 0]
                top_peak = jnp.max(peaks)
                into = TOP / (hidden * top_peak)
                back = hidden * top_peak / TOP
                peak_r = lax.dynamic_index_in_dim(peaks, lax.rem(me + blocks - 1, blocks), 0, False)
                peak_l = lax.dynamic_index_in_dim(peaks, lax.rem(me + 1, blocks), 0, False)
                spread = hidden * START_TOP
                scales = (
                    into / START_TOP, back * START_TOP,
                    TOP / (spread * own_peak), spread * peak_r / TOP, spread * peak_l / TOP,
                )
            else:
                (parts,) = product(indices, xs, table, blocks, False)
                grow = START_TOP if step == 0 else 1.0
                scales = (into / grow, back * grow, into / grow, back * grow, back * grow)
            step_weights = weights[step, :, rows].astype(jnp.float32)
            own_sum = jnp.sum(parts * step_weights, axis=(0, 2))
            sums = lax.all_gather(own_sum[None], ("state", "dp", "sub"), axis=0, tiled=True)
            normal = jnp.sum(sums, axis=0) / hidden
            summed = line_sum([parts[o] for o in range(blocks)], *scales)
            message = summed * step_weights[0] / normal[:, None]
            messages[h] = message
            step_messages.append(message)
            step_normals.append(normal)
        history.append(jnp.concatenate(step_messages, axis=0))
        normals.append(jnp.concatenate(step_normals, axis=0))
    log_scale = functools.reduce(lambda a, b: a + b, [jnp.log(x) for x in normals])
    out = jnp.stack(history).reshape(STEPS, seq_count, 1, 1, piece)
    return out, log_scale


SLOTS = ((3, 2, 1, 0), (0, 2, 3, 1), (3, 1, 0, 2), (0, 1, 2, 3))
PAIRS = [(0, 1), (1, 0), (2, 3), (3, 2)]
FROM_OUTER = [(0, 2), (3, 1)]
FROM_INNER = [(1, 2), (2, 1)]
LAST = [(1, 3), (2, 0), (0, 1), (3, 2)]
CHUNK = 512
VMEM = pl.BlockSpec(memory_space=pltpu.VMEM)
SMEM = pl.BlockSpec(memory_space=pltpu.SMEM)
ANY = pl.BlockSpec(memory_space=pl.ANY)
F32, BF16 = jnp.float32, jnp.bfloat16


def shape(dims, dtype):
    return jax.ShapeDtypeStruct(dims, dtype)


class Order:
    def __init__(self):
        self.last = None

    def __call__(self, body, outs, out_specs, args, specs, scratch=(), aliases=None, name=None):
        count = len(args)
        if self.last is not None:
            args, specs = [*args, self.last], [*specs, ANY]
        extra = len(args) - count

        def run(*refs):
            body(*refs[:count], *refs[count + extra :])

        result = pl.pallas_call(
            run,
            out_shape=tuple(outs),
            in_specs=list(specs),
            out_specs=tuple(out_specs),
            scratch_shapes=list(scratch),
            input_output_aliases=aliases or {},
            compiler_params=pltpu.CompilerParams(vmem_limit_bytes=12 * 2**20),
            cost_estimate=pl.CostEstimate(flops=0, bytes_accessed=1024, transcendentals=0),
            name=name,
        )(*args)
        self.last = result[0]
        return result


def encode(x):
    x = x * x
    x = x * x
    return (x * x).astype(BF16)


def decode(y):
    y = y.astype(F32)
    return jnp.where(y > 0.0, jnp.exp2(0.125 * jnp.log2(y)), 0.0)


def load_body(table_ref, held_ref, peak_ref, sems):
    count = sems.shape[0]
    rows = table_ref.shape[0] // count
    copies = [
        pltpu.make_async_copy(table_ref.at[pl.ds(i * rows, rows)], held_ref.at[pl.ds(i * rows, rows)], sems.at[i])
        for i in range(count)
    ]
    for copy in copies:
        copy.start()
    top = jnp.zeros((16, table_ref.shape[1]), BF16)
    for i, copy in enumerate(copies):
        copy.wait()

        def step(k, best, i=i):
            at = pl.multiple_of(i * rows + k * 16, 16)
            return jnp.maximum(best, held_ref[pl.ds(at, 16), :])

        top = lax.fori_loop(0, rows // 16, step, top)
    peak_ref[...] = jnp.full(peak_ref.shape, jnp.max(top.astype(F32)), F32)


def corner(ref):
    return ref[0:1, 0:1]


def top_of(peaks):
    return jnp.maximum(
        jnp.maximum(corner(peaks[0]), corner(peaks[1])), jnp.maximum(corner(peaks[2]), corner(peaks[3]))
    )


def all_swaps(tile, axes):
    return [tile] + [lax.ppermute(tile, axes, [(i, i ^ k) for i in range(4)]) for k in range(1, 4)]


def products(idx, slot, left_ref, table_ref, weights_ref, sums_ref, arrive, put):
    piece = weights_ref.shape[1]
    for c in range(piece // CHUNK):
        here = slice(c * CHUNK, (c + 1) * CHUNK)
        cols = pl.ds(pl.multiple_of(idx[slot] * piece + c * CHUNK, CHUNK), CHUNK)
        total = jnp.dot(left_ref[...], table_ref[:, cols], preferred_element_type=F32)
        put(here, total)
        if c == 0:
            arrive.wait()
        weighted = total * weights_ref[:, here].astype(F32)
        sums = sums_ref[...]
        for k in range(CHUNK // 128):
            sums = sums + weighted[:, k * 128 : (k + 1) * 128]
        sums_ref[...] = sums


def fetch_weights(idx, slots, step, at, weights_ref, held, sems):
    half = held.shape[1]
    copies = [
        pltpu.make_async_copy(weights_ref.at[step, idx[s], pl.ds(at, half)], held.at[k], sems.at[k])
        for k, s in enumerate(slots)
    ]
    for copy in copies:
        copy.start()
    return copies


def first_body(step, at, spread, extra, idx, x0, x1, x2, x3, table_ref, weights_ref, *refs):
    refs = refs[extra:]
    peaks, (out0_ref, out1_ref, sums_ref, left_ref, held, sems) = refs[:-6], refs[-6:]
    copies = fetch_weights(idx, (0, 1), step, at, weights_ref, held, sems)
    depth = x0.shape[1]
    for q, x in enumerate((x0, x1, x2, x3)):
        left_ref[:, pl.ds(pl.multiple_of(idx[4 + q] * depth, depth), depth)] = x[...]
    scale = (TOP / spread) / (corner(peaks[0]) if step == 0 else top_of(peaks))
    sums_ref[...] = jnp.zeros_like(sums_ref)
    for slot, out_ref in enumerate((out0_ref, out1_ref)):
        def put(here, total, out_ref=out_ref):
            out_ref[:, here] = encode(total * scale)

        products(idx, slot, left_ref, table_ref, held.at[slot], sums_ref, copies[slot], put)


def rest_body(step, at, write, has_out, extra, idx, left_ref, sums_in, table_ref, weights_ref, *refs):
    refs = refs[extra:]
    if write is not None:
        message_ref, refs = refs[0], refs[2 if has_out else 1 :]
    (part_ref, own_ref, tile_ref, own_weights_ref), refs = refs[:4], refs[4:]
    if write is not None:
        out_ref, refs = refs[0], refs[1:]
    sums_ref, held, sems = refs
    if write is not None:
        copy_out = pltpu.make_async_copy(message_ref, out_ref.at[write[0], pl.ds(write[1], message_ref.shape[0])], sems.at[2])
        copy_out.start()
    copies = fetch_weights(idx, (2, 3), step, at, weights_ref, held, sems)
    sums_ref[...] = sums_in[...]
    for k, out in enumerate((part_ref, own_ref)):
        def put(here, total, out=out):
            out[:, here] = total

        products(idx, 2 + k, left_ref, table_ref, held.at[k], sums_ref, copies[k], put)
    own_weights_ref[...] = held[1]
    tile_ref[...] = jnp.broadcast_to(jnp.sum(sums_ref[...].T, axis=0, keepdims=True), tile_ref.shape)
    if write is not None:
        copy_out.wait()


def add_body(a_ref, b_ref, table_ref, *refs):
    refs[-1][...] = a_ref[...] + b_ref[...]


def far_body(step, spread, forward, extra, idx, part_ref, pair_ref, table_ref, *refs):
    peaks, refs = refs[:4], refs[4 + extra :]
    if forward:
        refs[2][...] = refs[0][...]
        refs = refs[1:]
    out = refs[0]
    top = top_of(peaks)
    scale = (TOP / spread) / top

    @pl.when(idx[8] == 1)
    def _():
        pair = decode(pair_ref[...])
        if step == 0:
            pair = pair * (corner(peaks[1]) / top)
        out[...] = encode(part_ref[...] * scale + pair)

    @pl.when(idx[8] == 0)
    def _():
        out[...] = encode(part_ref[...] * scale)


def last_body(step, spread, hidden, finish, count, idx, own_ref, pair_ref, outer_ref, inner_ref, far_ref, weights_ref, table_ref, *refs):
    tiles, refs = [ref[...] for ref in refs[:count]], refs[count:]
    peaks, logs_in, refs = refs[:4], refs[4] if step else None, refs[5 if step else 4 :]
    if finish is not None:
        refs = refs[1:]
    lowered_ref, message_ref, logs_ref = refs[:3]
    if finish is not None:
        out_ref, mixed_ref, sem = refs[3:]
    else:
        (mixed_ref,) = refs[3:]
    half = own_ref.shape[0]
    top = top_of(peaks)
    unscale = top * (spread / TOP)
    total = tiles[0] + tiles[1]
    if count == 4:
        total = total + (tiles[2] + tiles[3])
    normal = total / hidden
    logs = jnp.log(normal)
    logs_ref[...] = logs if logs_in is None else logs_in[...] + logs
    inverse = jnp.broadcast_to(1.0 / normal[0:1, :], (half, half)).T

    def sent_by(k):
        return corner(peaks[k]) * (spread / TOP) if step == 0 else unscale

    @pl.when(idx[8] == 1)
    def _():
        mixed_ref[...] = (
            own_ref[...]
            + (decode(outer_ref[...]) * sent_by(2) + decode(inner_ref[...]) * sent_by(3))
            + decode(far_ref[...]) * unscale
        )

    @pl.when(idx[8] == 0)
    def _():
        mixed_ref[...] = own_ref[...] + (decode(pair_ref[...]) * sent_by(1) + decode(far_ref[...]) * unscale)

    for k in range(own_ref.shape[1] // 128):
        here = slice(k * 128, (k + 1) * 128)
        message = mixed_ref[:, here] * weights_ref[:, here].astype(F32) * inverse
        lowered_ref[:, here] = message.astype(BF16)
        message_ref[:, k, :] = message
    if finish is not None:
        write = pltpu.make_async_copy(message_ref, out_ref.at[finish[0], pl.ds(finish[1], half)], sem)
        write.start()
        write.wait()


def fast(transition, emission, start):
    seqs, piece = start.shape[0], start.shape[3]
    hidden = 16 * piece
    half = seqs // HALVES
    table = transition.reshape(4 * piece, 4 * piece)
    me = lax.axis_index("state")
    d = lax.axis_index("dp") * 2 + lax.axis_index("sub")
    slots = jnp.asarray(SLOTS, jnp.int32)[me]
    inner = jnp.logical_and(me > 0, me < 3)
    idx = jnp.concatenate([slots, jnp.stack([d, d ^ 1, d ^ 2, d ^ 3, inner]).astype(jnp.int32)])
    weights = jnp.transpose(emission[:, :, 0], (0, 2, 1, 3))
    wide, code = shape((half, piece), F32), shape((half, piece), BF16)
    square, tile = shape((half, 128), F32), shape((8, 128), F32)
    rows = shape((half, piece // 128, 128), F32)
    out_shape = shape((STEPS, seqs, piece // 128, 128), F32)
    dma = pltpu.SemaphoreType.DMA
    order = Order()

    table, weights, idx = lax.optimization_barrier((table, weights, idx))
    weights = pltpu.with_memory_space_constraint(weights, pltpu.HBM)
    held, peak = order(
        load_body, [pltpu.VMEM(table.shape, table.dtype), shape((8, 128), F32)], [VMEM] * 2, [table], [ANY],
        [dma((8,))], name="load_table",
    )
    order.last = peak
    held = pltpu.with_memory_space_constraint(held, pltpu.VMEM)
    peaks = all_swaps(peak, "state")

    spreads = [hidden * 1.01 * (START_TOP if step == 0 else 1.0) for step in range(STEPS)]
    state = [{"lowered": start[h * half : (h + 1) * half, 0, 0].astype(BF16)} for h in range(HALVES)]
    box = {"out": None}

    def swap(h, axis, k):
        s = state[h]
        s["their"] = lax.ppermute(s["tile"], axis, [(i, i ^ k) for i in range(lax.axis_size(axis))])

    def add(h, after=()):
        s = state[h]
        s["tile"] = order(
            add_body, [tile], [VMEM], [s["tile"], s["their"], held, *after], [VMEM] * 3 + [ANY] * len(after),
            name="add_sums",
        )[0]

    def gather(h):
        s = state[h]
        own = s["lowered"]
        s["across"] = lax.ppermute(own, "dp", [(0, 1), (1, 0)])
        s["xs"] = [own, lax.ppermute(own, "sub", [(0, 1), (1, 0)])]

    def gather_rest(h, across):
        state[h]["xs"] += [across, lax.ppermute(across, "sub", [(0, 1), (1, 0)])]

    def begin(step, h):
        s, at, spread = state[h], h * half, spreads[step]
        used = [peak] if step == 0 else peaks
        after = state[1]["xs"][2:] if step == h == 0 else []
        send0, send1, sums, left = order(
            functools.partial(first_body, step, at, spread, len(after)),
            [code, code, square, shape((half, 4 * piece), BF16)], [VMEM] * 4,
            [idx, *s["xs"], held, weights, *after, *used],
            [SMEM] + [VMEM] * 5 + [ANY] * (1 + len(after)) + [VMEM] * len(used),
            [pltpu.VMEM((2, half, piece), BF16), dma((2,))], name="product_first",
        )
        ends = step == STEPS - 1 and h == 1
        if "tile" in state[1 - h] and not ends:
            add(1 - h, [state[1 - h]["far"]])
            swap(1 - h, "sub", 1)
        s["pair"] = lax.ppermute(send0, "state", PAIRS)
        if ends:
            s["send1"] = send1
        else:
            s["outer"] = lax.ppermute(send1, "state", FROM_OUTER)
            s["inner"] = lax.ppermute(send1, "state", FROM_INNER)
        s["left"], s["sums"] = left, sums

    def proceed(step, h, forward, message=None, place=None):
        s, at = state[h], h * half
        args = [idx, s["left"], s["sums"], held, weights]
        after = [state[0]["far"]] if step == STEPS - 1 and h == 1 else []
        args, specs = args + after, [SMEM] + [VMEM] * 3 + [ANY] * (1 + len(after))
        outs, out_specs, aliases = [wide, wide, tile, code], [VMEM] * 4, None
        has_out = box["out"] is not None
        if place is not None:
            args, specs = args + [message], specs + [VMEM]
            outs, out_specs = outs + [out_shape], out_specs + [ANY]
            if has_out:
                aliases = {len(args): 4}
                args, specs = args + [box["out"]], specs + [ANY]
        result = order(
            functools.partial(rest_body, step, at, place, has_out, len(after)), outs, out_specs, args, specs,
            [pltpu.VMEM((half, 128), F32), pltpu.VMEM((2, half, piece), BF16), dma((3,))], aliases,
            name="product_rest",
        )
        part, s["own"], s["tile"], s["weights"] = result[:4]
        if place is not None:
            box["out"] = result[4]
        swap(h, "state", 1)
        ends = step == STEPS - 1 and h == 1
        args = [idx, part, s["pair"], held, *peaks]
        if ends:
            args.append(s["their"])
        specs = [SMEM] + [VMEM] * 7 + [ANY] * ends
        if forward or ends:
            args, specs = args + [s["send1"] if ends else state[1 - h]["across"]], specs + [VMEM]
        count = 2 if forward or ends else 1
        result = order(
            functools.partial(far_body, step, spreads[step], forward or ends, int(ends)), [code] * count, [VMEM] * count,
            args, specs, name="far_block",
        )
        if ends:
            add(h)
            swap(h, "state", 2)
            s["far"] = lax.ppermute(result[0], "state", LAST)
            s["outer"] = lax.ppermute(result[1], "state", FROM_OUTER)
            s["inner"] = lax.ppermute(result[1], "state", FROM_INNER)
            return
        if forward:
            gather_rest(1 - h, result[1])
        s["far"] = lax.ppermute(result[0], "state", LAST)
        add(h, [s["outer"]])
        swap(h, "dp", 1)
        add(h, [s["inner"]])
        swap(h, "state", 2)
        if step == STEPS - 1:
            add(h)
            swap(h, "sub", 1)

    def finish(step, h):
        s = state[h]
        args = [idx, s["own"], s["pair"], s["outer"], s["inner"], s["far"], s["weights"], held]
        tiles = s.get("tiles") or [s["tile"], s["their"]]
        args += [*tiles, *peaks]
        specs = [SMEM] + [VMEM] * (len(args) - 1)
        if step:
            args, specs = args + [s["logs"]], specs + [VMEM]
        outs, out_specs, aliases, place = [code, rows, tile], [VMEM] * 3, None, None
        scratch = [pltpu.VMEM((half, piece), F32)]
        if step == STEPS - 1:
            place = (step, h * half)
            aliases = {len(args): 3}
            args, specs = args + [box["out"]], specs + [ANY]
            outs, out_specs, scratch = outs + [out_shape], out_specs + [ANY], scratch + [dma]
        result = order(
            functools.partial(last_body, step, spreads[step], hidden, place, len(tiles)), outs, out_specs, args, specs,
            scratch, aliases, name="normalise",
        )
        s["lowered"], s["message"], s["logs"] = result[:3]
        if place is not None:
            box["out"] = result[3]

    for s in state:
        own = s["lowered"]
        s["xs"] = [own] + [lax.ppermute(own, ("dp", "sub"), [(i, i ^ k) for i in range(4)]) for k in (1, 2, 3)]
    for step in range(STEPS):
        begin(step, 0)
        if step:
            finish(step - 1, 1)
            gather(1)
            proceed(step, 0, True, state[1]["message"], (step - 1, half))
        else:
            proceed(step, 0, False)
        begin(step, 1)
        if step < STEPS - 1:
            finish(step, 0)
            gather(0)
            proceed(step, 1, True, state[0]["message"], (step, 0))
        else:
            proceed(step, 1, False)
            finish(step, 0)
    add(1)
    state[1]["tiles"] = all_swaps(state[1]["tile"], ("dp", "sub"))
    finish(STEPS - 1, 1)
    log_scale = jnp.concatenate([s["logs"][0] for s in state])
    return box["out"].reshape(STEPS, seqs, 1, 1, piece), log_scale


def shards(transition, emission, start):
    sizes = [lax.axis_size(name) for name in ("state", "dp", "sub")]
    if sizes == [4, 2, 2] and start.shape[0] == HALVES * 128 and start.shape[3] % CHUNK == 0:
        return fast(transition, emission, start)
    return general(transition, emission, start)


def solution(mesh):
    in_specs = (
        P(None, "state", None, ("dp", "sub")),
        P(None, "groups", ("dp", "sub"), None, None),
        P("groups", ("dp", "sub"), "state", None),
    )
    out_specs = (P(None, "groups", ("dp", "sub"), "state", None), P("groups"))
    return jax.shard_map(shards, mesh=mesh, in_specs=in_specs, out_specs=out_specs, check_vma=False)
```

```python
import functools

import jax
import jax.numpy as jnp
from jax import lax
from jax.experimental import pallas as pl
from jax.experimental.pallas import tpu as pltpu
from jax.sharding import PartitionSpec as P

STEPS = 4
HALVES = 2
TOP = 60000.0
START_TOP = 10.0


def product_kernel(num_x, with_peak, idx_ref, *refs):
    x_refs, t_ref, out_ref = refs[:num_x], refs[num_x], refs[num_x + 1]
    depth = x_refs[0].shape[1]
    total = None
    for q in range(num_x):
        rows = pl.ds(pl.multiple_of(idx_ref[1 + q] * depth, depth), depth)
        term = jnp.dot(x_refs[q][...], t_ref[rows, :], preferred_element_type=jnp.float32)
        total = term if total is None else total + term
    out_ref[0] = total
    if with_peak:
        peak_ref = refs[num_x + 2]
        here = jnp.max(t_ref[...].astype(jnp.float32).reshape(-1, 8, t_ref.shape[1]), axis=0)
        first = jnp.logical_and(pl.program_id(0) == 0, pl.program_id(1) == 0)

        @pl.when(first)
        def _():
            peak_ref[...] = here

        @pl.when(jnp.logical_not(first))
        def _():
            peak_ref[...] = jnp.maximum(peak_ref[...], here)


def product(indices, xs, table, blocks, with_peak):
    seqs, depth = xs[0].shape
    rows, width = table.shape
    piece = width // blocks
    tile = min(512, piece)
    per = piece // tile

    def place(o, c, idx):
        return (0, lax.rem(idx[0] + o, blocks) * per + c)

    out_shape = [jax.ShapeDtypeStruct((blocks, seqs, piece), jnp.float32)]
    out_specs = [pl.BlockSpec((1, seqs, tile), lambda o, c, idx: (o, 0, c))]
    if with_peak:
        out_shape.append(jax.ShapeDtypeStruct((8, tile), jnp.float32))
        out_specs.append(pl.BlockSpec((8, tile), lambda o, c, idx: (0, 0)))
    return pl.pallas_call(
        functools.partial(product_kernel, len(xs), with_peak),
        grid_spec=pltpu.PrefetchScalarGridSpec(
            num_scalar_prefetch=1,
            grid=(blocks, per),
            in_specs=[pl.BlockSpec((seqs, depth), lambda o, c, idx: (0, 0)) for _ in xs]
            + [pl.BlockSpec((rows, tile), place)],
            out_specs=out_specs,
        ),
        out_shape=out_shape,
        compiler_params=pltpu.CompilerParams(vmem_limit_bytes=32 * 2**20),
        cost_estimate=pl.CostEstimate(
            flops=2 * seqs * rows * width, bytes_accessed=2 * rows * width, transcendentals=0
        ),
        name="product_peak" if with_peak else "product",
    )(indices, *xs, table)


def gather_blocks(block):
    dp, sub = lax.axis_size("dp"), lax.axis_size("sub")
    found = [block]
    for k in range(1, dp):
        found.append(lax.ppermute(block, "dp", [(i, (i + k) % dp) for i in range(dp)]))
    out = []
    for l in range(sub):
        for item in found:
            out.append(item if l == 0 else lax.ppermute(item, "sub", [(i, (i + l) % sub) for i in range(sub)]))
    return out


def block_owners():
    dp, sub = lax.axis_size("dp"), lax.axis_size("sub")
    x, c = lax.axis_index("dp"), lax.axis_index("sub")
    return [
        lax.rem(x + dp - k, dp) * sub + lax.rem(c + sub - l, sub) for l in range(sub) for k in range(dp)
    ]


def line_sum(parts, into, back, first_into, first_back_r, first_back_l):
    n = lax.axis_size("state")
    right = left = None
    for k in range(1, n):
        scale = first_into if k == 1 else into
        to_r, to_l = parts[n - k], parts[k]
        if k > 1:
            to_r = to_r + right.astype(jnp.float32) * (first_back_r if k == 2 else back)
            to_l = to_l + left.astype(jnp.float32) * (first_back_l if k == 2 else back)
        right = lax.ppermute((to_r * scale).astype(jnp.float16), "state", [(i, i + 1) for i in range(k)])
        left = lax.ppermute((to_l * scale).astype(jnp.float16), "state", [(i, i - 1) for i in range(n - k, n)])
    last_r, last_l = (first_back_r, first_back_l) if n == 2 else (back, back)
    return parts[0] + right.astype(jnp.float32) * last_r + left.astype(jnp.float32) * last_l


def general(transition, emission, start):
    seq_count = start.shape[0]
    piece = start.shape[3]
    blocks = lax.axis_size("state")
    me = lax.axis_index("state")
    table = transition.reshape(transition.shape[0] * piece, transition.shape[3])
    hidden = blocks * piece * lax.axis_size("dp") * lax.axis_size("sub")
    half = seq_count // HALVES
    indices = jnp.stack([me] + block_owners()).astype(jnp.int32)
    weights = jnp.transpose(emission[:, :, 0], (0, 2, 1, 3))
    weights = jnp.concatenate([weights, weights], axis=1)
    weights = lax.dynamic_slice_in_dim(weights, me, blocks, 1)

    messages = [start[h * half : (h + 1) * half, 0, 0] for h in range(HALVES)]
    history, normals = [], []
    into = back = None
    for step in range(STEPS):
        step_messages, step_normals = [], []
        for h in range(HALVES):
            rows = slice(h * half, (h + 1) * half)
            xs = gather_blocks(messages[h].astype(jnp.bfloat16))
            first = step == 0 and h == 0
            if first:
                parts, peak = product(indices, xs, table, blocks, True)
                own_peak = jnp.max(peak)
                peaks = lax.all_gather(jnp.full((1, 128), own_peak), "state", axis=0, tiled=True)[:, 0]
                top_peak = jnp.max(peaks)
                into = TOP / (hidden * top_peak)
                back = hidden * top_peak / TOP
                peak_r = lax.dynamic_index_in_dim(peaks, lax.rem(me + blocks - 1, blocks), 0, False)
                peak_l = lax.dynamic_index_in_dim(peaks, lax.rem(me + 1, blocks), 0, False)
                spread = hidden * START_TOP
                scales = (
                    into / START_TOP, back * START_TOP,
                    TOP / (spread * own_peak), spread * peak_r / TOP, spread * peak_l / TOP,
                )
            else:
                (parts,) = product(indices, xs, table, blocks, False)
                grow = START_TOP if step == 0 else 1.0
                scales = (into / grow, back * grow, into / grow, back * grow, back * grow)
            step_weights = weights[step, :, rows].astype(jnp.float32)
            own_sum = jnp.sum(parts * step_weights, axis=(0, 2))
            sums = lax.all_gather(own_sum[None], ("state", "dp", "sub"), axis=0, tiled=True)
            normal = jnp.sum(sums, axis=0) / hidden
            summed = line_sum([parts[o] for o in range(blocks)], *scales)
            message = summed * step_weights[0] / normal[:, None]
            messages[h] = message
            step_messages.append(message)
            step_normals.append(normal)
        history.append(jnp.concatenate(step_messages, axis=0))
        normals.append(jnp.concatenate(step_normals, axis=0))
    log_scale = functools.reduce(lambda a, b: a + b, [jnp.log(x) for x in normals])
    out = jnp.stack(history).reshape(STEPS, seq_count, 1, 1, piece)
    return out, log_scale


SLOTS = ((3, 2, 1, 0), (0, 2, 3, 1), (3, 1, 0, 2), (0, 1, 2, 3))
PAIRS = [(0, 1), (1, 0), (2, 3), (3, 2)]
FROM_OUTER = [(0, 2), (3, 1)]
FROM_INNER = [(1, 2), (2, 1)]
LAST = [(1, 3), (2, 0), (0, 1), (3, 2)]
CHUNK = 512
VMEM = pl.BlockSpec(memory_space=pltpu.VMEM)
SMEM = pl.BlockSpec(memory_space=pltpu.SMEM)
ANY = pl.BlockSpec(memory_space=pl.ANY)
F32, BF16 = jnp.float32, jnp.bfloat16


def shape(dims, dtype):
    return jax.ShapeDtypeStruct(dims, dtype)


class Order:
    def __init__(self):
        self.last = None

    def __call__(self, body, outs, out_specs, args, specs, scratch=(), aliases=None, name=None):
        count = len(args)
        if self.last is not None:
            args, specs = [*args, self.last], [*specs, ANY]
        extra = len(args) - count

        def run(*refs):
            body(*refs[:count], *refs[count + extra :])

        result = pl.pallas_call(
            run,
            out_shape=tuple(outs),
            in_specs=list(specs),
            out_specs=tuple(out_specs),
            scratch_shapes=list(scratch),
            input_output_aliases=aliases or {},
            compiler_params=pltpu.CompilerParams(vmem_limit_bytes=12 * 2**20),
            cost_estimate=pl.CostEstimate(flops=0, bytes_accessed=1024, transcendentals=0),
            name=name,
        )(*args)
        self.last = result[0]
        return result


def encode(x):
    x = x * x
    x = x * x
    return (x * x).astype(BF16)


def decode(y):
    y = y.astype(F32)
    return jnp.where(y > 0.0, jnp.exp2(0.125 * jnp.log2(y)), 0.0)


def load_body(table_ref, held_ref, peak_ref, sems):
    count = sems.shape[0]
    rows = table_ref.shape[0] // count
    copies = [
        pltpu.make_async_copy(table_ref.at[pl.ds(i * rows, rows)], held_ref.at[pl.ds(i * rows, rows)], sems.at[i])
        for i in range(count)
    ]
    for copy in copies:
        copy.start()
    top = jnp.zeros((16, table_ref.shape[1]), BF16)
    for i, copy in enumerate(copies):
        copy.wait()

        def step(k, best, i=i):
            at = pl.multiple_of(i * rows + k * 16, 16)
            return jnp.maximum(best, held_ref[pl.ds(at, 16), :])

        top = lax.fori_loop(0, rows // 16, step, top)
    peak_ref[...] = jnp.full(peak_ref.shape, jnp.max(top.astype(F32)), F32)


def corner(ref):
    return ref[0:1, 0:1]


def top_of(peaks):
    return jnp.maximum(
        jnp.maximum(corner(peaks[0]), corner(peaks[1])), jnp.maximum(corner(peaks[2]), corner(peaks[3]))
    )


def all_swaps(tile, axes):
    return [tile] + [lax.ppermute(tile, axes, [(i, i ^ k) for i in range(4)]) for k in range(1, 4)]


def products(idx, slot, left_ref, table_ref, weights_ref, sums_ref, arrive, put):
    piece = weights_ref.shape[1]
    for c in range(piece // CHUNK):
        here = slice(c * CHUNK, (c + 1) * CHUNK)
        cols = pl.ds(pl.multiple_of(idx[slot] * piece + c * CHUNK, CHUNK), CHUNK)
        total = jnp.dot(left_ref[...], table_ref[:, cols], preferred_element_type=F32)
        put(here, total)
        if c == 0:
            arrive.wait()
        weighted = total * weights_ref[:, here].astype(F32)
        sums = sums_ref[...]
        for k in range(CHUNK // 128):
            sums = sums + weighted[:, k * 128 : (k + 1) * 128]
        sums_ref[...] = sums


def fetch_weights(idx, slots, step, at, weights_ref, held, sems):
    half = held.shape[1]
    copies = [
        pltpu.make_async_copy(weights_ref.at[step, idx[s], pl.ds(at, half)], held.at[k], sems.at[k])
        for k, s in enumerate(slots)
    ]
    for copy in copies:
        copy.start()
    return copies


def first_body(step, at, spread, extra, idx, x0, x1, x2, x3, table_ref, weights_ref, *refs):
    refs = refs[extra:]
    peaks, (out0_ref, out1_ref, sums_ref, left_ref, held, sems) = refs[:-6], refs[-6:]
    copies = fetch_weights(idx, (0, 1), step, at, weights_ref, held, sems)
    depth = x0.shape[1]
    for q, x in enumerate((x0, x1, x2, x3)):
        left_ref[:, pl.ds(pl.multiple_of(idx[4 + q] * depth, depth), depth)] = x[...]
    scale = (TOP / spread) / (corner(peaks[0]) if step == 0 else top_of(peaks))
    sums_ref[...] = jnp.zeros_like(sums_ref)
    for slot, out_ref in enumerate((out0_ref, out1_ref)):
        def put(here, total, out_ref=out_ref):
            out_ref[:, here] = encode(total * scale)

        products(idx, slot, left_ref, table_ref, held.at[slot], sums_ref, copies[slot], put)


def rest_body(step, at, write, has_out, extra, idx, left_ref, sums_in, table_ref, weights_ref, *refs):
    refs = refs[extra:]
    if write is not None:
        message_ref, refs = refs[0], refs[2 if has_out else 1 :]
    (part_ref, own_ref, tile_ref, own_weights_ref), refs = refs[:4], refs[4:]
    if write is not None:
        out_ref, refs = refs[0], refs[1:]
    sums_ref, held, sems = refs
    if write is not None:
        copy_out = pltpu.make_async_copy(message_ref, out_ref.at[write[0], pl.ds(write[1], message_ref.shape[0])], sems.at[2])
        copy_out.start()
    copies = fetch_weights(idx, (2, 3), step, at, weights_ref, held, sems)
    sums_ref[...] = sums_in[...]
    for k, out in enumerate((part_ref, own_ref)):
        def put(here, total, out=out):
            out[:, here] = total

        products(idx, 2 + k, left_ref, table_ref, held.at[k], sums_ref, copies[k], put)
    own_weights_ref[...] = held[1]
    tile_ref[...] = jnp.broadcast_to(jnp.sum(sums_ref[...].T, axis=0, keepdims=True), tile_ref.shape)
    if write is not None:
        copy_out.wait()


def add_body(a_ref, b_ref, table_ref, *refs):
    refs[-1][...] = a_ref[...] + b_ref[...]


def far_body(step, spread, forward, extra, idx, part_ref, pair_ref, table_ref, *refs):
    peaks, refs = refs[:4], refs[4 + extra :]
    if forward:
        refs[2][...] = refs[0][...]
        refs = refs[1:]
    out = refs[0]
    top = top_of(peaks)
    scale = (TOP / spread) / top

    @pl.when(idx[8] == 1)
    def _():
        pair = decode(pair_ref[...])
        if step == 0:
            pair = pair * (corner(peaks[1]) / top)
        out[...] = encode(part_ref[...] * scale + pair)

    @pl.when(idx[8] == 0)
    def _():
        out[...] = encode(part_ref[...] * scale)


def last_body(step, spread, hidden, finish, count, idx, own_ref, pair_ref, outer_ref, inner_ref, far_ref, weights_ref, table_ref, *refs):
    tiles, refs = [ref[...] for ref in refs[:count]], refs[count:]
    peaks, logs_in, refs = refs[:4], refs[4] if step else None, refs[5 if step else 4 :]
    if finish is not None:
        refs = refs[1:]
    lowered_ref, message_ref, logs_ref = refs[:3]
    if finish is not None:
        out_ref, mixed_ref, sem = refs[3:]
    else:
        (mixed_ref,) = refs[3:]
    half = own_ref.shape[0]
    top = top_of(peaks)
    unscale = top * (spread / TOP)
    total = tiles[0] + tiles[1]
    if count == 4:
        total = total + (tiles[2] + tiles[3])
    normal = total / hidden
    logs = jnp.log(normal)
    logs_ref[...] = logs if logs_in is None else logs_in[...] + logs
    inverse = jnp.broadcast_to(1.0 / normal[0:1, :], (half, half)).T

    def sent_by(k):
        return corner(peaks[k]) * (spread / TOP) if step == 0 else unscale

    @pl.when(idx[8] == 1)
    def _():
        mixed_ref[...] = (
            own_ref[...]
            + (decode(outer_ref[...]) * sent_by(2) + decode(inner_ref[...]) * sent_by(3))
            + decode(far_ref[...]) * unscale
        )

    @pl.when(idx[8] == 0)
    def _():
        mixed_ref[...] = own_ref[...] + (decode(pair_ref[...]) * sent_by(1) + decode(far_ref[...]) * unscale)

    for k in range(own_ref.shape[1] // 128):
        here = slice(k * 128, (k + 1) * 128)
        message = mixed_ref[:, here] * weights_ref[:, here].astype(F32) * inverse
        lowered_ref[:, here] = message.astype(BF16)
        message_ref[:, k, :] = message
    if finish is not None:
        write = pltpu.make_async_copy(message_ref, out_ref.at[finish[0], pl.ds(finish[1], half)], sem)
        write.start()
        write.wait()


def fast(transition, emission, start):
    seqs, piece = start.shape[0], start.shape[3]
    hidden = 16 * piece
    half = seqs // HALVES
    table = transition.reshape(4 * piece, 4 * piece)
    me = lax.axis_index("state")
    d = lax.axis_index("dp") * 2 + lax.axis_index("sub")
    slots = jnp.asarray(SLOTS, jnp.int32)[me]
    inner = jnp.logical_and(me > 0, me < 3)
    idx = jnp.concatenate([slots, jnp.stack([d, d ^ 1, d ^ 2, d ^ 3, inner]).astype(jnp.int32)])
    weights = jnp.transpose(emission[:, :, 0], (0, 2, 1, 3))
    wide, code = shape((half, piece), F32), shape((half, piece), BF16)
    square, tile = shape((half, 128), F32), shape((8, 128), F32)
    rows = shape((half, piece // 128, 128), F32)
    out_shape = shape((STEPS, seqs, piece // 128, 128), F32)
    dma = pltpu.SemaphoreType.DMA
    order = Order()

    table, weights, idx = lax.optimization_barrier((table, weights, idx))
    weights = pltpu.with_memory_space_constraint(weights, pltpu.HBM)
    held, peak = order(
        load_body, [pltpu.VMEM(table.shape, table.dtype), shape((8, 128), F32)], [VMEM] * 2, [table], [ANY],
        [dma((8,))], name="load_table",
    )
    order.last = peak
    held = pltpu.with_memory_space_constraint(held, pltpu.VMEM)
    peaks = all_swaps(peak, "state")

    spreads = [hidden * 1.01 * (START_TOP if step == 0 else 1.0) for step in range(STEPS)]
    state = [{"lowered": start[h * half : (h + 1) * half, 0, 0].astype(BF16)} for h in range(HALVES)]
    box = {"out": None}

    def swap(h, axis, k):
        s = state[h]
        s["their"] = lax.ppermute(s["tile"], axis, [(i, i ^ k) for i in range(lax.axis_size(axis))])

    def add(h, after=()):
        s = state[h]
        s["tile"] = order(
            add_body, [tile], [VMEM], [s["tile"], s["their"], held, *after], [VMEM] * 3 + [ANY] * len(after),
            name="add_sums",
        )[0]

    def gather(h):
        s = state[h]
        own = s["lowered"]
        s["across"] = lax.ppermute(own, "dp", [(0, 1), (1, 0)])
        s["xs"] = [own, lax.ppermute(own, "sub", [(0, 1), (1, 0)])]

    def gather_rest(h, across):
        state[h]["xs"] += [across, lax.ppermute(across, "sub", [(0, 1), (1, 0)])]

    def begin(step, h):
        s, at, spread = state[h], h * half, spreads[step]
        used = [peak] if step == 0 else peaks
        after = state[1]["xs"][2:] if step == h == 0 else []
        send0, send1, sums, left = order(
            functools.partial(first_body, step, at, spread, len(after)),
            [code, code, square, shape((half, 4 * piece), BF16)], [VMEM] * 4,
            [idx, *s["xs"], held, weights, *after, *used],
            [SMEM] + [VMEM] * 5 + [ANY] * (1 + len(after)) + [VMEM] * len(used),
            [pltpu.VMEM((2, half, piece), BF16), dma((2,))], name="product_first",
        )
        ends = step == STEPS - 1 and h == 1
        if "tile" in state[1 - h] and not ends:
            add(1 - h, [state[1 - h]["far"]])
            swap(1 - h, "sub", 1)
        s["pair"] = lax.ppermute(send0, "state", PAIRS)
        s["outer"] = lax.ppermute(send1, "state", FROM_OUTER)
        s["inner"] = lax.ppermute(send1, "state", FROM_INNER)
        s["left"], s["sums"] = left, sums

    def proceed(step, h, forward, message=None, place=None):
        s, at = state[h], h * half
        args = [idx, s["left"], s["sums"], held, weights]
        after = [state[0]["far"]] if step == STEPS - 1 and h == 1 else []
        args, specs = args + after, [SMEM] + [VMEM] * 3 + [ANY] * (1 + len(after))
        outs, out_specs, aliases = [wide, wide, tile, code], [VMEM] * 4, None
        has_out = box["out"] is not None
        if place is not None:
            args, specs = args + [message], specs + [VMEM]
            outs, out_specs = outs + [out_shape], out_specs + [ANY]
            if has_out:
                aliases = {len(args): 4}
                args, specs = args + [box["out"]], specs + [ANY]
        result = order(
            functools.partial(rest_body, step, at, place, has_out, len(after)), outs, out_specs, args, specs,
            [pltpu.VMEM((half, 128), F32), pltpu.VMEM((2, half, piece), BF16), dma((3,))], aliases,
            name="product_rest",
        )
        part, s["own"], s["tile"], s["weights"] = result[:4]
        if place is not None:
            box["out"] = result[4]
        swap(h, "state", 1)
        ends = step == STEPS - 1 and h == 1
        args = [idx, part, s["pair"], held, *peaks]
        after = [s["their"]] if ends or step == 0 else []
        args, specs = args + after, [SMEM] + [VMEM] * 7 + [ANY] * len(after)
        if forward:
            args, specs = args + [state[1 - h]["across"]], specs + [VMEM]
        count = 2 if forward else 1
        result = order(
            functools.partial(far_body, step, spreads[step], forward, len(after)), [code] * count, [VMEM] * count,
            args, specs, name="far_block",
        )
        if ends:
            s["far"] = lax.ppermute(result[0], "state", LAST)
            add(h)
            swap(h, "state", 2)
            return
        if forward:
            gather_rest(1 - h, result[1])
        s["far"] = lax.ppermute(result[0], "state", LAST)
        add(h, [s["outer"]])
        swap(h, "dp", 1)
        add(h, [s["inner"]])
        swap(h, "state", 2)
        if step == STEPS - 1:
            add(h)
            swap(h, "sub", 1)

    def finish(step, h):
        s = state[h]
        args = [idx, s["own"], s["pair"], s["outer"], s["inner"], s["far"], s["weights"], held]
        tiles = s.get("tiles") or [s["tile"], s["their"]]
        args += [*tiles, *peaks]
        specs = [SMEM] + [VMEM] * (len(args) - 1)
        if step:
            args, specs = args + [s["logs"]], specs + [VMEM]
        outs, out_specs, aliases, place = [code, rows, tile], [VMEM] * 3, None, None
        scratch = [pltpu.VMEM((half, piece), F32)]
        if step == STEPS - 1:
            place = (step, h * half)
            aliases = {len(args): 3}
            args, specs = args + [box["out"]], specs + [ANY]
            outs, out_specs, scratch = outs + [out_shape], out_specs + [ANY], scratch + [dma]
        result = order(
            functools.partial(last_body, step, spreads[step], hidden, place, len(tiles)), outs, out_specs, args, specs,
            scratch, aliases, name="normalise",
        )
        s["lowered"], s["message"], s["logs"] = result[:3]
        if place is not None:
            box["out"] = result[3]

    for s in state:
        own = s["lowered"]
        s["xs"] = [own] + [lax.ppermute(own, ("dp", "sub"), [(i, i ^ k) for i in range(4)]) for k in (1, 2, 3)]
    for step in range(STEPS):
        begin(step, 0)
        if step:
            finish(step - 1, 1)
            gather(1)
            proceed(step, 0, True, state[1]["message"], (step - 1, half))
        else:
            proceed(step, 0, False)
        begin(step, 1)
        if step < STEPS - 1:
            finish(step, 0)
            gather(0)
            proceed(step, 1, True, state[0]["message"], (step, 0))
        else:
            proceed(step, 1, False)
            finish(step, 0)
    add(1)
    state[1]["tiles"] = all_swaps(state[1]["tile"], ("dp", "sub"))
    finish(STEPS - 1, 1)
    log_scale = jnp.concatenate([s["logs"][0] for s in state])
    return box["out"].reshape(STEPS, seqs, 1, 1, piece), log_scale


def shards(transition, emission, start):
    sizes = [lax.axis_size(name) for name in ("state", "dp", "sub")]
    if sizes == [4, 2, 2] and start.shape[0] == HALVES * 128 and start.shape[3] % CHUNK == 0:
        return fast(transition, emission, start)
    return general(transition, emission, start)


def solution(mesh):
    in_specs = (
        P(None, "state", None, ("dp", "sub")),
        P(None, "groups", ("dp", "sub"), None, None),
        P("groups", ("dp", "sub"), "state", None),
    )
    out_specs = (P(None, "groups", ("dp", "sub"), "state", None), P("groups"))
    return jax.shard_map(shards, mesh=mesh, in_specs=in_specs, out_specs=out_specs, check_vma=False)
```

```python
import functools

import jax
import jax.numpy as jnp
from jax import lax
from jax.experimental import pallas as pl
from jax.experimental.pallas import tpu as pltpu
from jax.sharding import PartitionSpec as P

STEPS = 4
HALVES = 2
TOP = 60000.0
START_TOP = 10.0


def product_kernel(num_x, with_peak, idx_ref, *refs):
    x_refs, t_ref, out_ref = refs[:num_x], refs[num_x], refs[num_x + 1]
    depth = x_refs[0].shape[1]
    total = None
    for q in range(num_x):
        rows = pl.ds(pl.multiple_of(idx_ref[1 + q] * depth, depth), depth)
        term = jnp.dot(x_refs[q][...], t_ref[rows, :], preferred_element_type=jnp.float32)
        total = term if total is None else total + term
    out_ref[0] = total
    if with_peak:
        peak_ref = refs[num_x + 2]
        here = jnp.max(t_ref[...].astype(jnp.float32).reshape(-1, 8, t_ref.shape[1]), axis=0)
        first = jnp.logical_and(pl.program_id(0) == 0, pl.program_id(1) == 0)

        @pl.when(first)
        def _():
            peak_ref[...] = here

        @pl.when(jnp.logical_not(first))
        def _():
            peak_ref[...] = jnp.maximum(peak_ref[...], here)


def product(indices, xs, table, blocks, with_peak):
    seqs, depth = xs[0].shape
    rows, width = table.shape
    piece = width // blocks
    tile = min(512, piece)
    per = piece // tile

    def place(o, c, idx):
        return (0, lax.rem(idx[0] + o, blocks) * per + c)

    out_shape = [jax.ShapeDtypeStruct((blocks, seqs, piece), jnp.float32)]
    out_specs = [pl.BlockSpec((1, seqs, tile), lambda o, c, idx: (o, 0, c))]
    if with_peak:
        out_shape.append(jax.ShapeDtypeStruct((8, tile), jnp.float32))
        out_specs.append(pl.BlockSpec((8, tile), lambda o, c, idx: (0, 0)))
    return pl.pallas_call(
        functools.partial(product_kernel, len(xs), with_peak),
        grid_spec=pltpu.PrefetchScalarGridSpec(
            num_scalar_prefetch=1,
            grid=(blocks, per),
            in_specs=[pl.BlockSpec((seqs, depth), lambda o, c, idx: (0, 0)) for _ in xs]
            + [pl.BlockSpec((rows, tile), place)],
            out_specs=out_specs,
        ),
        out_shape=out_shape,
        compiler_params=pltpu.CompilerParams(vmem_limit_bytes=32 * 2**20),
        cost_estimate=pl.CostEstimate(
            flops=2 * seqs * rows * width, bytes_accessed=2 * rows * width, transcendentals=0
        ),
        name="product_peak" if with_peak else "product",
    )(indices, *xs, table)


def gather_blocks(block):
    dp, sub = lax.axis_size("dp"), lax.axis_size("sub")
    found = [block]
    for k in range(1, dp):
        found.append(lax.ppermute(block, "dp", [(i, (i + k) % dp) for i in range(dp)]))
    out = []
    for l in range(sub):
        for item in found:
            out.append(item if l == 0 else lax.ppermute(item, "sub", [(i, (i + l) % sub) for i in range(sub)]))
    return out


def block_owners():
    dp, sub = lax.axis_size("dp"), lax.axis_size("sub")
    x, c = lax.axis_index("dp"), lax.axis_index("sub")
    return [
        lax.rem(x + dp - k, dp) * sub + lax.rem(c + sub - l, sub) for l in range(sub) for k in range(dp)
    ]


def line_sum(parts, into, back, first_into, first_back_r, first_back_l):
    n = lax.axis_size("state")
    right = left = None
    for k in range(1, n):
        scale = first_into if k == 1 else into
        to_r, to_l = parts[n - k], parts[k]
        if k > 1:
            to_r = to_r + right.astype(jnp.float32) * (first_back_r if k == 2 else back)
            to_l = to_l + left.astype(jnp.float32) * (first_back_l if k == 2 else back)
        right = lax.ppermute((to_r * scale).astype(jnp.float16), "state", [(i, i + 1) for i in range(k)])
        left = lax.ppermute((to_l * scale).astype(jnp.float16), "state", [(i, i - 1) for i in range(n - k, n)])
    last_r, last_l = (first_back_r, first_back_l) if n == 2 else (back, back)
    return parts[0] + right.astype(jnp.float32) * last_r + left.astype(jnp.float32) * last_l


def general(transition, emission, start):
    seq_count = start.shape[0]
    piece = start.shape[3]
    blocks = lax.axis_size("state")
    me = lax.axis_index("state")
    table = transition.reshape(transition.shape[0] * piece, transition.shape[3])
    hidden = blocks * piece * lax.axis_size("dp") * lax.axis_size("sub")
    half = seq_count // HALVES
    indices = jnp.stack([me] + block_owners()).astype(jnp.int32)
    weights = jnp.transpose(emission[:, :, 0], (0, 2, 1, 3))
    weights = jnp.concatenate([weights, weights], axis=1)
    weights = lax.dynamic_slice_in_dim(weights, me, blocks, 1)

    messages = [start[h * half : (h + 1) * half, 0, 0] for h in range(HALVES)]
    history, normals = [], []
    into = back = None
    for step in range(STEPS):
        step_messages, step_normals = [], []
        for h in range(HALVES):
            rows = slice(h * half, (h + 1) * half)
            xs = gather_blocks(messages[h].astype(jnp.bfloat16))
            first = step == 0 and h == 0
            if first:
                parts, peak = product(indices, xs, table, blocks, True)
                own_peak = jnp.max(peak)
                peaks = lax.all_gather(jnp.full((1, 128), own_peak), "state", axis=0, tiled=True)[:, 0]
                top_peak = jnp.max(peaks)
                into = TOP / (hidden * top_peak)
                back = hidden * top_peak / TOP
                peak_r = lax.dynamic_index_in_dim(peaks, lax.rem(me + blocks - 1, blocks), 0, False)
                peak_l = lax.dynamic_index_in_dim(peaks, lax.rem(me + 1, blocks), 0, False)
                spread = hidden * START_TOP
                scales = (
                    into / START_TOP, back * START_TOP,
                    TOP / (spread * own_peak), spread * peak_r / TOP, spread * peak_l / TOP,
                )
            else:
                (parts,) = product(indices, xs, table, blocks, False)
                grow = START_TOP if step == 0 else 1.0
                scales = (into / grow, back * grow, into / grow, back * grow, back * grow)
            step_weights = weights[step, :, rows].astype(jnp.float32)
            own_sum = jnp.sum(parts * step_weights, axis=(0, 2))
            sums = lax.all_gather(own_sum[None], ("state", "dp", "sub"), axis=0, tiled=True)
            normal = jnp.sum(sums, axis=0) / hidden
            summed = line_sum([parts[o] for o in range(blocks)], *scales)
            message = summed * step_weights[0] / normal[:, None]
            messages[h] = message
            step_messages.append(message)
            step_normals.append(normal)
        history.append(jnp.concatenate(step_messages, axis=0))
        normals.append(jnp.concatenate(step_normals, axis=0))
    log_scale = functools.reduce(lambda a, b: a + b, [jnp.log(x) for x in normals])
    out = jnp.stack(history).reshape(STEPS, seq_count, 1, 1, piece)
    return out, log_scale


SLOTS = ((3, 2, 1, 0), (0, 2, 3, 1), (3, 1, 0, 2), (0, 1, 2, 3))
PAIRS = [(0, 1), (1, 0), (2, 3), (3, 2)]
FROM_OUTER = [(0, 2), (3, 1)]
FROM_INNER = [(1, 2), (2, 1)]
LAST = [(1, 3), (2, 0), (0, 1), (3, 2)]
CHUNK = 512
VMEM = pl.BlockSpec(memory_space=pltpu.VMEM)
SMEM = pl.BlockSpec(memory_space=pltpu.SMEM)
ANY = pl.BlockSpec(memory_space=pl.ANY)
F32, BF16 = jnp.float32, jnp.bfloat16


def shape(dims, dtype):
    return jax.ShapeDtypeStruct(dims, dtype)


class Order:
    def __init__(self):
        self.last = None

    def __call__(self, body, outs, out_specs, args, specs, scratch=(), aliases=None, name=None):
        count = len(args)
        if self.last is not None:
            args, specs = [*args, self.last], [*specs, ANY]
        extra = len(args) - count

        def run(*refs):
            body(*refs[:count], *refs[count + extra :])

        result = pl.pallas_call(
            run,
            out_shape=tuple(outs),
            in_specs=list(specs),
            out_specs=tuple(out_specs),
            scratch_shapes=list(scratch),
            input_output_aliases=aliases or {},
            compiler_params=pltpu.CompilerParams(vmem_limit_bytes=12 * 2**20),
            cost_estimate=pl.CostEstimate(flops=0, bytes_accessed=1024, transcendentals=0),
            name=name,
        )(*args)
        self.last = result[0]
        return result


def encode(x):
    x = x * x
    x = x * x
    return (x * x).astype(BF16)


def decode(y):
    y = y.astype(F32)
    return jnp.where(y > 0.0, jnp.exp2(0.125 * jnp.log2(y)), 0.0)


def load_body(table_ref, held_ref, peak_ref, sems):
    count = sems.shape[0]
    rows = table_ref.shape[0] // count
    copies = [
        pltpu.make_async_copy(table_ref.at[pl.ds(i * rows, rows)], held_ref.at[pl.ds(i * rows, rows)], sems.at[i])
        for i in range(count)
    ]
    for copy in copies:
        copy.start()
    top = jnp.zeros((16, table_ref.shape[1]), BF16)
    for i, copy in enumerate(copies):
        copy.wait()

        def step(k, best, i=i):
            at = pl.multiple_of(i * rows + k * 16, 16)
            return jnp.maximum(best, held_ref[pl.ds(at, 16), :])

        top = lax.fori_loop(0, rows // 16, step, top)
    peak_ref[...] = jnp.full(peak_ref.shape, jnp.max(top.astype(F32)), F32)


def corner(ref):
    return ref[0:1, 0:1]


def top_of(peaks):
    return jnp.maximum(
        jnp.maximum(corner(peaks[0]), corner(peaks[1])), jnp.maximum(corner(peaks[2]), corner(peaks[3]))
    )


def all_swaps(tile, axes):
    return [tile] + [lax.ppermute(tile, axes, [(i, i ^ k) for i in range(4)]) for k in range(1, 4)]


def products(idx, slot, left_ref, table_ref, weights_ref, sums_ref, arrive, put):
    piece = weights_ref.shape[1]
    for c in range(piece // CHUNK):
        here = slice(c * CHUNK, (c + 1) * CHUNK)
        cols = pl.ds(pl.multiple_of(idx[slot] * piece + c * CHUNK, CHUNK), CHUNK)
        total = jnp.dot(left_ref[...], table_ref[:, cols], preferred_element_type=F32)
        put(here, total)
        if c == 0:
            arrive.wait()
        weighted = total * weights_ref[:, here].astype(F32)
        sums = sums_ref[...]
        for k in range(CHUNK // 128):
            sums = sums + weighted[:, k * 128 : (k + 1) * 128]
        sums_ref[...] = sums


def fetch_weights(idx, slots, step, at, weights_ref, held, sems):
    half = held.shape[1]
    copies = [
        pltpu.make_async_copy(weights_ref.at[step, idx[s], pl.ds(at, half)], held.at[k], sems.at[k])
        for k, s in enumerate(slots)
    ]
    for copy in copies:
        copy.start()
    return copies


def first_body(step, at, spread, extra, idx, x0, x1, x2, x3, table_ref, weights_ref, *refs):
    refs = refs[extra:]
    peaks, (out0_ref, out1_ref, sums_ref, left_ref, held, sems) = refs[:-6], refs[-6:]
    copies = fetch_weights(idx, (0, 1), step, at, weights_ref, held, sems)
    depth = x0.shape[1]
    for q, x in enumerate((x0, x1, x2, x3)):
        left_ref[:, pl.ds(pl.multiple_of(idx[4 + q] * depth, depth), depth)] = x[...]
    scale = (TOP / spread) / (corner(peaks[0]) if step == 0 else top_of(peaks))
    sums_ref[...] = jnp.zeros_like(sums_ref)
    for slot, out_ref in enumerate((out0_ref, out1_ref)):
        def put(here, total, out_ref=out_ref):
            out_ref[:, here] = encode(total * scale)

        products(idx, slot, left_ref, table_ref, held.at[slot], sums_ref, copies[slot], put)


def rest_body(step, at, write, has_out, extra, idx, left_ref, sums_in, table_ref, weights_ref, *refs):
    refs = refs[extra:]
    if write is not None:
        message_ref, refs = refs[0], refs[2 if has_out else 1 :]
    (part_ref, own_ref, tile_ref, own_weights_ref), refs = refs[:4], refs[4:]
    if write is not None:
        out_ref, refs = refs[0], refs[1:]
    sums_ref, held, sems = refs
    if write is not None:
        copy_out = pltpu.make_async_copy(message_ref, out_ref.at[write[0], pl.ds(write[1], message_ref.shape[0])], sems.at[2])
        copy_out.start()
    copies = fetch_weights(idx, (2, 3), step, at, weights_ref, held, sems)
    sums_ref[...] = sums_in[...]
    for k, out in enumerate((part_ref, own_ref)):
        def put(here, total, out=out):
            out[:, here] = total

        products(idx, 2 + k, left_ref, table_ref, held.at[k], sums_ref, copies[k], put)
    own_weights_ref[...] = held[1]
    tile_ref[...] = jnp.broadcast_to(jnp.sum(sums_ref[...].T, axis=0, keepdims=True), tile_ref.shape)
    if write is not None:
        copy_out.wait()


def add_body(a_ref, b_ref, table_ref, *refs):
    refs[-1][...] = a_ref[...] + b_ref[...]


def far_body(step, spread, forward, extra, idx, part_ref, pair_ref, table_ref, *refs):
    peaks, refs = refs[:4], refs[4 + extra :]
    if forward:
        refs[2][...] = refs[0][...]
        refs = refs[1:]
    out = refs[0]
    top = top_of(peaks)
    scale = (TOP / spread) / top

    @pl.when(idx[8] == 1)
    def _():
        pair = decode(pair_ref[...])
        if step == 0:
            pair = pair * (corner(peaks[1]) / top)
        out[...] = encode(part_ref[...] * scale + pair)

    @pl.when(idx[8] == 0)
    def _():
        out[...] = encode(part_ref[...] * scale)


def last_body(step, spread, hidden, finish, count, idx, own_ref, pair_ref, outer_ref, inner_ref, far_ref, weights_ref, table_ref, *refs):
    tiles, refs = [ref[...] for ref in refs[:count]], refs[count:]
    peaks, logs_in, refs = refs[:4], refs[4] if step else None, refs[5 if step else 4 :]
    if finish is not None:
        refs = refs[1:]
    lowered_ref, message_ref, logs_ref = refs[:3]
    if finish is not None:
        out_ref, mixed_ref, sem = refs[3:]
    else:
        (mixed_ref,) = refs[3:]
    half = own_ref.shape[0]
    top = top_of(peaks)
    unscale = top * (spread / TOP)
    total = tiles[0] + tiles[1]
    if count == 4:
        total = total + (tiles[2] + tiles[3])
    normal = total / hidden
    logs = jnp.log(normal)
    logs_ref[...] = logs if logs_in is None else logs_in[...] + logs
    inverse = jnp.broadcast_to(1.0 / normal[0:1, :], (half, half)).T

    def sent_by(k):
        return corner(peaks[k]) * (spread / TOP) if step == 0 else unscale

    @pl.when(idx[8] == 1)
    def _():
        mixed_ref[...] = (
            own_ref[...]
            + (decode(outer_ref[...]) * sent_by(2) + decode(inner_ref[...]) * sent_by(3))
            + decode(far_ref[...]) * unscale
        )

    @pl.when(idx[8] == 0)
    def _():
        mixed_ref[...] = own_ref[...] + (decode(pair_ref[...]) * sent_by(1) + decode(far_ref[...]) * unscale)

    writes = []
    parts = 1 if finish is None else 2
    for part in range(parts):
        rows = slice(part * half // parts, (part + 1) * half // parts)
        for k in range(own_ref.shape[1] // 128):
            here = slice(k * 128, (k + 1) * 128)
            message = mixed_ref[rows, here] * weights_ref[rows, here].astype(F32) * inverse[rows, :]
            lowered_ref[rows, here] = message.astype(BF16)
            message_ref[rows, k, :] = message
        if finish is not None:
            size = half // parts
            place = out_ref.at[finish[0], pl.ds(finish[1] + part * size, size)]
            writes.append(pltpu.make_async_copy(message_ref.at[pl.ds(part * size, size)], place, sem.at[part]))
            writes[-1].start()
    for write in writes:
        write.wait()


def fast(transition, emission, start):
    seqs, piece = start.shape[0], start.shape[3]
    hidden = 16 * piece
    half = seqs // HALVES
    table = transition.reshape(4 * piece, 4 * piece)
    me = lax.axis_index("state")
    d = lax.axis_index("dp") * 2 + lax.axis_index("sub")
    slots = jnp.asarray(SLOTS, jnp.int32)[me]
    inner = jnp.logical_and(me > 0, me < 3)
    idx = jnp.concatenate([slots, jnp.stack([d, d ^ 1, d ^ 2, d ^ 3, inner]).astype(jnp.int32)])
    weights = jnp.transpose(emission[:, :, 0], (0, 2, 1, 3))
    wide, code = shape((half, piece), F32), shape((half, piece), BF16)
    square, tile = shape((half, 128), F32), shape((8, 128), F32)
    rows = shape((half, piece // 128, 128), F32)
    out_shape = shape((STEPS, seqs, piece // 128, 128), F32)
    dma = pltpu.SemaphoreType.DMA
    order = Order()

    table, weights, idx = lax.optimization_barrier((table, weights, idx))
    weights = pltpu.with_memory_space_constraint(weights, pltpu.HBM)
    held, peak = order(
        load_body, [pltpu.VMEM(table.shape, table.dtype), shape((8, 128), F32)], [VMEM] * 2, [table], [ANY],
        [dma((8,))], name="load_table",
    )
    order.last = peak
    held = pltpu.with_memory_space_constraint(held, pltpu.VMEM)
    peaks = all_swaps(peak, "state")

    spreads = [hidden * 1.01 * (START_TOP if step == 0 else 1.0) for step in range(STEPS)]
    state = [{"lowered": start[h * half : (h + 1) * half, 0, 0].astype(BF16)} for h in range(HALVES)]
    box = {"out": None}

    def swap(h, axis, k):
        s = state[h]
        s["their"] = lax.ppermute(s["tile"], axis, [(i, i ^ k) for i in range(lax.axis_size(axis))])

    def add(h, after=()):
        s = state[h]
        s["tile"] = order(
            add_body, [tile], [VMEM], [s["tile"], s["their"], held, *after], [VMEM] * 3 + [ANY] * len(after),
            name="add_sums",
        )[0]

    def gather(h):
        s = state[h]
        own = s["lowered"]
        s["across"] = lax.ppermute(own, "dp", [(0, 1), (1, 0)])
        s["xs"] = [own, lax.ppermute(own, "sub", [(0, 1), (1, 0)])]

    def gather_rest(h, across):
        state[h]["xs"] += [across, lax.ppermute(across, "sub", [(0, 1), (1, 0)])]

    def begin(step, h):
        s, at, spread = state[h], h * half, spreads[step]
        used = [peak] if step == 0 else peaks
        after = state[1]["xs"][2:] if step == h == 0 else []
        send0, send1, sums, left = order(
            functools.partial(first_body, step, at, spread, len(after)),
            [code, code, square, shape((half, 4 * piece), BF16)], [VMEM] * 4,
            [idx, *s["xs"], held, weights, *after, *used],
            [SMEM] + [VMEM] * 5 + [ANY] * (1 + len(after)) + [VMEM] * len(used),
            [pltpu.VMEM((2, half, piece), BF16), dma((2,))], name="product_first",
        )
        ends = step == STEPS - 1 and h == 1
        if "tile" in state[1 - h] and not ends:
            add(1 - h, [state[1 - h]["far"]])
            swap(1 - h, "sub", 1)
        s["pair"] = lax.ppermute(send0, "state", PAIRS)
        s["outer"] = lax.ppermute(send1, "state", FROM_OUTER)
        s["inner"] = lax.ppermute(send1, "state", FROM_INNER)
        s["left"], s["sums"] = left, sums

    def proceed(step, h, forward, message=None, place=None):
        s, at = state[h], h * half
        args = [idx, s["left"], s["sums"], held, weights]
        after = [state[0]["far"]] if step == STEPS - 1 and h == 1 else []
        args, specs = args + after, [SMEM] + [VMEM] * 3 + [ANY] * (1 + len(after))
        outs, out_specs, aliases = [wide, wide, tile, code], [VMEM] * 4, None
        has_out = box["out"] is not None
        if place is not None:
            args, specs = args + [message], specs + [VMEM]
            outs, out_specs = outs + [out_shape], out_specs + [ANY]
            if has_out:
                aliases = {len(args): 4}
                args, specs = args + [box["out"]], specs + [ANY]
        result = order(
            functools.partial(rest_body, step, at, place, has_out, len(after)), outs, out_specs, args, specs,
            [pltpu.VMEM((half, 128), F32), pltpu.VMEM((2, half, piece), BF16), dma((3,))], aliases,
            name="product_rest",
        )
        part, s["own"], s["tile"], s["weights"] = result[:4]
        if place is not None:
            box["out"] = result[4]
        swap(h, "state", 1)
        ends = step == STEPS - 1 and h == 1
        args = [idx, part, s["pair"], held, *peaks]
        if ends:
            add(h)
            swap(h, "state", 2)
        after = [s["their"]] if ends or step == 0 else []
        args, specs = args + after, [SMEM] + [VMEM] * 7 + [ANY] * len(after)
        if forward:
            args, specs = args + [state[1 - h]["across"]], specs + [VMEM]
        count = 2 if forward else 1
        result = order(
            functools.partial(far_body, step, spreads[step], forward, len(after)), [code] * count, [VMEM] * count,
            args, specs, name="far_block",
        )
        if ends:
            s["far"] = lax.ppermute(result[0], "state", LAST)
            return
        if forward:
            gather_rest(1 - h, result[1])
        s["far"] = lax.ppermute(result[0], "state", LAST)
        add(h, [s["outer"]])
        swap(h, "dp", 1)
        add(h, [s["inner"]])
        swap(h, "state", 2)
        if step == STEPS - 1:
            add(h)
            swap(h, "sub", 1)

    def finish(step, h):
        s = state[h]
        args = [idx, s["own"], s["pair"], s["outer"], s["inner"], s["far"], s["weights"], held]
        tiles = s.get("tiles") or [s["tile"], s["their"]]
        args += [*tiles, *peaks]
        specs = [SMEM] + [VMEM] * (len(args) - 1)
        if step:
            args, specs = args + [s["logs"]], specs + [VMEM]
        outs, out_specs, aliases, place = [code, rows, tile], [VMEM] * 3, None, None
        scratch = [pltpu.VMEM((half, piece), F32)]
        if step == STEPS - 1:
            place = (step, h * half)
            aliases = {len(args): 3}
            args, specs = args + [box["out"]], specs + [ANY]
            outs, out_specs, scratch = outs + [out_shape], out_specs + [ANY], scratch + [dma((2,))]
        result = order(
            functools.partial(last_body, step, spreads[step], hidden, place, len(tiles)), outs, out_specs, args, specs,
            scratch, aliases, name="normalise",
        )
        s["lowered"], s["message"], s["logs"] = result[:3]
        if place is not None:
            box["out"] = result[3]

    for s in state:
        own = s["lowered"]
        s["xs"] = [own] + [lax.ppermute(own, ("dp", "sub"), [(i, i ^ k) for i in range(4)]) for k in (1, 2, 3)]
    for step in range(STEPS):
        begin(step, 0)
        if step:
            finish(step - 1, 1)
            gather(1)
            proceed(step, 0, True, state[1]["message"], (step - 1, half))
        else:
            proceed(step, 0, False)
        begin(step, 1)
        if step < STEPS - 1:
            finish(step, 0)
            gather(0)
            proceed(step, 1, True, state[0]["message"], (step, 0))
        else:
            proceed(step, 1, False)
            finish(step, 0)
    add(1)
    state[1]["tiles"] = all_swaps(state[1]["tile"], ("dp", "sub"))
    finish(STEPS - 1, 1)
    log_scale = jnp.concatenate([s["logs"][0] for s in state])
    return box["out"].reshape(STEPS, seqs, 1, 1, piece), log_scale


def shards(transition, emission, start):
    sizes = [lax.axis_size(name) for name in ("state", "dp", "sub")]
    if sizes == [4, 2, 2] and start.shape[0] == HALVES * 128 and start.shape[3] % CHUNK == 0:
        return fast(transition, emission, start)
    return general(transition, emission, start)


def solution(mesh):
    in_specs = (
        P(None, "state", None, ("dp", "sub")),
        P(None, "groups", ("dp", "sub"), None, None),
        P("groups", ("dp", "sub"), "state", None),
    )
    out_specs = (P(None, "groups", ("dp", "sub"), "state", None), P("groups"))
    return jax.shard_map(shards, mesh=mesh, in_specs=in_specs, out_specs=out_specs, check_vma=False)
```

```python
import functools

import jax
import jax.numpy as jnp
from jax import lax
from jax.experimental import pallas as pl
from jax.experimental.pallas import tpu as pltpu
from jax.sharding import PartitionSpec as P

STEPS = 4
HALVES = 2
TOP = 60000.0
START_TOP = 10.0


def product_kernel(num_x, with_peak, idx_ref, *refs):
    x_refs, t_ref, out_ref = refs[:num_x], refs[num_x], refs[num_x + 1]
    depth = x_refs[0].shape[1]
    total = None
    for q in range(num_x):
        rows = pl.ds(pl.multiple_of(idx_ref[1 + q] * depth, depth), depth)
        term = jnp.dot(x_refs[q][...], t_ref[rows, :], preferred_element_type=jnp.float32)
        total = term if total is None else total + term
    out_ref[0] = total
    if with_peak:
        peak_ref = refs[num_x + 2]
        here = jnp.max(t_ref[...].astype(jnp.float32).reshape(-1, 8, t_ref.shape[1]), axis=0)
        first = jnp.logical_and(pl.program_id(0) == 0, pl.program_id(1) == 0)

        @pl.when(first)
        def _():
            peak_ref[...] = here

        @pl.when(jnp.logical_not(first))
        def _():
            peak_ref[...] = jnp.maximum(peak_ref[...], here)


def product(indices, xs, table, blocks, with_peak):
    seqs, depth = xs[0].shape
    rows, width = table.shape
    piece = width // blocks
    tile = min(512, piece)
    per = piece // tile

    def place(o, c, idx):
        return (0, lax.rem(idx[0] + o, blocks) * per + c)

    out_shape = [jax.ShapeDtypeStruct((blocks, seqs, piece), jnp.float32)]
    out_specs = [pl.BlockSpec((1, seqs, tile), lambda o, c, idx: (o, 0, c))]
    if with_peak:
        out_shape.append(jax.ShapeDtypeStruct((8, tile), jnp.float32))
        out_specs.append(pl.BlockSpec((8, tile), lambda o, c, idx: (0, 0)))
    return pl.pallas_call(
        functools.partial(product_kernel, len(xs), with_peak),
        grid_spec=pltpu.PrefetchScalarGridSpec(
            num_scalar_prefetch=1,
            grid=(blocks, per),
            in_specs=[pl.BlockSpec((seqs, depth), lambda o, c, idx: (0, 0)) for _ in xs]
            + [pl.BlockSpec((rows, tile), place)],
            out_specs=out_specs,
        ),
        out_shape=out_shape,
        compiler_params=pltpu.CompilerParams(vmem_limit_bytes=32 * 2**20),
        cost_estimate=pl.CostEstimate(
            flops=2 * seqs * rows * width, bytes_accessed=2 * rows * width, transcendentals=0
        ),
        name="product_peak" if with_peak else "product",
    )(indices, *xs, table)


def gather_blocks(block):
    dp, sub = lax.axis_size("dp"), lax.axis_size("sub")
    found = [block]
    for k in range(1, dp):
        found.append(lax.ppermute(block, "dp", [(i, (i + k) % dp) for i in range(dp)]))
    out = []
    for l in range(sub):
        for item in found:
            out.append(item if l == 0 else lax.ppermute(item, "sub", [(i, (i + l) % sub) for i in range(sub)]))
    return out


def block_owners():
    dp, sub = lax.axis_size("dp"), lax.axis_size("sub")
    x, c = lax.axis_index("dp"), lax.axis_index("sub")
    return [
        lax.rem(x + dp - k, dp) * sub + lax.rem(c + sub - l, sub) for l in range(sub) for k in range(dp)
    ]


def line_sum(parts, into, back, first_into, first_back_r, first_back_l):
    n = lax.axis_size("state")
    right = left = None
    for k in range(1, n):
        scale = first_into if k == 1 else into
        to_r, to_l = parts[n - k], parts[k]
        if k > 1:
            to_r = to_r + right.astype(jnp.float32) * (first_back_r if k == 2 else back)
            to_l = to_l + left.astype(jnp.float32) * (first_back_l if k == 2 else back)
        right = lax.ppermute((to_r * scale).astype(jnp.float16), "state", [(i, i + 1) for i in range(k)])
        left = lax.ppermute((to_l * scale).astype(jnp.float16), "state", [(i, i - 1) for i in range(n - k, n)])
    last_r, last_l = (first_back_r, first_back_l) if n == 2 else (back, back)
    return parts[0] + right.astype(jnp.float32) * last_r + left.astype(jnp.float32) * last_l


def general(transition, emission, start):
    seq_count = start.shape[0]
    piece = start.shape[3]
    blocks = lax.axis_size("state")
    me = lax.axis_index("state")
    table = transition.reshape(transition.shape[0] * piece, transition.shape[3])
    hidden = blocks * piece * lax.axis_size("dp") * lax.axis_size("sub")
    half = seq_count // HALVES
    indices = jnp.stack([me] + block_owners()).astype(jnp.int32)
    weights = jnp.transpose(emission[:, :, 0], (0, 2, 1, 3))
    weights = jnp.concatenate([weights, weights], axis=1)
    weights = lax.dynamic_slice_in_dim(weights, me, blocks, 1)

    messages = [start[h * half : (h + 1) * half, 0, 0] for h in range(HALVES)]
    history, normals = [], []
    into = back = None
    for step in range(STEPS):
        step_messages, step_normals = [], []
        for h in range(HALVES):
            rows = slice(h * half, (h + 1) * half)
            xs = gather_blocks(messages[h].astype(jnp.bfloat16))
            first = step == 0 and h == 0
            if first:
                parts, peak = product(indices, xs, table, blocks, True)
                own_peak = jnp.max(peak)
                peaks = lax.all_gather(jnp.full((1, 128), own_peak), "state", axis=0, tiled=True)[:, 0]
                top_peak = jnp.max(peaks)
                into = TOP / (hidden * top_peak)
                back = hidden * top_peak / TOP
                peak_r = lax.dynamic_index_in_dim(peaks, lax.rem(me + blocks - 1, blocks), 0, False)
                peak_l = lax.dynamic_index_in_dim(peaks, lax.rem(me + 1, blocks), 0, False)
                spread = hidden * START_TOP
                scales = (
                    into / START_TOP, back * START_TOP,
                    TOP / (spread * own_peak), spread * peak_r / TOP, spread * peak_l / TOP,
                )
            else:
                (parts,) = product(indices, xs, table, blocks, False)
                grow = START_TOP if step == 0 else 1.0
                scales = (into / grow, back * grow, into / grow, back * grow, back * grow)
            step_weights = weights[step, :, rows].astype(jnp.float32)
            own_sum = jnp.sum(parts * step_weights, axis=(0, 2))
            sums = lax.all_gather(own_sum[None], ("state", "dp", "sub"), axis=0, tiled=True)
            normal = jnp.sum(sums, axis=0) / hidden
            summed = line_sum([parts[o] for o in range(blocks)], *scales)
            message = summed * step_weights[0] / normal[:, None]
            messages[h] = message
            step_messages.append(message)
            step_normals.append(normal)
        history.append(jnp.concatenate(step_messages, axis=0))
        normals.append(jnp.concatenate(step_normals, axis=0))
    log_scale = functools.reduce(lambda a, b: a + b, [jnp.log(x) for x in normals])
    out = jnp.stack(history).reshape(STEPS, seq_count, 1, 1, piece)
    return out, log_scale


SLOTS = ((3, 2, 1, 0), (0, 2, 3, 1), (3, 1, 0, 2), (0, 1, 2, 3))
PAIRS = [(0, 1), (1, 0), (2, 3), (3, 2)]
FROM_OUTER = [(0, 2), (3, 1)]
FROM_INNER = [(1, 2), (2, 1)]
LAST = [(1, 3), (2, 0), (0, 1), (3, 2)]
CHUNK = 512
VMEM = pl.BlockSpec(memory_space=pltpu.VMEM)
SMEM = pl.BlockSpec(memory_space=pltpu.SMEM)
ANY = pl.BlockSpec(memory_space=pl.ANY)
F32, BF16 = jnp.float32, jnp.bfloat16


def shape(dims, dtype):
    return jax.ShapeDtypeStruct(dims, dtype)


class Order:
    def __init__(self):
        self.last = None

    def __call__(self, body, outs, out_specs, args, specs, scratch=(), aliases=None, name=None):
        count = len(args)
        if self.last is not None:
            args, specs = [*args, self.last], [*specs, ANY]
        extra = len(args) - count

        def run(*refs):
            body(*refs[:count], *refs[count + extra :])

        result = pl.pallas_call(
            run,
            out_shape=tuple(outs),
            in_specs=list(specs),
            out_specs=tuple(out_specs),
            scratch_shapes=list(scratch),
            input_output_aliases=aliases or {},
            compiler_params=pltpu.CompilerParams(vmem_limit_bytes=12 * 2**20),
            cost_estimate=pl.CostEstimate(flops=0, bytes_accessed=1024, transcendentals=0),
            name=name,
        )(*args)
        self.last = result[0]
        return result


def encode(x):
    x = x * x
    x = x * x
    return (x * x).astype(BF16)


def decode(y):
    y = y.astype(F32)
    return jnp.where(y > 0.0, jnp.exp2(0.125 * jnp.log2(y)), 0.0)


def load_body(table_ref, held_ref, peak_ref, sems):
    count = sems.shape[0]
    rows = table_ref.shape[0] // count
    copies = [
        pltpu.make_async_copy(table_ref.at[pl.ds(i * rows, rows)], held_ref.at[pl.ds(i * rows, rows)], sems.at[i])
        for i in range(count)
    ]
    for copy in copies:
        copy.start()
    top = jnp.zeros((16, table_ref.shape[1]), BF16)
    for i, copy in enumerate(copies):
        copy.wait()

        def step(k, best, i=i):
            at = pl.multiple_of(i * rows + k * 16, 16)
            return jnp.maximum(best, held_ref[pl.ds(at, 16), :])

        top = lax.fori_loop(0, rows // 16, step, top)
    peak_ref[...] = jnp.full(peak_ref.shape, jnp.max(top.astype(F32)), F32)


def corner(ref):
    return ref[0:1, 0:1]


def top_of(peaks):
    return jnp.maximum(
        jnp.maximum(corner(peaks[0]), corner(peaks[1])), jnp.maximum(corner(peaks[2]), corner(peaks[3]))
    )


def all_swaps(tile, axes):
    return [tile] + [lax.ppermute(tile, axes, [(i, i ^ k) for i in range(4)]) for k in range(1, 4)]


def products(idx, slot, left_ref, table_ref, weights_ref, sums_ref, arrive, put):
    piece = weights_ref.shape[1]
    for c in range(piece // CHUNK):
        here = slice(c * CHUNK, (c + 1) * CHUNK)
        cols = pl.ds(pl.multiple_of(idx[slot] * piece + c * CHUNK, CHUNK), CHUNK)
        total = jnp.dot(left_ref[...], table_ref[:, cols], preferred_element_type=F32)
        put(here, total)
        if c == 0:
            arrive.wait()
        weighted = total * weights_ref[:, here].astype(F32)
        sums = sums_ref[...]
        for k in range(CHUNK // 128):
            sums = sums + weighted[:, k * 128 : (k + 1) * 128]
        sums_ref[...] = sums


def fetch_weights(idx, slots, step, at, weights_ref, held, sems):
    half = held.shape[1]
    copies = [
        pltpu.make_async_copy(weights_ref.at[step, idx[s], pl.ds(at, half)], held.at[k], sems.at[k])
        for k, s in enumerate(slots)
    ]
    for copy in copies:
        copy.start()
    return copies


def first_body(step, at, spread, extra, idx, x0, x1, x2, x3, table_ref, weights_ref, *refs):
    refs = refs[extra:]
    peaks, (out0_ref, out1_ref, sums_ref, left_ref, held, sems) = refs[:-6], refs[-6:]
    copies = fetch_weights(idx, (0, 1), step, at, weights_ref, held, sems)
    depth = x0.shape[1]
    for q, x in enumerate((x0, x1, x2, x3)):
        left_ref[:, pl.ds(pl.multiple_of(idx[4 + q] * depth, depth), depth)] = x[...]
    scale = (TOP / spread) / (corner(peaks[0]) if step == 0 else top_of(peaks))
    sums_ref[...] = jnp.zeros_like(sums_ref)
    for slot, out_ref in enumerate((out0_ref, out1_ref)):
        def put(here, total, out_ref=out_ref):
            out_ref[:, here] = encode(total * scale)

        products(idx, slot, left_ref, table_ref, held.at[slot], sums_ref, copies[slot], put)


def rest_body(step, at, write, has_out, extra, idx, left_ref, sums_in, table_ref, weights_ref, *refs):
    refs = refs[extra:]
    if write is not None:
        message_ref, refs = refs[0], refs[2 if has_out else 1 :]
    (part_ref, own_ref, tile_ref, own_weights_ref), refs = refs[:4], refs[4:]
    if write is not None:
        out_ref, refs = refs[0], refs[1:]
    sums_ref, held, sems = refs
    if write is not None:
        copy_out = pltpu.make_async_copy(message_ref, out_ref.at[write[0], pl.ds(write[1], message_ref.shape[0])], sems.at[2])
        copy_out.start()
    copies = fetch_weights(idx, (2, 3), step, at, weights_ref, held, sems)
    sums_ref[...] = sums_in[...]
    for k, out in enumerate((part_ref, own_ref)):
        def put(here, total, out=out):
            out[:, here] = total

        products(idx, 2 + k, left_ref, table_ref, held.at[k], sums_ref, copies[k], put)
    own_weights_ref[...] = held[1]
    tile_ref[...] = jnp.broadcast_to(jnp.sum(sums_ref[...].T, axis=0, keepdims=True), tile_ref.shape)
    if write is not None:
        copy_out.wait()


def add_body(a_ref, b_ref, table_ref, *refs):
    refs[-1][...] = a_ref[...] + b_ref[...]


def far_body(step, spread, forward, extra, idx, part_ref, pair_ref, table_ref, *refs):
    peaks, refs = refs[:4], refs[4 + extra :]
    if forward:
        refs[2][...] = refs[0][...]
        refs = refs[1:]
    out = refs[0]
    top = top_of(peaks)
    scale = (TOP / spread) / top

    @pl.when(idx[8] == 1)
    def _():
        pair = decode(pair_ref[...])
        if step == 0:
            pair = pair * (corner(peaks[1]) / top)
        out[...] = encode(part_ref[...] * scale + pair)

    @pl.when(idx[8] == 0)
    def _():
        out[...] = encode(part_ref[...] * scale)


def last_body(step, spread, hidden, finish, count, idx, own_ref, pair_ref, outer_ref, inner_ref, far_ref, weights_ref, table_ref, *refs):
    tiles, refs = [ref[...] for ref in refs[:count]], refs[count:]
    peaks, logs_in, refs = refs[:4], refs[4] if step else None, refs[5 if step else 4 :]
    if finish is not None:
        refs = refs[1:]
    lowered_ref, message_ref, logs_ref = refs[:3]
    if finish is not None:
        out_ref, mixed_ref, sem = refs[3:]
    else:
        (mixed_ref,) = refs[3:]
    half = own_ref.shape[0]
    top = top_of(peaks)
    unscale = top * (spread / TOP)
    total = tiles[0] + tiles[1]
    if count == 4:
        total = total + (tiles[2] + tiles[3])
    normal = total / hidden
    logs = jnp.log(normal)
    logs_ref[...] = logs if logs_in is None else logs_in[...] + logs
    inverse = jnp.broadcast_to(1.0 / normal[0:1, :], (half, half)).T

    def sent_by(k):
        return corner(peaks[k]) * (spread / TOP) if step == 0 else unscale

    @pl.when(idx[8] == 1)
    def _():
        mixed_ref[...] = (
            own_ref[...]
            + (decode(outer_ref[...]) * sent_by(2) + decode(inner_ref[...]) * sent_by(3))
            + decode(far_ref[...]) * unscale
        )

    @pl.when(idx[8] == 0)
    def _():
        mixed_ref[...] = own_ref[...] + (decode(pair_ref[...]) * sent_by(1) + decode(far_ref[...]) * unscale)

    writes = []
    parts = 1 if finish is None else 2
    for part in range(parts):
        rows = slice(part * half // parts, (part + 1) * half // parts)
        for k in range(own_ref.shape[1] // 128):
            here = slice(k * 128, (k + 1) * 128)
            message = mixed_ref[rows, here] * weights_ref[rows, here].astype(F32) * inverse[rows, :]
            lowered_ref[rows, here] = message.astype(BF16)
            message_ref[rows, k, :] = message
        if finish is not None:
            size = half // parts
            place = out_ref.at[finish[0], pl.ds(finish[1] + part * size, size)]
            writes.append(pltpu.make_async_copy(message_ref.at[pl.ds(part * size, size)], place, sem.at[part]))
            writes[-1].start()
    for write in writes:
        write.wait()


def fast(transition, emission, start):
    seqs, piece = start.shape[0], start.shape[3]
    hidden = 16 * piece
    half = seqs // HALVES
    table = transition.reshape(4 * piece, 4 * piece)
    me = lax.axis_index("state")
    d = lax.axis_index("dp") * 2 + lax.axis_index("sub")
    slots = jnp.asarray(SLOTS, jnp.int32)[me]
    inner = jnp.logical_and(me > 0, me < 3)
    idx = jnp.concatenate([slots, jnp.stack([d, d ^ 1, d ^ 2, d ^ 3, inner]).astype(jnp.int32)])
    weights = jnp.transpose(emission[:, :, 0], (0, 2, 1, 3))
    wide, code = shape((half, piece), F32), shape((half, piece), BF16)
    square, tile = shape((half, 128), F32), shape((8, 128), F32)
    rows = shape((half, piece // 128, 128), F32)
    out_shape = shape((STEPS, seqs, piece // 128, 128), F32)
    dma = pltpu.SemaphoreType.DMA
    order = Order()

    table, weights, idx = lax.optimization_barrier((table, weights, idx))
    weights = pltpu.with_memory_space_constraint(weights, pltpu.HBM)
    held, peak = order(
        load_body, [pltpu.VMEM(table.shape, table.dtype), shape((8, 128), F32)], [VMEM] * 2, [table], [ANY],
        [dma((8,))], name="load_table",
    )
    order.last = peak
    held = pltpu.with_memory_space_constraint(held, pltpu.VMEM)
    peaks = all_swaps(peak, "state")

    spreads = [hidden * 1.01 * (START_TOP if step == 0 else 1.0) for step in range(STEPS)]
    state = [{"lowered": start[h * half : (h + 1) * half, 0, 0].astype(BF16)} for h in range(HALVES)]
    box = {"out": None}

    def swap(h, axis, k):
        s = state[h]
        s["their"] = lax.ppermute(s["tile"], axis, [(i, i ^ k) for i in range(lax.axis_size(axis))])

    def add(h, after=()):
        s = state[h]
        s["tile"] = order(
            add_body, [tile], [VMEM], [s["tile"], s["their"], held, *after], [VMEM] * 3 + [ANY] * len(after),
            name="add_sums",
        )[0]

    def gather(h):
        s = state[h]
        own = s["lowered"]
        s["across"] = lax.ppermute(own, "dp", [(0, 1), (1, 0)])
        s["xs"] = [own, lax.ppermute(own, "sub", [(0, 1), (1, 0)])]

    def gather_rest(h, across):
        state[h]["xs"] += [across, lax.ppermute(across, "sub", [(0, 1), (1, 0)])]

    def begin(step, h):
        s, at, spread = state[h], h * half, spreads[step]
        used = [peak] if step == 0 else peaks
        after = state[1]["xs"][2:] if step == h == 0 else []
        send0, send1, sums, left = order(
            functools.partial(first_body, step, at, spread, len(after)),
            [code, code, square, shape((half, 4 * piece), BF16)], [VMEM] * 4,
            [idx, *s["xs"], held, weights, *after, *used],
            [SMEM] + [VMEM] * 5 + [ANY] * (1 + len(after)) + [VMEM] * len(used),
            [pltpu.VMEM((2, half, piece), BF16), dma((2,))], name="product_first",
        )
        ends = step == STEPS - 1 and h == 1
        if "tile" in state[1 - h] and not ends:
            add(1 - h, [state[1 - h]["far"]])
            swap(1 - h, "sub", 1)
        s["pair"] = lax.ppermute(send0, "state", PAIRS)
        s["outer"] = lax.ppermute(send1, "state", FROM_OUTER)
        s["inner"] = lax.ppermute(send1, "state", FROM_INNER)
        s["left"], s["sums"] = left, sums

    def proceed(step, h, forward, message=None, place=None):
        s, at = state[h], h * half
        args = [idx, s["left"], s["sums"], held, weights]
        after = [state[0]["far"]] if step == STEPS - 1 and h == 1 else []
        args, specs = args + after, [SMEM] + [VMEM] * 3 + [ANY] * (1 + len(after))
        outs, out_specs, aliases = [wide, wide, tile, code], [VMEM] * 4, None
        has_out = box["out"] is not None
        if place is not None:
            args, specs = args + [message], specs + [VMEM]
            outs, out_specs = outs + [out_shape], out_specs + [ANY]
            if has_out:
                aliases = {len(args): 4}
                args, specs = args + [box["out"]], specs + [ANY]
        result = order(
            functools.partial(rest_body, step, at, place, has_out, len(after)), outs, out_specs, args, specs,
            [pltpu.VMEM((half, 128), F32), pltpu.VMEM((2, half, piece), BF16), dma((3,))], aliases,
            name="product_rest",
        )
        part, s["own"], s["tile"], s["weights"] = result[:4]
        if place is not None:
            box["out"] = result[4]
        swap(h, "state", 1)
        ends = step == STEPS - 1 and h == 1
        args = [idx, part, s["pair"], held, *peaks]
        if ends:
            add(h)
            swap(h, "state", 2)
        after = [s["their"]] if ends or step == 0 else []
        args, specs = args + after, [SMEM] + [VMEM] * 7 + [ANY] * len(after)
        if forward:
            args, specs = args + [state[1 - h]["across"]], specs + [VMEM]
        count = 2 if forward else 1
        result = order(
            functools.partial(far_body, step, spreads[step], forward, len(after)), [code] * count, [VMEM] * count,
            args, specs, name="far_block",
        )
        if ends:
            s["far"] = lax.ppermute(result[0], "state", LAST)
            return
        if forward:
            gather_rest(1 - h, result[1])
        s["far"] = lax.ppermute(result[0], "state", LAST)
        add(h, [s["outer"]])
        swap(h, "dp", 1)
        add(h, [s["inner"]])
        swap(h, "state", 2)
        if step == STEPS - 1:
            add(h)
            swap(h, "sub", 1)

    def finish(step, h):
        s = state[h]
        args = [idx, s["own"], s["pair"], s["outer"], s["inner"], s["far"], s["weights"], held]
        tiles = s.get("tiles") or [s["tile"], s["their"]]
        args += [*tiles, *peaks]
        specs = [SMEM] + [VMEM] * (len(args) - 1)
        if step:
            args, specs = args + [s["logs"]], specs + [VMEM]
        outs, out_specs, aliases, place = [code, rows, tile], [VMEM] * 3, None, None
        scratch = [pltpu.VMEM((half, piece), F32)]
        if step == STEPS - 1:
            place = (step, h * half)
            aliases = {len(args): 3}
            args, specs = args + [box["out"]], specs + [ANY]
            outs, out_specs, scratch = outs + [out_shape], out_specs + [ANY], scratch + [dma((2,))]
        result = order(
            functools.partial(last_body, step, spreads[step], hidden, place, len(tiles)), outs, out_specs, args, specs,
            scratch, aliases, name="normalise",
        )
        s["lowered"], s["message"], s["logs"] = result[:3]
        if place is not None:
            box["out"] = result[3]

    for s in state:
        own = s["lowered"]
        s["xs"] = [own] + [lax.ppermute(own, ("dp", "sub"), [(i, i ^ k) for i in range(4)]) for k in (1, 2, 3)]
    for step in range(STEPS):
        begin(step, 0)
        if step:
            finish(step - 1, 1)
            gather(1)
            proceed(step, 0, True, state[1]["message"], (step - 1, half))
        else:
            proceed(step, 0, False)
        begin(step, 1)
        if step < STEPS - 1:
            finish(step, 0)
            gather(0)
            proceed(step, 1, True, state[0]["message"], (step, 0))
        else:
            proceed(step, 1, False)
            add(1)
            state[1]["tiles"] = all_swaps(state[1]["tile"], ("dp", "sub"))
            finish(step, 0)
    finish(STEPS - 1, 1)
    log_scale = jnp.concatenate([s["logs"][0] for s in state])
    return box["out"].reshape(STEPS, seqs, 1, 1, piece), log_scale


def shards(transition, emission, start):
    sizes = [lax.axis_size(name) for name in ("state", "dp", "sub")]
    if sizes == [4, 2, 2] and start.shape[0] == HALVES * 128 and start.shape[3] % CHUNK == 0:
        return fast(transition, emission, start)
    return general(transition, emission, start)


def solution(mesh):
    in_specs = (
        P(None, "state", None, ("dp", "sub")),
        P(None, "groups", ("dp", "sub"), None, None),
        P("groups", ("dp", "sub"), "state", None),
    )
    out_specs = (P(None, "groups", ("dp", "sub"), "state", None), P("groups"))
    return jax.shard_map(shards, mesh=mesh, in_specs=in_specs, out_specs=out_specs, check_vma=False)
```

```python
import functools

import jax
import jax.numpy as jnp
from jax import lax
from jax.experimental import pallas as pl
from jax.experimental.pallas import tpu as pltpu
from jax.sharding import PartitionSpec as P

STEPS = 4
HALVES = 2
TOP = 60000.0
START_TOP = 10.0


def product_kernel(num_x, with_peak, idx_ref, *refs):
    x_refs, t_ref, out_ref = refs[:num_x], refs[num_x], refs[num_x + 1]
    depth = x_refs[0].shape[1]
    total = None
    for q in range(num_x):
        rows = pl.ds(pl.multiple_of(idx_ref[1 + q] * depth, depth), depth)
        term = jnp.dot(x_refs[q][...], t_ref[rows, :], preferred_element_type=jnp.float32)
        total = term if total is None else total + term
    out_ref[0] = total
    if with_peak:
        peak_ref = refs[num_x + 2]
        here = jnp.max(t_ref[...].astype(jnp.float32).reshape(-1, 8, t_ref.shape[1]), axis=0)
        first = jnp.logical_and(pl.program_id(0) == 0, pl.program_id(1) == 0)

        @pl.when(first)
        def _():
            peak_ref[...] = here

        @pl.when(jnp.logical_not(first))
        def _():
            peak_ref[...] = jnp.maximum(peak_ref[...], here)


def product(indices, xs, table, blocks, with_peak):
    seqs, depth = xs[0].shape
    rows, width = table.shape
    piece = width // blocks
    tile = min(512, piece)
    per = piece // tile

    def place(o, c, idx):
        return (0, lax.rem(idx[0] + o, blocks) * per + c)

    out_shape = [jax.ShapeDtypeStruct((blocks, seqs, piece), jnp.float32)]
    out_specs = [pl.BlockSpec((1, seqs, tile), lambda o, c, idx: (o, 0, c))]
    if with_peak:
        out_shape.append(jax.ShapeDtypeStruct((8, tile), jnp.float32))
        out_specs.append(pl.BlockSpec((8, tile), lambda o, c, idx: (0, 0)))
    return pl.pallas_call(
        functools.partial(product_kernel, len(xs), with_peak),
        grid_spec=pltpu.PrefetchScalarGridSpec(
            num_scalar_prefetch=1,
            grid=(blocks, per),
            in_specs=[pl.BlockSpec((seqs, depth), lambda o, c, idx: (0, 0)) for _ in xs]
            + [pl.BlockSpec((rows, tile), place)],
            out_specs=out_specs,
        ),
        out_shape=out_shape,
        compiler_params=pltpu.CompilerParams(vmem_limit_bytes=32 * 2**20),
        cost_estimate=pl.CostEstimate(
            flops=2 * seqs * rows * width, bytes_accessed=2 * rows * width, transcendentals=0
        ),
        name="product_peak" if with_peak else "product",
    )(indices, *xs, table)


def gather_blocks(block):
    dp, sub = lax.axis_size("dp"), lax.axis_size("sub")
    found = [block]
    for k in range(1, dp):
        found.append(lax.ppermute(block, "dp", [(i, (i + k) % dp) for i in range(dp)]))
    out = []
    for l in range(sub):
        for item in found:
            out.append(item if l == 0 else lax.ppermute(item, "sub", [(i, (i + l) % sub) for i in range(sub)]))
    return out


def block_owners():
    dp, sub = lax.axis_size("dp"), lax.axis_size("sub")
    x, c = lax.axis_index("dp"), lax.axis_index("sub")
    return [
        lax.rem(x + dp - k, dp) * sub + lax.rem(c + sub - l, sub) for l in range(sub) for k in range(dp)
    ]


def line_sum(parts, into, back, first_into, first_back_r, first_back_l):
    n = lax.axis_size("state")
    right = left = None
    for k in range(1, n):
        scale = first_into if k == 1 else into
        to_r, to_l = parts[n - k], parts[k]
        if k > 1:
            to_r = to_r + right.astype(jnp.float32) * (first_back_r if k == 2 else back)
            to_l = to_l + left.astype(jnp.float32) * (first_back_l if k == 2 else back)
        right = lax.ppermute((to_r * scale).astype(jnp.float16), "state", [(i, i + 1) for i in range(k)])
        left = lax.ppermute((to_l * scale).astype(jnp.float16), "state", [(i, i - 1) for i in range(n - k, n)])
    last_r, last_l = (first_back_r, first_back_l) if n == 2 else (back, back)
    return parts[0] + right.astype(jnp.float32) * last_r + left.astype(jnp.float32) * last_l


def general(transition, emission, start):
    seq_count = start.shape[0]
    piece = start.shape[3]
    blocks = lax.axis_size("state")
    me = lax.axis_index("state")
    table = transition.reshape(transition.shape[0] * piece, transition.shape[3])
    hidden = blocks * piece * lax.axis_size("dp") * lax.axis_size("sub")
    half = seq_count // HALVES
    indices = jnp.stack([me] + block_owners()).astype(jnp.int32)
    weights = jnp.transpose(emission[:, :, 0], (0, 2, 1, 3))
    weights = jnp.concatenate([weights, weights], axis=1)
    weights = lax.dynamic_slice_in_dim(weights, me, blocks, 1)

    messages = [start[h * half : (h + 1) * half, 0, 0] for h in range(HALVES)]
    history, normals = [], []
    into = back = None
    for step in range(STEPS):
        step_messages, step_normals = [], []
        for h in range(HALVES):
            rows = slice(h * half, (h + 1) * half)
            xs = gather_blocks(messages[h].astype(jnp.bfloat16))
            first = step == 0 and h == 0
            if first:
                parts, peak = product(indices, xs, table, blocks, True)
                own_peak = jnp.max(peak)
                peaks = lax.all_gather(jnp.full((1, 128), own_peak), "state", axis=0, tiled=True)[:, 0]
                top_peak = jnp.max(peaks)
                into = TOP / (hidden * top_peak)
                back = hidden * top_peak / TOP
                peak_r = lax.dynamic_index_in_dim(peaks, lax.rem(me + blocks - 1, blocks), 0, False)
                peak_l = lax.dynamic_index_in_dim(peaks, lax.rem(me + 1, blocks), 0, False)
                spread = hidden * START_TOP
                scales = (
                    into / START_TOP, back * START_TOP,
                    TOP / (spread * own_peak), spread * peak_r / TOP, spread * peak_l / TOP,
                )
            else:
                (parts,) = product(indices, xs, table, blocks, False)
                grow = START_TOP if step == 0 else 1.0
                scales = (into / grow, back * grow, into / grow, back * grow, back * grow)
            step_weights = weights[step, :, rows].astype(jnp.float32)
            own_sum = jnp.sum(parts * step_weights, axis=(0, 2))
            sums = lax.all_gather(own_sum[None], ("state", "dp", "sub"), axis=0, tiled=True)
            normal = jnp.sum(sums, axis=0) / hidden
            summed = line_sum([parts[o] for o in range(blocks)], *scales)
            message = summed * step_weights[0] / normal[:, None]
            messages[h] = message
            step_messages.append(message)
            step_normals.append(normal)
        history.append(jnp.concatenate(step_messages, axis=0))
        normals.append(jnp.concatenate(step_normals, axis=0))
    log_scale = functools.reduce(lambda a, b: a + b, [jnp.log(x) for x in normals])
    out = jnp.stack(history).reshape(STEPS, seq_count, 1, 1, piece)
    return out, log_scale


SLOTS = ((3, 2, 1, 0), (0, 2, 3, 1), (3, 1, 0, 2), (0, 1, 2, 3))
PAIRS = [(0, 1), (1, 0), (2, 3), (3, 2)]
FROM_OUTER = [(0, 2), (3, 1)]
FROM_INNER = [(1, 2), (2, 1)]
LAST = [(1, 3), (2, 0), (0, 1), (3, 2)]
CHUNK = 1024
VMEM = pl.BlockSpec(memory_space=pltpu.VMEM)
SMEM = pl.BlockSpec(memory_space=pltpu.SMEM)
ANY = pl.BlockSpec(memory_space=pl.ANY)
F32, BF16 = jnp.float32, jnp.bfloat16


def shape(dims, dtype):
    return jax.ShapeDtypeStruct(dims, dtype)


class Order:
    def __init__(self):
        self.last = None

    def __call__(self, body, outs, out_specs, args, specs, scratch=(), aliases=None, name=None):
        count = len(args)
        if self.last is not None:
            args, specs = [*args, self.last], [*specs, ANY]
        extra = len(args) - count

        def run(*refs):
            body(*refs[:count], *refs[count + extra :])

        result = pl.pallas_call(
            run,
            out_shape=tuple(outs),
            in_specs=list(specs),
            out_specs=tuple(out_specs),
            scratch_shapes=list(scratch),
            input_output_aliases=aliases or {},
            compiler_params=pltpu.CompilerParams(vmem_limit_bytes=12 * 2**20),
            cost_estimate=pl.CostEstimate(flops=0, bytes_accessed=1024, transcendentals=0),
            name=name,
        )(*args)
        self.last = result[0]
        return result


def encode(x):
    x = x * x
    x = x * x
    return (x * x).astype(BF16)


def decode(y):
    y = y.astype(F32)
    return jnp.where(y > 0.0, jnp.exp2(0.125 * jnp.log2(y)), 0.0)


def load_body(table_ref, held_ref, peak_ref, sems):
    count = sems.shape[0]
    rows = table_ref.shape[0] // count
    copies = [
        pltpu.make_async_copy(table_ref.at[pl.ds(i * rows, rows)], held_ref.at[pl.ds(i * rows, rows)], sems.at[i])
        for i in range(count)
    ]
    for copy in copies:
        copy.start()
    top = jnp.zeros((16, table_ref.shape[1]), BF16)
    for i, copy in enumerate(copies):
        copy.wait()

        def step(k, best, i=i):
            at = pl.multiple_of(i * rows + k * 16, 16)
            return jnp.maximum(best, held_ref[pl.ds(at, 16), :])

        top = lax.fori_loop(0, rows // 16, step, top)
    peak_ref[...] = jnp.full(peak_ref.shape, jnp.max(top.astype(F32)), F32)


def corner(ref):
    return ref[0:1, 0:1]


def top_of(peaks):
    return jnp.maximum(
        jnp.maximum(corner(peaks[0]), corner(peaks[1])), jnp.maximum(corner(peaks[2]), corner(peaks[3]))
    )


def all_swaps(tile, axes):
    return [tile] + [lax.ppermute(tile, axes, [(i, i ^ k) for i in range(4)]) for k in range(1, 4)]


def products(idx, slot, left_ref, table_ref, weights_ref, sums_ref, arrive, put):
    piece = weights_ref.shape[1]
    for c in range(piece // CHUNK):
        here = slice(c * CHUNK, (c + 1) * CHUNK)
        cols = pl.ds(pl.multiple_of(idx[slot] * piece + c * CHUNK, CHUNK), CHUNK)
        total = jnp.dot(left_ref[...], table_ref[:, cols], preferred_element_type=F32)
        put(here, total)
        if c == 0:
            arrive.wait()
        weighted = total * weights_ref[:, here].astype(F32)
        sums = sums_ref[...]
        for k in range(CHUNK // 128):
            sums = sums + weighted[:, k * 128 : (k + 1) * 128]
        sums_ref[...] = sums


def fetch_weights(idx, slots, step, at, weights_ref, held, sems):
    half = held.shape[1]
    copies = [
        pltpu.make_async_copy(weights_ref.at[step, idx[s], pl.ds(at, half)], held.at[k], sems.at[k])
        for k, s in enumerate(slots)
    ]
    for copy in copies:
        copy.start()
    return copies


def first_body(step, at, spread, extra, idx, x0, x1, x2, x3, table_ref, weights_ref, *refs):
    refs = refs[extra:]
    peaks, (out0_ref, out1_ref, sums_ref, left_ref, held, sems) = refs[:-6], refs[-6:]
    copies = fetch_weights(idx, (0, 1), step, at, weights_ref, held, sems)
    depth = x0.shape[1]
    for q, x in enumerate((x0, x1, x2, x3)):
        left_ref[:, pl.ds(pl.multiple_of(idx[4 + q] * depth, depth), depth)] = x[...]
    scale = (TOP / spread) / (corner(peaks[0]) if step == 0 else top_of(peaks))
    sums_ref[...] = jnp.zeros_like(sums_ref)
    for slot, out_ref in enumerate((out0_ref, out1_ref)):
        def put(here, total, out_ref=out_ref):
            out_ref[:, here] = encode(total * scale)

        products(idx, slot, left_ref, table_ref, held.at[slot], sums_ref, copies[slot], put)


def rest_body(step, at, write, has_out, extra, idx, left_ref, sums_in, table_ref, weights_ref, *refs):
    refs = refs[extra:]
    if write is not None:
        message_ref, refs = refs[0], refs[2 if has_out else 1 :]
    (part_ref, own_ref, tile_ref, own_weights_ref), refs = refs[:4], refs[4:]
    if write is not None:
        out_ref, refs = refs[0], refs[1:]
    sums_ref, held, sems = refs
    if write is not None:
        copy_out = pltpu.make_async_copy(message_ref, out_ref.at[write[0], pl.ds(write[1], message_ref.shape[0])], sems.at[2])
        copy_out.start()
    copies = fetch_weights(idx, (2, 3), step, at, weights_ref, held, sems)
    sums_ref[...] = sums_in[...]
    for k, out in enumerate((part_ref, own_ref)):
        def put(here, total, out=out):
            out[:, here] = total

        products(idx, 2 + k, left_ref, table_ref, held.at[k], sums_ref, copies[k], put)
    own_weights_ref[...] = held[1]
    tile_ref[...] = jnp.broadcast_to(jnp.sum(sums_ref[...].T, axis=0, keepdims=True), tile_ref.shape)
    if write is not None:
        copy_out.wait()


def add_body(a_ref, b_ref, table_ref, *refs):
    refs[-1][...] = a_ref[...] + b_ref[...]


def far_body(step, spread, forward, extra, idx, part_ref, pair_ref, table_ref, *refs):
    peaks, refs = refs[:4], refs[4 + extra :]
    if forward:
        refs[2][...] = refs[0][...]
        refs = refs[1:]
    out = refs[0]
    top = top_of(peaks)
    scale = (TOP / spread) / top

    @pl.when(idx[8] == 1)
    def _():
        pair = decode(pair_ref[...])
        if step == 0:
            pair = pair * (corner(peaks[1]) / top)
        out[...] = encode(part_ref[...] * scale + pair)

    @pl.when(idx[8] == 0)
    def _():
        out[...] = encode(part_ref[...] * scale)


def last_body(step, spread, hidden, finish, count, idx, own_ref, pair_ref, outer_ref, inner_ref, far_ref, weights_ref, table_ref, *refs):
    tiles, refs = [ref[...] for ref in refs[:count]], refs[count:]
    peaks, logs_in, refs = refs[:4], refs[4] if step else None, refs[5 if step else 4 :]
    if finish is not None:
        refs = refs[1:]
    lowered_ref, message_ref, logs_ref = refs[:3]
    if finish is not None:
        out_ref, mixed_ref, sem = refs[3:]
    else:
        (mixed_ref,) = refs[3:]
    half = own_ref.shape[0]
    top = top_of(peaks)
    unscale = top * (spread / TOP)
    total = tiles[0] + tiles[1]
    if count == 4:
        total = total + (tiles[2] + tiles[3])
    normal = total / hidden
    logs = jnp.log(normal)
    logs_ref[...] = logs if logs_in is None else logs_in[...] + logs
    inverse = jnp.broadcast_to(1.0 / normal[0:1, :], (half, half)).T

    def sent_by(k):
        return corner(peaks[k]) * (spread / TOP) if step == 0 else unscale

    @pl.when(idx[8] == 1)
    def _():
        mixed_ref[...] = (
            own_ref[...]
            + (decode(outer_ref[...]) * sent_by(2) + decode(inner_ref[...]) * sent_by(3))
            + decode(far_ref[...]) * unscale
        )

    @pl.when(idx[8] == 0)
    def _():
        mixed_ref[...] = own_ref[...] + (decode(pair_ref[...]) * sent_by(1) + decode(far_ref[...]) * unscale)

    for k in range(own_ref.shape[1] // 128):
        here = slice(k * 128, (k + 1) * 128)
        message = mixed_ref[:, here] * weights_ref[:, here].astype(F32) * inverse
        lowered_ref[:, here] = message.astype(BF16)
        message_ref[:, k, :] = message
    if finish is not None:
        write = pltpu.make_async_copy(message_ref, out_ref.at[finish[0], pl.ds(finish[1], half)], sem)
        write.start()
        write.wait()


def fast(transition, emission, start):
    seqs, piece = start.shape[0], start.shape[3]
    hidden = 16 * piece
    half = seqs // HALVES
    table = transition.reshape(4 * piece, 4 * piece)
    me = lax.axis_index("state")
    d = lax.axis_index("dp") * 2 + lax.axis_index("sub")
    slots = jnp.asarray(SLOTS, jnp.int32)[me]
    inner = jnp.logical_and(me > 0, me < 3)
    idx = jnp.concatenate([slots, jnp.stack([d, d ^ 1, d ^ 2, d ^ 3, inner]).astype(jnp.int32)])
    weights = jnp.transpose(emission[:, :, 0], (0, 2, 1, 3))
    wide, code = shape((half, piece), F32), shape((half, piece), BF16)
    square, tile = shape((half, 128), F32), shape((8, 128), F32)
    rows = shape((half, piece // 128, 128), F32)
    out_shape = shape((STEPS, seqs, piece // 128, 128), F32)
    dma = pltpu.SemaphoreType.DMA
    order = Order()

    table, weights, idx = lax.optimization_barrier((table, weights, idx))
    weights = pltpu.with_memory_space_constraint(weights, pltpu.HBM)
    held, peak = order(
        load_body, [pltpu.VMEM(table.shape, table.dtype), shape((8, 128), F32)], [VMEM] * 2, [table], [ANY],
        [dma((8,))], name="load_table",
    )
    order.last = peak
    held = pltpu.with_memory_space_constraint(held, pltpu.VMEM)
    peaks = all_swaps(peak, "state")

    spreads = [hidden * 1.01 * (START_TOP if step == 0 else 1.0) for step in range(STEPS)]
    state = [{"lowered": start[h * half : (h + 1) * half, 0, 0].astype(BF16)} for h in range(HALVES)]
    box = {"out": None}

    def swap(h, axis, k):
        s = state[h]
        s["their"] = lax.ppermute(s["tile"], axis, [(i, i ^ k) for i in range(lax.axis_size(axis))])

    def add(h, after=()):
        s = state[h]
        s["tile"] = order(
            add_body, [tile], [VMEM], [s["tile"], s["their"], held, *after], [VMEM] * 3 + [ANY] * len(after),
            name="add_sums",
        )[0]

    def gather(h):
        s = state[h]
        own = s["lowered"]
        s["across"] = lax.ppermute(own, "dp", [(0, 1), (1, 0)])
        s["xs"] = [own, lax.ppermute(own, "sub", [(0, 1), (1, 0)])]

    def gather_rest(h, across):
        state[h]["xs"] += [across, lax.ppermute(across, "sub", [(0, 1), (1, 0)])]

    def begin(step, h):
        s, at, spread = state[h], h * half, spreads[step]
        used = [peak] if step == 0 else peaks
        after = state[1]["xs"][2:] if step == h == 0 else []
        send0, send1, sums, left = order(
            functools.partial(first_body, step, at, spread, len(after)),
            [code, code, square, shape((half, 4 * piece), BF16)], [VMEM] * 4,
            [idx, *s["xs"], held, weights, *after, *used],
            [SMEM] + [VMEM] * 5 + [ANY] * (1 + len(after)) + [VMEM] * len(used),
            [pltpu.VMEM((2, half, piece), BF16), dma((2,))], name="product_first",
        )
        ends = step == STEPS - 1 and h == 1
        if "tile" in state[1 - h] and not ends:
            add(1 - h, [state[1 - h]["far"]])
            swap(1 - h, "sub", 1)
        s["pair"] = lax.ppermute(send0, "state", PAIRS)
        s["outer"] = lax.ppermute(send1, "state", FROM_OUTER)
        s["inner"] = lax.ppermute(send1, "state", FROM_INNER)
        s["left"], s["sums"] = left, sums

    def proceed(step, h, forward, message=None, place=None):
        s, at = state[h], h * half
        args = [idx, s["left"], s["sums"], held, weights]
        after = [state[0]["far"]] if step == STEPS - 1 and h == 1 else []
        args, specs = args + after, [SMEM] + [VMEM] * 3 + [ANY] * (1 + len(after))
        outs, out_specs, aliases = [wide, wide, tile, code], [VMEM] * 4, None
        has_out = box["out"] is not None
        if place is not None:
            args, specs = args + [message], specs + [VMEM]
            outs, out_specs = outs + [out_shape], out_specs + [ANY]
            if has_out:
                aliases = {len(args): 4}
                args, specs = args + [box["out"]], specs + [ANY]
        result = order(
            functools.partial(rest_body, step, at, place, has_out, len(after)), outs, out_specs, args, specs,
            [pltpu.VMEM((half, 128), F32), pltpu.VMEM((2, half, piece), BF16), dma((3,))], aliases,
            name="product_rest",
        )
        part, s["own"], s["tile"], s["weights"] = result[:4]
        if place is not None:
            box["out"] = result[4]
        swap(h, "state", 1)
        ends = step == STEPS - 1 and h == 1
        args = [idx, part, s["pair"], held, *peaks]
        after = [s["their"]] if ends or step == 0 else []
        args, specs = args + after, [SMEM] + [VMEM] * 7 + [ANY] * len(after)
        if forward:
            args, specs = args + [state[1 - h]["across"]], specs + [VMEM]
        count = 2 if forward else 1
        result = order(
            functools.partial(far_body, step, spreads[step], forward, len(after)), [code] * count, [VMEM] * count,
            args, specs, name="far_block",
        )
        if ends:
            s["far"] = lax.ppermute(result[0], "state", LAST)
            add(h)
            swap(h, "state", 2)
            return
        if forward:
            gather_rest(1 - h, result[1])
        s["far"] = lax.ppermute(result[0], "state", LAST)
        add(h, [s["outer"]])
        swap(h, "dp", 1)
        add(h, [s["inner"]])
        swap(h, "state", 2)
        if step == STEPS - 1:
            add(h)
            swap(h, "sub", 1)

    def finish(step, h):
        s = state[h]
        args = [idx, s["own"], s["pair"], s["outer"], s["inner"], s["far"], s["weights"], held]
        tiles = s.get("tiles") or [s["tile"], s["their"]]
        args += [*tiles, *peaks]
        specs = [SMEM] + [VMEM] * (len(args) - 1)
        if step:
            args, specs = args + [s["logs"]], specs + [VMEM]
        outs, out_specs, aliases, place = [code, rows, tile], [VMEM] * 3, None, None
        scratch = [pltpu.VMEM((half, piece), F32)]
        if step == STEPS - 1:
            place = (step, h * half)
            aliases = {len(args): 3}
            args, specs = args + [box["out"]], specs + [ANY]
            outs, out_specs, scratch = outs + [out_shape], out_specs + [ANY], scratch + [dma]
        result = order(
            functools.partial(last_body, step, spreads[step], hidden, place, len(tiles)), outs, out_specs, args, specs,
            scratch, aliases, name="normalise",
        )
        s["lowered"], s["message"], s["logs"] = result[:3]
        if place is not None:
            box["out"] = result[3]

    for s in state:
        own = s["lowered"]
        s["xs"] = [own] + [lax.ppermute(own, ("dp", "sub"), [(i, i ^ k) for i in range(4)]) for k in (1, 2, 3)]
    for step in range(STEPS):
        begin(step, 0)
        if step:
            finish(step - 1, 1)
            gather(1)
            proceed(step, 0, True, state[1]["message"], (step - 1, half))
        else:
            proceed(step, 0, False)
        begin(step, 1)
        if step < STEPS - 1:
            finish(step, 0)
            gather(0)
            proceed(step, 1, True, state[0]["message"], (step, 0))
        else:
            proceed(step, 1, False)
            finish(step, 0)
    add(1)
    state[1]["tiles"] = all_swaps(state[1]["tile"], ("dp", "sub"))
    finish(STEPS - 1, 1)
    log_scale = jnp.concatenate([s["logs"][0] for s in state])
    return box["out"].reshape(STEPS, seqs, 1, 1, piece), log_scale


def shards(transition, emission, start):
    sizes = [lax.axis_size(name) for name in ("state", "dp", "sub")]
    if sizes == [4, 2, 2] and start.shape[0] == HALVES * 128 and start.shape[3] % CHUNK == 0:
        return fast(transition, emission, start)
    return general(transition, emission, start)


def solution(mesh):
    in_specs = (
        P(None, "state", None, ("dp", "sub")),
        P(None, "groups", ("dp", "sub"), None, None),
        P("groups", ("dp", "sub"), "state", None),
    )
    out_specs = (P(None, "groups", ("dp", "sub"), "state", None), P("groups"))
    return jax.shard_map(shards, mesh=mesh, in_specs=in_specs, out_specs=out_specs, check_vma=False)
```
